32 devices in a mesh: dp: 8 (over z, y), tensor: 4 (over x, core).
Axes of the slice: x: 2, y: 2, z: 4, core: 2. Of those that a mesh axis runs over, the one named last changes fastest.
Arguments:
- inputs: bfloat16 [25600, 768], P(('dp', 'tensor')), may hold values from -6 to 6
- res_ids: int32 [32], P(('dp', 'tensor')), may hold values from 0 to 1
- memory: bfloat16 [2, 6400, 768], P(None, ('dp', 'tensor')), may hold values from -6 to 6
- gain_one: float32 [768], replicated, may hold values from 0.5 to 1.5
- bias_one: float32 [768], replicated, may hold values from -1.8 to 1.8
- w_qkv: bfloat16 [768, 2304], replicated, may hold values from -0.21875 to 0.21875
- b_qkv: float32 [2304], replicated, may hold values from -1.8 to 1.8
- pool_weight: float32 [3, 27, 96], replicated, may hold values from -1.25 to 1.25
- pool_gain: float32 [3, 96], replicated, may hold values from 0.5 to 1.5
- pool_bias: float32 [3, 96], replicated, may hold values from -1.8 to 1.8
- rel_table: float32 [53, 96], replicated, may hold values from -0.6 to 0.6
- w_proj: bfloat16 [768, 768], replicated, may hold values from -0.21875 to 0.21875
- b_proj: float32 [768], replicated, may hold values from -1.8 to 1.8
- gain_two: float32 [768], replicated, may hold values from 0.5 to 1.5
- bias_two: float32 [768], replicated, may hold values from -1.8 to 1.8
- w_up: bfloat16 [768, 3072], P(None, 'tensor'), may hold values from -0.21875 to 0.21875
- b_up: bfloat16 [3072], P('tensor'), may hold values from -1.796875 to 1.796875
- w_down: bfloat16 [3072, 768], P('tensor'), may hold values from -0.109375 to 0.109375
- b_down: float32 [768], replicated, may hold values from -1.8 to 1.8
- cotangent: bfloat16 [25600, 768], P(('dp', 'tensor')), may hold values from -6 to 6
Outputs:
- output: bfloat16 [25600, 768], P(('dp', 'tensor'))
- input_grad: float32 [25600, 768], P(('dp', 'tensor'))
- grad_gain_one: float32 [768], replicated
- grad_bias_one: float32 [768], replicated
- grad_w_qkv: float32 [768, 2304], replicated
- grad_b_qkv: float32 [2304], replicated
- grad_pool_weight: float32 [3, 27, 96], replicated
- grad_pool_gain: float32 [3, 96], replicated
- grad_pool_bias: float32 [3, 96], replicated
- grad_rel_table: float32 [53, 96], replicated
- grad_w_proj: float32 [768, 768], replicated
- grad_b_proj: float32 [768], replicated
- grad_gain_two: float32 [768], replicated
- grad_bias_two: float32 [768], replicated
- grad_w_up: float32 [768, 3072], P(None, 'tensor')
- grad_b_up: float32 [3072], P('tensor')
- grad_w_down: float32 [3072, 768], P('tensor')
- grad_b_down: float32 [768], replicated
The draws below stay inside these ranges and needn't reach their ends.
Inputs may be any that keep to these rules, and one draw needn't show every extreme that they name: `res_ids`: 0 marks a clip whose frames hold 7 x 7 tokens in the corner of the 10 x 10 grid, 1 a clip that fills it.
All inputs are finite; a program needn't handle non-finite values.
Results may differ from the reference program's by a relative error of at most 0.012.
Values may be sent and summed in bfloat16 or wider, within the bound.
A program may use at most 384 MiB of HBM per device.

```python
from functools import partial
import jax
import jax.numpy as jnp
from jax import lax

D = 768
HEADS = 8
HEAD_DIM = 96
FF = 3072
FRAMES = 8
SIDE = 10
SMALL_SIDE = 7
LENGTH = 800
MEM = 200
OFFSETS = 28
REL_ROWS = 53
CLIPS = 32
TOKENS = 25600
MEM_TOKENS = 6400


def touch_ends(values, rng, low, top_value):
    longest = values.shape.index(max(values.shape))
    spots = []
    for shift in (0, 1):
        where = [jax.random.randint(jax.random.fold_in(rng, axis), (), 0, length) for axis, length in enumerate(values.shape)]
        where[longest] = (where[longest] + shift) % values.shape[longest]
        spots.append(tuple(where))
    return values.at[spots[0]].set(low).at[spots[1]].set(top_value)


def level_of(rng, shape, cuts, smallest, top_value):
    level, own = 1.0, jax.random.fold_in(rng, 6)
    for dim, parts in cuts:
        heights = jnp.exp(jax.random.uniform(jax.random.fold_in(own, dim), (parts,), jnp.float32, smallest / len(cuts), top_value / len(cuts)))
        level = level * jnp.repeat(heights, shape[dim] // parts).reshape([-1 if axis == dim else 1 for axis in range(len(shape))])
    return level


def bell_draw(own_key, dims, width, most, pieces=(), kind=jnp.bfloat16):
    values = jax.random.normal(own_key, dims, jnp.float32) * width
    if len(pieces) > 0:
        values = level_of(own_key, dims, pieces, -0.22, 0.18) * values
    return jnp.clip(values, min=-most, max=most).astype(kind)


def setup_inputs(seed: int = 0) -> dict:
    key_of = jax.random.split(jax.random.key(seed), 21)
    inputs = bell_draw(key_of[0], (TOKENS, D), 1.0, 6.0, ((0, 32),))
    res_ids = touch_ends(jax.random.randint(key_of[1], (CLIPS,), 0, 2), jax.random.fold_in(key_of[1], 1), 0, 1).astype(jnp.int32)
    memory = bell_draw(key_of[2], (2, MEM_TOKENS, D), 1.0, 6.0, ((1, 32),))
    gain_one = jnp.clip(1.0 + 0.1 * jax.random.normal(key_of[3], (D,), jnp.float32), 0.5, 1.5)
    bias_one = bell_draw(key_of[4], (D,), 0.3, 1.8, (), jnp.float32)
    w_qkv = bell_draw(key_of[5], (D, 3 * D), D ** -0.5, 0.21875)
    b_qkv = bell_draw(key_of[6], (3 * D,), 0.3, 1.8, (), jnp.float32)
    pool_weight = bell_draw(key_of[7], (3, 27, HEAD_DIM), 27 ** -0.5, 1.25, (), jnp.float32)
    pool_gain = jnp.clip(1.0 + 0.1 * jax.random.normal(key_of[8], (3, HEAD_DIM), jnp.float32), 0.5, 1.5)
    pool_bias = bell_draw(key_of[9], (3, HEAD_DIM), 0.3, 1.8, (), jnp.float32)
    rel_table = bell_draw(key_of[10], (REL_ROWS, HEAD_DIM), 0.1, 0.6, (), jnp.float32)
    w_proj = bell_draw(key_of[11], (D, D), D ** -0.5, 0.21875)
    b_proj = bell_draw(key_of[12], (D,), 0.3, 1.8, (), jnp.float32)
    gain_two = jnp.clip(1.0 + 0.1 * jax.random.normal(key_of[13], (D,), jnp.float32), 0.5, 1.5)
    bias_two = bell_draw(key_of[14], (D,), 0.3, 1.8, (), jnp.float32)
    w_up = bell_draw(key_of[15], (D, FF), D ** -0.5, 0.21875, ((1, 4),))
    b_up = bell_draw(key_of[16], (FF,), 0.3, 1.796875, ((0, 4),))
    w_down = bell_draw(key_of[17], (FF, D), FF ** -0.5, 0.109375, ((0, 4),))
    b_down = bell_draw(key_of[18], (D,), 0.3, 1.8, (), jnp.float32)
    cotangent = bell_draw(key_of[19], (TOKENS, D), 1.0, 6.0, ((0, 32),))
    return {"inputs": inputs, "res_ids": res_ids, "memory": memory, "gain_one": gain_one, "bias_one": bias_one, "w_qkv": w_qkv, "b_qkv": b_qkv, "pool_weight": pool_weight, "pool_gain": pool_gain, "pool_bias": pool_bias, "rel_table": rel_table, "w_proj": w_proj, "b_proj": b_proj, "gain_two": gain_two, "bias_two": bias_two, "w_up": w_up, "b_up": b_up, "w_down": w_down, "b_down": b_down, "cotangent": cotangent}


@jax.custom_vjp
def low(v):
    return lax.optimization_barrier(v.astype(jnp.bfloat16)).astype(jnp.float32)

@jax.custom_vjp
def low_back(v):
    return v

def low_keep(v):
    return (low(v), None)

def low_pass(kept, grad):
    return (grad,)

def back_keep(v):
    return (v, None)

def back_low(kept, grad):
    return (low(grad),)
low.defvjp(low_keep, low_pass)
low_back.defvjp(back_keep, back_low)
HIGHEST = lax.Precision.HIGHEST
NORM_EPS = 1e-06
INV_ROOT_TWO = 0.7071067811865476

def layer_norm(values, gain_vec, shift_vec):
    average = lax.optimization_barrier(jnp.mean(values, axis=-1, keepdims=True))
    centered = values - average
    variance = lax.optimization_barrier(jnp.mean(centered * centered, axis=-1, keepdims=True))
    return centered * lax.rsqrt(variance + NORM_EPS) * gain_vec + shift_vec

def gelu_exact(values):
    return 0.5 * values * (1.0 + lax.erf(values * INV_ROOT_TWO))

def grid_tables(res_ids):
    position = jnp.arange(LENGTH, dtype=jnp.int32)
    frame_of = position // (SIDE * SIDE)
    row_of = position // SIDE % SIDE
    column_of = position % SIDE
    large_clip = res_ids[:, None] == 1
    inside = (row_of < SMALL_SIDE) & (column_of < SMALL_SIDE)
    token_valid = large_clip | inside[None, :]
    memory_side = (SIDE + 1) // 2
    memory_small = (SMALL_SIDE + 1) // 2
    memory_index = jnp.arange(MEM, dtype=jnp.int32) % (MEM // 2)
    memory_row = memory_index // memory_side % memory_side
    memory_column = memory_index % memory_side
    memory_inside = (memory_row < memory_small) & (memory_column < memory_small)
    memory_valid = large_clip | memory_inside[None, :]
    frame_range = jnp.arange(FRAMES, dtype=jnp.int32)
    side_range = jnp.arange(SIDE, dtype=jnp.int32)
    row_base = 2 * FRAMES - 1
    column_base = row_base + 2 * SIDE - 1
    target = jnp.concatenate([frame_of[:, None] - frame_range[None, :] + FRAMES - 1, row_base + row_of[:, None] - side_range[None, :] + SIDE - 1, column_base + column_of[:, None] - side_range[None, :] + SIDE - 1], axis=1)
    select_table = (target[:, :, None] == jnp.arange(REL_ROWS, dtype=jnp.int32)[None, None, :]).astype(jnp.float32)
    key_onehot = jnp.concatenate([frame_of[:, None] == frame_range[None, :], row_of[:, None] == side_range[None, :], column_of[:, None] == side_range[None, :]], axis=1).astype(jnp.float32)
    return (token_valid, memory_valid, select_table, key_onehot)

def pool_field(field, kernel):
    kernel_wide = jnp.tile(kernel, (1, HEADS))
    padded = jnp.pad(field, ((0, 0), (1, 1), (1, 1), (1, 1), (0, 0)))
    accumulated = jnp.zeros_like(field)
    for kernel_tap in range(27):
        frame_shift = kernel_tap // 9
        row_shift = kernel_tap // 3 % 3
        column_shift = kernel_tap % 3
        window = padded[:, frame_shift:frame_shift + FRAMES, row_shift:row_shift + SIDE, column_shift:column_shift + SIDE, :]
        accumulated = accumulated + window * kernel_wide[kernel_tap]
    return accumulated

def pool_norm(stacked, pool_weight, pool_gain, pool_bias):
    clip_count = stacked.shape[1]
    results = []
    for branch_index in range(3):
        pooled = pool_field(stacked[branch_index], pool_weight[branch_index])
        per_head = pooled.reshape(clip_count, LENGTH, HEADS, HEAD_DIM)
        results.append(layer_norm(per_head, pool_gain[branch_index], pool_bias[branch_index]))
    return jnp.stack(results)

def build_offsets(queries, rel_table, select_table):
    rel_scores = jnp.einsum('...lhe,re->...lhr', queries, rel_table, precision=HIGHEST)
    return jnp.einsum('...lhr,lpr->...lhp', rel_scores, select_table, precision=HIGHEST)

def clip_attention(items, rel_table, select_table, key_onehot):
    queries, keys_now, values_now, memory_pair, key_valid, memory_valid = items
    scale_factor = HEAD_DIM ** (-0.5)
    offsets = build_offsets(queries, rel_table, select_table)
    query_ext = low(jnp.concatenate([queries * scale_factor, offsets], axis=-1))
    memory_keys = memory_pair[0].reshape(MEM, HEADS, HEAD_DIM)
    memory_values = memory_pair[1].reshape(MEM, HEADS, HEAD_DIM)
    onehot_heads = jnp.broadcast_to(key_onehot[:, None, :], (LENGTH, HEADS, OFFSETS))
    keys_ext = jnp.concatenate([jnp.concatenate([low(keys_now), onehot_heads], axis=-1), jnp.concatenate([memory_keys, jnp.zeros((MEM, HEADS, OFFSETS), jnp.float32)], axis=-1)], axis=0)
    values_all = jnp.concatenate([low(values_now), memory_values], axis=0)
    valid_all = jnp.concatenate([key_valid, memory_valid])
    scores = low_back(jnp.einsum('qhc,khc->hqk', query_ext, keys_ext, precision=HIGHEST))
    scores = jnp.where(valid_all[None, None, :], scores, -1e+30)
    row_top = lax.optimization_barrier(jnp.max(scores, axis=-1, keepdims=True))
    exponents = jnp.exp(scores - row_top)
    probabilities = exponents / lax.optimization_barrier(jnp.sum(exponents, axis=-1, keepdims=True))
    weighted = low_back(jnp.einsum('hqk,khe->qhe', low(probabilities), values_all, precision=HIGHEST))
    return (weighted + queries).reshape(LENGTH, D)

def forward(inputs, gain_one, bias_one, w_qkv, b_qkv, pool_weight, pool_gain, pool_bias, rel_table, w_proj, b_proj, gain_two, bias_two, w_up, b_up, w_down, b_down, memory_wide, token_valid, memory_valid, select_table, key_onehot):
    token_weight = token_valid.reshape(-1).astype(jnp.float32)[:, None]
    normed_one = layer_norm(inputs, gain_one, bias_one)
    qkv = low_back(jnp.dot(low(normed_one), w_qkv, precision=HIGHEST)) + b_qkv
    masked = qkv * token_weight
    stacked = jnp.moveaxis(masked.reshape(CLIPS, FRAMES, SIDE, SIDE, 3, D), 4, 0)
    pooled = pool_norm(stacked, pool_weight, pool_gain, pool_bias)
    memory_clip = jnp.moveaxis(memory_wide.reshape(2, CLIPS, MEM, D), 1, 0)
    attend = jax.checkpoint(partial(clip_attention, rel_table=rel_table, select_table=select_table, key_onehot=key_onehot))
    attended = lax.map(attend, (pooled[0], pooled[1], pooled[2], memory_clip, token_valid, memory_valid))
    attended = attended.reshape(TOKENS, D)
    middle = inputs + (low_back(jnp.dot(low(attended), w_proj, precision=HIGHEST)) + b_proj)
    normed_two = low(layer_norm(middle, gain_two, bias_two))
    hidden = low_back(jnp.dot(normed_two, w_up, precision=HIGHEST)) + b_up
    activated = low(gelu_exact(hidden))
    mlp_out = low_back(jnp.dot(activated, w_down, precision=HIGHEST)) + b_down
    return (middle + mlp_out) * token_weight

def reference(inputs, res_ids, memory, gain_one, bias_one, w_qkv, b_qkv, pool_weight, pool_gain, pool_bias, rel_table, w_proj, b_proj, gain_two, bias_two, w_up, b_up, w_down, b_down, cotangent):
    token_valid, memory_valid, select_table, key_onehot = grid_tables(res_ids)
    memory_wide = memory.astype(jnp.float32)
    primals = (inputs.astype(jnp.float32), gain_one, bias_one, w_qkv.astype(jnp.float32), b_qkv, pool_weight, pool_gain, pool_bias, rel_table, w_proj.astype(jnp.float32), b_proj, gain_two, bias_two, w_up.astype(jnp.float32), b_up.astype(jnp.float32), w_down.astype(jnp.float32), b_down)
    bound = partial(forward, memory_wide=memory_wide, token_valid=token_valid, memory_valid=memory_valid, select_table=select_table, key_onehot=key_onehot)
    result, pullback = jax.vjp(bound, *primals)
    grads = pullback(cotangent.astype(jnp.float32))
    return (result.astype(jnp.bfloat16), grads[0], grads[1], grads[2], grads[3], grads[4], grads[5], grads[6], grads[7], grads[8], grads[9], grads[10], grads[11], grads[12], grads[13], grads[14], grads[15], grads[16])
```

```python
import functools

import jax
import jax.numpy as jnp
import numpy as np
from jax import lax
from jax.experimental import pallas as pl
from jax.experimental.pallas import tpu as pltpu
from jax.sharding import PartitionSpec as P

D = 768
HEADS = 8
HEAD_DIM = 96
FRAMES = 8
SIDE = 10
SMALL_SIDE = 7
SPOTS = SIDE * SIDE
LENGTH = FRAMES * SPOTS
MEM = 200
KEYS = 1024
OFFSETS = FRAMES + 2 * SIDE
REL_ROWS = 53
GROUPS = 2
PER = HEADS // GROUPS
WIDE = PER * HEAD_DIM
TAPS = 27
LANES = 128
BAND = SIDE * FRAMES
CHUNK = 160
PAIRS = 384
MASK_LANE = HEAD_DIM + OFFSETS
EPS = 1e-6
SCALE = HEAD_DIM**-0.5
F32 = jnp.float32
BF16 = jnp.bfloat16
NEG = -1e30
VMEM_LIMIT = 60 * 1024 * 1024


def nn(a, b):
    return jnp.dot(a, b, preferred_element_type=F32)


def nt(a, b):
    return lax.dot_general(a, b, (((1,), (1,)), ((), ())), preferred_element_type=F32)


def tn(a, b):
    return lax.dot_general(a, b, (((0,), (0,)), ((), ())), preferred_element_type=F32)


def lane_of(shape):
    return lax.broadcasted_iota(jnp.int32, shape, len(shape) - 1)


def to_heads(tiles):
    t0, t1, t2 = tiles
    lane = lane_of(t0.shape)
    own = lane < HEAD_DIM
    h1 = pltpu.roll(jnp.where(lane >= 96, t0, t1), 32, t0.ndim - 1)
    h2 = pltpu.roll(jnp.where(lane >= 64, t1, t2), 64, t0.ndim - 1)
    h3 = pltpu.roll(t2, 96, t0.ndim - 1)
    return [jnp.where(own, h, 0.0) for h in (t0, h1, h2, h3)]


def to_dense(heads):
    p0, p1, p2, p3 = heads
    lane = lane_of(p0.shape)
    r1 = pltpu.roll(p1, 96, p0.ndim - 1)
    r2 = pltpu.roll(p2, 64, p0.ndim - 1)
    r3 = pltpu.roll(p3, 32, p0.ndim - 1)
    return [jnp.where(lane < 96, p0, r1), jnp.where(lane < 64, r1, r2), jnp.where(lane < 32, r2, r3)]


def row_norm(x):
    mean = jnp.mean(x, axis=-1, keepdims=True)
    c = x - mean
    rstd = lax.rsqrt(jnp.mean(c * c, axis=-1, keepdims=True) + EPS)
    return c * rstd, rstd


def frame_shift(x, up):
    frame = lax.broadcasted_iota(jnp.int32, x.shape, 1)
    if up:
        return jnp.where(frame == 0, 0.0, pltpu.roll(x, 1, 1))
    return jnp.where(frame == FRAMES - 1, 0.0, pltpu.roll(x, FRAMES - 1, 1))


def fold8(x):
    return jnp.sum(x.reshape(x.shape[0] // 8, 8, x.shape[1]), axis=0)


def tile_at(j):
    return pl.ds(pl.multiple_of(j * LANES, LANES), LANES)


def rows_at(r, size):
    return pl.ds(pl.multiple_of(r * size, size), size)


def fwd_kernel(
    x_ref, vec_ref, valid_ref, wq_ref, wk_ref, wv_ref, bq_ref, bk_ref, bv_ref, pw_ref, ln_ref,
    tall_ref, cmp_ref, sel_ref, kc_ref, memk_ref, memv_ref, wp_ref,
    mid_ref, field_ref, xh_ref, q_ref, k_ref, v_ref, p_ref, o_ref, att_ref,
    n_s, fld_s, pool_s, q_s, acc_s,
):
    g, h = pl.program_id(0), pl.program_id(1)

    @pl.when((g == 0) & (h == 0))
    def _():
        def body(i, _):
            rows = rows_at(i, BAND)
            xh, _ = row_norm(x_ref[rows, :].astype(F32))
            n_s[rows, :] = (xh * vec_ref[0:1, :] + vec_ref[1:2, :]).astype(BF16)
            return 0

        lax.fori_loop(0, SIDE, body, 0)
        for a in range(3):
            fld_s[a, 0:SIDE] = jnp.zeros((SIDE, 8, 3 * WIDE), F32)
            fld_s[a, SPOTS + SIDE : SPOTS + 2 * SIDE] = jnp.zeros((SIDE, 8, 3 * WIDE), F32)

    @pl.when(h == 0)
    def _():
        for p, (w, b) in enumerate(((wq_ref, bq_ref), (wk_ref, bk_ref), (wv_ref, bv_ref))):
            y = nn(n_s[...], w[...]) + b[...]
            field_ref[:, :, p * WIDE : (p + 1) * WIDE] = y.reshape(SPOTS, 8, WIDE)

        def spread(r, _):
            spots = rows_at(r, SIDE)
            ok = valid_ref[spots]
            for j in range(9):
                lanes = slice(j * LANES, (j + 1) * LANES)
                y = field_ref[spots, :, lanes] * ok
                field_ref[spots, :, lanes] = y
                there = rows_at(r + 1, SIDE)
                fld_s[0, there, :, lanes] = frame_shift(y, True)
                fld_s[1, there, :, lanes] = y
                fld_s[2, there, :, lanes] = frame_shift(y, False)
            return 0

        lax.fori_loop(0, SIDE, spread, 0)

        def pool(pj, _):
            p, j = pj // 3, pj % 3
            lanes, own = tile_at(pj), tile_at(j)
            w = [jnp.broadcast_to(pw_ref[p, t : t + 1, own], (8, LANES)) for t in range(TAPS)]

            def row(r, _):
                acc = [None] * SIDE
                for c_in in range(SIDE):
                    for b in range(3):
                        for a in range(3):
                            x = fld_s[a, (r + b) * SIDE + c_in, :, lanes]
                            for e in range(3):
                                c = c_in - e + 1
                                if 0 <= c < SIDE:
                                    term = w[9 * a + 3 * b + e] * x
                                    acc[c] = term if acc[c] is None else acc[c] + term
                for c in range(SIDE):
                    pool_s[r * SIDE + c, :, lanes] = acc[c]
                return 0

            lax.fori_loop(0, SIDE, row, 0)
            return 0

        lax.fori_loop(0, 9, pool, 0)
        lane = lane_of((BAND, LANES))

        def norm(r, _):
            spots, rows = rows_at(r, SIDE), rows_at(r, BAND)
            for p in range(3):
                tiles = [
                    pool_s[spots, :, (3 * p + j) * LANES : (3 * p + j + 1) * LANES].reshape(BAND, LANES)
                    for j in range(3)
                ]
                for i, x in enumerate(to_heads(tiles)):
                    mean = jnp.sum(x, axis=-1, keepdims=True) * (1 / HEAD_DIM)
                    c = jnp.where(lane < HEAD_DIM, x - mean, 0.0)
                    var = jnp.sum(c * c, axis=-1, keepdims=True) * (1 / HEAD_DIM)
                    rstd = lax.rsqrt(var + EPS)
                    xh = c * rstd
                    xh_ref[i, p, rows, :] = jnp.where(lane == HEAD_DIM, rstd, xh)
                    y = xh * ln_ref[p : p + 1, :] + ln_ref[3 + p : 4 + p, :]
                    if p == 0:
                        q_s[i, rows, :] = y
                    elif p == 1:
                        k_ref[i, rows, :] = (y + kc_ref[rows, :]).astype(BF16)
                    else:
                        one = (lane == HEAD_DIM) | (lane == HEAD_DIM + 1)
                        v_ref[i, rows, :] = jnp.where(one, 1.0, y).astype(BF16)
            return 0

        lax.fori_loop(0, SIDE, norm, 0)
        for i in range(PER):
            k_ref[i, LENGTH:KEYS, :] = memk_ref[i]
            v_ref[i, LENGTH:KEYS, :] = memv_ref[i]

    def prepare(r, _):
        rows = rows_at(r, CHUNK)
        q = q_s[h, rows, :]
        near = (nt(q.astype(BF16), tall_ref[...]) * sel_ref[rows, :]).astype(BF16)
        lane = lane_of((CHUNK, LANES))
        ext = q * SCALE + nn(near, cmp_ref[...])
        q_ref[h, rows, :] = jnp.where(lane == MASK_LANE, 1.0, ext).astype(BF16)
        return 0

    lax.fori_loop(0, LENGTH // CHUNK, prepare, 0)

    def attend(r, _):
        rows = rows_at(r, CHUNK)
        lane = lane_of((CHUNK, LANES))
        s = nt(q_ref[h, rows, :], k_ref[h])
        e = jnp.exp(s - jnp.max(s, axis=-1, keepdims=True)).astype(BF16)
        p_ref[0, rows, :] = e
        o = nn(e, v_ref[h])
        total = o[:, HEAD_DIM : HEAD_DIM + 1]
        o = jnp.where(lane < HEAD_DIM, o * (1.0 / total), 0.0)
        o_ref[0, rows, :] = jnp.where(lane == HEAD_DIM, total, o)
        q_s[h, rows, :] += o
        return 0

    lax.fori_loop(0, LENGTH // CHUNK, attend, 0)

    @pl.when(h == PER - 1)
    def _():
        def join(r, _):
            rows = rows_at(r, BAND)
            for j, t in enumerate(to_dense([q_s[i, rows, :] for i in range(PER)])):
                att_ref[rows, j * LANES : (j + 1) * LANES] = t.astype(BF16)
            return 0

        lax.fori_loop(0, SIDE, join, 0)

    @pl.when((h == PER - 1) & (g == 0))
    def _():
        acc_s[...] = nn(att_ref[...], wp_ref[...])

    @pl.when((h == PER - 1) & (g == GROUPS - 1))
    def _():
        mid_ref[...] = x_ref[...].astype(F32) + acc_s[...] + nn(att_ref[...], wp_ref[...]) + vec_ref[4:5, :]


def mlp_kernel(
    mid_ref, cot_ref, vec_ref, valid_ref, up_ref, bu_ref, down_ref,
    out_ref, gm_ref, gml_ref, small_ref, gup_ref, gbu_ref, gdown_ref,
    n_s, nt_s, go_s, y_s, gn_s,
):
    step = pl.program_id(0)

    @pl.when(step == 0)
    def _():
        def body(i, sums):
            rows = rows_at(i, BAND)
            xh, _ = row_norm(mid_ref[rows, :])
            n_s[rows, :] = (xh * vec_ref[2:3, :] + vec_ref[3:4, :]).astype(BF16)
            go = cot_ref[rows, :].astype(F32) * valid_ref[rows, 0:1]
            go_s[rows, :] = go.astype(BF16)
            return sums + fold8(go)

        sums = lax.fori_loop(0, SIDE, body, jnp.zeros((8, D), F32))
        small_ref[2] = sums
        nt_s[...] = n_s[...].T

    pre = nn(n_s[...], up_ref[0]) + bu_ref[0, 0:1, :].astype(F32)
    cdf = 0.5 * (1.0 + lax.erf(pre * 0.7071067811865476))
    act = (pre * cdf).astype(BF16)
    slope = cdf + pre * jnp.exp(pre * pre * -0.5) * 0.3989422804014327
    ga = nt(go_s[...], down_ref[0])
    gh = ga * slope
    gbu_ref[0] = fold8(gh)
    ghl = gh.astype(BF16)
    gdown_ref[0] = tn(act, go_s[...]).astype(gdown_ref.dtype)
    gup_ref[0] = nn(nt_s[...], ghl).astype(gup_ref.dtype)
    y = nn(act, down_ref[0])
    gn = nt(ghl, up_ref[0])

    @pl.when(step == 0)
    def _():
        y_s[...] = y
        gn_s[...] = gn

    @pl.when(step > 0)
    def _():
        y_s[...] += y
        gn_s[...] += gn

    @pl.when(step == pl.num_programs(0) - 1)
    def _():
        def body(i, sums):
            rows = rows_at(i, BAND)
            mid = mid_ref[rows, :]
            ok = valid_ref[rows, 0:1]
            out_ref[rows, :] = ((mid + y_s[rows, :] + vec_ref[5:6, :]) * ok).astype(BF16)
            xh, rstd = row_norm(mid)
            gy = gn_s[rows, :]
            gx = gy * vec_ref[2:3, :]
            m1 = jnp.mean(gx, axis=-1, keepdims=True)
            m2 = jnp.mean(gx * xh, axis=-1, keepdims=True)
            gm = cot_ref[rows, :].astype(F32) * ok + (gx - m1 - xh * m2) * rstd
            gm_ref[rows, :] = gm
            gml_ref[rows, :] = gm.astype(BF16)
            return sums[0] + fold8(gy * xh), sums[1] + fold8(gy), sums[2] + fold8(gm)

        zero = jnp.zeros((8, D), F32)
        sums = lax.fori_loop(0, SIDE, body, (zero, zero, zero))
        small_ref[0] = sums[0]
        small_ref[1] = sums[1]
        small_ref[3] = sums[2]


def bwd_kernel(
    x_ref, vec_ref, valid_ref, gm_ref, gml_ref, wq_ref, wk_ref, wv_ref, pw_ref, ln_ref,
    tall_ref, cmp_ref, sel_ref, wp_ref, field_ref, xh_ref, q_ref, k_ref, v_ref, p_ref, o_ref, att_ref,
    gx_ref, small_ref, gwq_ref, gwk_ref, gwv_ref, gb_ref, gpw_ref, gln_ref, gtall_ref, gwp_ref,
    n_s, do_s, ds_s, dpp_s, g_s, gq_s, gin_s, gn_s,
):
    g, h = pl.program_id(0), pl.program_id(1)

    @pl.when((g == 0) & (h == 0))
    def _():
        def body(i, _):
            rows = rows_at(i, BAND)
            xh, _ = row_norm(x_ref[rows, :].astype(F32))
            n_s[rows, :] = (xh * vec_ref[0:1, :] + vec_ref[1:2, :]).astype(BF16)
            return 0

        lax.fori_loop(0, SIDE, body, 0)
        for a in range(3):
            g_s[a, 0:SIDE] = jnp.zeros((SIDE, 8, WIDE), F32)
            g_s[a, SPOTS + SIDE : SPOTS + 2 * SIDE] = jnp.zeros((SIDE, 8, WIDE), F32)
        gtall_ref[...] = jnp.zeros(gtall_ref.shape, F32)
        gln_ref[...] = jnp.zeros(gln_ref.shape, F32)

    @pl.when(h == 0)
    def _():
        gin_s[:, 0:WIDE] = nt(gml_ref[...], wp_ref[...])

        def split(r, _):
            rows = rows_at(r, BAND)
            tiles = [gin_s[rows, j * LANES : (j + 1) * LANES] for j in range(3)]
            for i, t in enumerate(to_heads(tiles)):
                do_s[i, rows, :] = t
            return 0

        lax.fori_loop(0, SIDE, split, 0)
        gwp_ref[...] = tn(att_ref[...], gml_ref[...]).astype(gwp_ref.dtype)

    lane = lane_of((LENGTH, LANES))
    do = do_s[h]
    o = o_ref[0]
    inv = 1.0 / o[:, HEAD_DIM : HEAD_DIM + 1]
    delta = jnp.sum(do * o, axis=-1, keepdims=True) * inv
    high = delta.astype(BF16).astype(F32)
    doe = jnp.where(lane == HEAD_DIM, -high, jnp.where(lane == HEAD_DIM + 1, high - delta, do * inv)).astype(BF16)
    gq_s[:, 0:LANES] = doe

    def scores(r, _):
        rows = rows_at(r, CHUNK)
        dp = nt(gq_s[rows, 0:LANES], v_ref[0])
        ds_s[rows, :] = (p_ref[0, rows, :].astype(F32) * dp).astype(BF16)
        return 0

    lax.fori_loop(0, LENGTH // CHUNK, scores, 0)
    dqe = nn(ds_s[...], k_ref[0])
    dk = tn(q_ref[0], ds_s[...]).T[:LENGTH]
    dv = tn(doe, p_ref[0]).T[:LENGTH]
    far = (nt(dqe.astype(BF16), cmp_ref[...]) * sel_ref[...]).astype(BF16)
    xq = xh_ref[0, 0]
    query = (jnp.where(lane < HEAD_DIM, xq, 0.0) * ln_ref[0:1, :] + ln_ref[3:4, :]).astype(BF16)
    gtall_ref[...] += tn(far, query)
    dq = dqe * SCALE + do + nn(far, tall_ref[...])
    for p, gy in enumerate((dq, dk, dv)):
        raw = xh_ref[0, p]
        rstd = raw[:, HEAD_DIM : HEAD_DIM + 1]
        gx = gy * ln_ref[p : p + 1, :]
        m1 = jnp.sum(gx, axis=-1, keepdims=True) * (1 / HEAD_DIM)
        m2 = jnp.sum(gx * raw, axis=-1, keepdims=True) * (1 / HEAD_DIM)
        dpp_s[h, p] = (gx - m1 - raw * m2) * rstd
        gln_ref[p] += fold8(gy * raw)
        gln_ref[3 + p] += fold8(gy)

    @pl.when(h == PER - 1)
    def _():
        def branch(p, _):
            def spread(r, _):
                there, rows = rows_at(r + 1, SIDE), rows_at(r, BAND)
                for j, t in enumerate(to_dense([dpp_s[i, p, rows, :] for i in range(PER)])):
                    lanes = slice(j * LANES, (j + 1) * LANES)
                    t = t.reshape(SIDE, 8, LANES)
                    g_s[0, there, :, lanes] = frame_shift(t, False)
                    g_s[1, there, :, lanes] = t
                    g_s[2, there, :, lanes] = frame_shift(t, True)
                return 0

            lax.fori_loop(0, SIDE, spread, 0)

            def pool(j, _):
                lanes, own = tile_at(3 * p + j), tile_at(j)
                for a in range(3):
                    w = [
                        jnp.broadcast_to(pw_ref[p, t : t + 1, own], (8, LANES))
                        for t in range(9 * a, 9 * a + 9)
                    ]

                    def row(r, sums):
                        sums = list(sums)
                        x = [field_ref[r * SIDE + c, :, lanes] for c in range(SIDE)]
                        acc = [None] * SIDE
                        for c_in in range(SIDE):
                            for b in range(3):
                                t = g_s[a, (r + 2 - b) * SIDE + c_in, :, own]
                                for e in range(3):
                                    c = c_in + e - 1
                                    if 0 <= c < SIDE:
                                        term = w[3 * b + e] * t
                                        acc[c] = term if acc[c] is None else acc[c] + term
                                        sums[3 * b + e] = sums[3 * b + e] + x[c] * t
                        for c in range(SIDE):
                            at = pl.ds(pl.multiple_of(r * BAND + c * 8, 8), 8)
                            if a == 0:
                                gin_s[at, lanes] = acc[c]
                            else:
                                gin_s[at, lanes] += acc[c]
                        return tuple(sums)

                    sums = lax.fori_loop(0, SIDE, row, tuple(jnp.zeros((8, LANES), F32) for _ in range(9)))
                    for t in range(9):
                        gpw_ref[p, 9 * a + t, :, own] = sums[t]
                return 0

            lax.fori_loop(0, 3, pool, 0)
            return 0

        lax.fori_loop(0, 3, branch, 0)

        def finish(r, sums):
            rows = rows_at(r, BAND)
            t = gin_s[rows, :] * valid_ref[rows, 0:1]
            gq_s[rows, :] = t.astype(BF16)
            return sums + fold8(t)

        gb_ref[...] = lax.fori_loop(0, SIDE, finish, jnp.zeros((8, 3 * WIDE), F32))
        gn = None
        for p, (w, gw) in enumerate(((wq_ref, gwq_ref), (wk_ref, gwk_ref), (wv_ref, gwv_ref))):
            piece = gq_s[:, p * WIDE : (p + 1) * WIDE]
            gw[...] = tn(n_s[...], piece).astype(gw.dtype)
            term = nt(piece, w[...])
            gn = term if gn is None else gn + term

        @pl.when(g == 0)
        def _():
            gn_s[...] = gn

        @pl.when(g > 0)
        def _():
            gn_s[...] += gn

    @pl.when((h == PER - 1) & (g == GROUPS - 1))
    def _():
        def body(i, sums):
            rows = rows_at(i, BAND)
            xh, rstd = row_norm(x_ref[rows, :].astype(F32))
            gy = gn_s[rows, :]
            gx = gy * vec_ref[0:1, :]
            m1 = jnp.mean(gx, axis=-1, keepdims=True)
            m2 = jnp.mean(gx * xh, axis=-1, keepdims=True)
            gx_ref[rows, :] = gm_ref[rows, :] + (gx - m1 - xh * m2) * rstd
            return sums[0] + fold8(gy * xh), sums[1] + fold8(gy)

        zero = jnp.zeros((8, D), F32)
        sums = lax.fori_loop(0, SIDE, body, (zero, zero))
        small_ref[0] = sums[0]
        small_ref[1] = sums[1]


def position_tables():
    spot = np.arange(LENGTH) // FRAMES
    frame, row, column = np.arange(LENGTH) % FRAMES, spot // SIDE, spot % SIDE
    kinds = ((frame, FRAMES, 0), (row, SIDE, FRAMES), (column, SIDE, FRAMES + SIDE))
    bases = (FRAMES - 1, 2 * FRAMES - 1 + SIDE - 1, 2 * FRAMES - 1 + 2 * SIDE - 1 + SIDE - 1)
    pick = np.zeros((PAIRS, REL_ROWS), np.float32)
    squeeze = np.zeros((PAIRS, LANES), np.float32)
    select = np.zeros((LENGTH, PAIRS), np.float32)
    marks = np.zeros((LENGTH, LANES), np.float32)
    for tile, ((where, size, first), base) in enumerate(zip(kinds, bases)):
        for at in range(size):
            for m in range(size):
                col = tile * LANES + at * size + m
                pick[col, base + at - m] = 1.0
                squeeze[col, HEAD_DIM + first + m] = 1.0
                select[:, col] = where == at
        marks[np.arange(LENGTH), HEAD_DIM + first + where] = 1.0
    inside = (row < SMALL_SIDE) & (column < SMALL_SIDE)
    memory_at = np.arange(KEYS - LENGTH) % (MEM // 2)
    half, small = (SIDE + 1) // 2, (SMALL_SIDE + 1) // 2
    memory_inside = (memory_at // half % half < small) & (memory_at % half < small)
    exists = np.arange(KEYS - LENGTH) < MEM
    return pick, squeeze, select, marks, inside, memory_inside & exists, exists


def blocked(shape, index, single=False):
    if single:
        return pl.BlockSpec(shape, index, pipeline_mode=pl.Buffered(1))
    return pl.BlockSpec(shape, index)


def const(shape):
    return blocked(shape, lambda *_: (0,) * len(shape), True)


def to_spots(x):
    return x.reshape(FRAMES, SPOTS, -1).transpose(1, 0, 2).reshape(LENGTH, -1)


def to_frames(x):
    return x.reshape(SPOTS, FRAMES, -1).transpose(1, 0, 2).reshape(LENGTH, -1)


def sds(shape, dtype):
    return jax.ShapeDtypeStruct(shape, dtype)


def per_device(
    inputs, res_ids, memory, gain_one, bias_one, w_qkv, b_qkv, pool_weight, pool_gain, pool_bias, rel_table,
    w_proj, b_proj, gain_two, bias_two, w_up, b_up, w_down, b_down, cotangent,
):
    split = lax.axis_size("tensor")
    pick, squeeze, select, marks, inside, memory_inside, exists = position_tables()
    up_all = lax.all_gather(w_up, "tensor")
    down_all = lax.all_gather(w_down, "tensor")
    bu_all = lax.all_gather(b_up.reshape(1, -1), "tensor")

    large = res_ids[0] == 1
    valid = (large | inside).astype(F32)
    valid_rows = jnp.broadcast_to(valid[:, None], (LENGTH, LANES))
    x = to_spots(inputs)
    cot = to_spots(cotangent)
    vec = jnp.stack([gain_one, bias_one, gain_two, bias_two, b_proj, b_down, b_down, b_down])
    pw = jnp.pad(jnp.tile(pool_weight, (1, 1, PER)), ((0, 0), (0, 5), (0, 0)))
    ln = jnp.pad(jnp.concatenate([pool_gain, pool_bias]), ((0, 2), (0, LANES - HEAD_DIM)))
    tall = jnp.dot(pick, rel_table, precision=lax.Precision.HIGHEST)
    tall = jnp.pad(tall, ((0, 0), (0, LANES - HEAD_DIM))).astype(BF16)
    cmp = jnp.asarray(squeeze, BF16)
    lanes = np.arange(LANES)
    bar = np.where(lanes == MASK_LANE, np.float32(NEG), np.float32(0))
    kc = marks + (1.0 - valid)[:, None] * bar
    memory_ok = ((large & exists) | memory_inside).astype(F32)
    heads = memory.reshape(2, MEM, HEADS, HEAD_DIM).transpose(0, 2, 1, 3)
    heads = jnp.pad(heads, ((0, 0), (0, 0), (0, KEYS - LENGTH - MEM), (0, LANES - HEAD_DIM)))
    memk = heads[0] + ((1.0 - memory_ok)[:, None] * bar).astype(BF16)
    memv = heads[1] + ((lanes == HEAD_DIM) | (lanes == HEAD_DIM + 1)).astype(BF16)
    bq = b_qkv.reshape(1, -1)

    params = pltpu.CompilerParams(vmem_limit_bytes=VMEM_LIMIT)
    w_spec = [blocked((D, WIDE), lambda g, h, p=p: (0, GROUPS * p + g)) for p in range(3)]
    b_spec = [blocked((1, WIDE), lambda g, h, p=p: (0, GROUPS * p + g)) for p in range(3)]

    def per_group(*shape):
        return blocked(shape, lambda g, h: (g,) + (0,) * (len(shape) - 1))

    def per_head(*shape):
        return blocked(shape, lambda g, h: (PER * g + h,) + (0,) * (len(shape) - 1))

    field_spec = blocked((SPOTS, 8, 3 * WIDE), lambda g, h: (0, 0, g))
    att_spec = blocked((LENGTH, WIDE), lambda g, h: (0, g))
    mid, field, xh, qx, kx, vx, probs, outs, att = pl.pallas_call(
        fwd_kernel,
        grid=(GROUPS, PER),
        in_specs=[
            const((LENGTH, D)), const((8, D)), const((SPOTS, 8, LANES)), *w_spec, *b_spec,
            const((3, 32, WIDE)), const((8, LANES)), const((PAIRS, LANES)), const((PAIRS, LANES)),
            const((LENGTH, PAIRS)), const((LENGTH, LANES)),
            per_group(PER, KEYS - LENGTH, LANES), per_group(PER, KEYS - LENGTH, LANES),
            blocked((WIDE, D), lambda g, h: (g, 0)),
        ],
        out_specs=[
            const((LENGTH, D)), field_spec, per_group(PER, 3, LENGTH, LANES), per_group(PER, LENGTH, LANES),
            per_group(PER, KEYS, LANES), per_group(PER, KEYS, LANES), per_head(1, LENGTH, KEYS),
            per_head(1, LENGTH, LANES), att_spec,
        ],
        out_shape=[
            sds((LENGTH, D), F32), sds((SPOTS, 8, 3 * D), F32), sds((HEADS, 3, LENGTH, LANES), F32),
            sds((HEADS, LENGTH, LANES), BF16), sds((HEADS, KEYS, LANES), BF16), sds((HEADS, KEYS, LANES), BF16),
            sds((HEADS, LENGTH, KEYS), BF16), sds((HEADS, LENGTH, LANES), F32), sds((LENGTH, D), BF16),
        ],
        scratch_shapes=[
            pltpu.VMEM((LENGTH, D), BF16),
            pltpu.VMEM((3, SPOTS + 2 * SIDE, 8, 3 * WIDE), F32),
            pltpu.VMEM((SPOTS, 8, 3 * WIDE), F32),
            pltpu.VMEM((PER, LENGTH, LANES), F32),
            pltpu.VMEM((LENGTH, D), F32),
        ],
        compiler_params=params,
        name="attend",
        cost_estimate=pl.CostEstimate(flops=2 * 3_500_000_000, bytes_accessed=60_000_000, transcendentals=6_500_000),
    )(
        x, vec, valid_rows.reshape(SPOTS, 8, LANES), w_qkv, w_qkv, w_qkv, bq, bq, bq, pw, ln,
        tall, cmp, jnp.asarray(select), kc, memk, memv, w_proj,
    )

    hidden = w_up.shape[1]
    piece = 384
    parts = hidden // piece
    out, gm, gml, small, gup, gbu, gdown = pl.pallas_call(
        mlp_kernel,
        grid=(split * parts,),
        in_specs=[
            const((LENGTH, D)), const((LENGTH, D)), const((8, D)), const((LENGTH, LANES)),
            blocked((1, D, piece), lambda i: (i // parts, 0, i % parts)),
            blocked((1, 1, piece), lambda i: (i // parts, 0, i % parts)),
            blocked((1, piece, D), lambda i: (i // parts, i % parts, 0)),
        ],
        out_specs=[
            const((LENGTH, D)), const((LENGTH, D)), const((LENGTH, D)), const((4, 8, D)),
            blocked((1, D, piece), lambda i: (i // parts, 0, i % parts)),
            blocked((1, 8, piece), lambda i: (i // parts, 0, i % parts)),
            blocked((1, piece, D), lambda i: (i // parts, i % parts, 0)),
        ],
        out_shape=[
            sds((LENGTH, D), BF16), sds((LENGTH, D), F32), sds((LENGTH, D), BF16), sds((4, 8, D), F32),
            sds((split, D, hidden), BF16), sds((split, 8, hidden), F32), sds((split, hidden, D), BF16),
        ],
        scratch_shapes=[
            pltpu.VMEM((LENGTH, D), BF16),
            pltpu.VMEM((D, LENGTH), BF16),
            pltpu.VMEM((LENGTH, D), BF16),
            pltpu.VMEM((LENGTH, D), F32),
            pltpu.VMEM((LENGTH, D), F32),
        ],
        compiler_params=params,
        name="mlp",
        cost_estimate=pl.CostEstimate(flops=2 * 11_300_000_000, bytes_accessed=40_000_000, transcendentals=5_000_000),
    )(mid, cot, vec, valid_rows, up_all, bu_all, down_all)

    gup = lax.psum_scatter(gup, "tensor", scatter_dimension=0, tiled=False)
    gdown = lax.psum_scatter(gdown, "tensor", scatter_dimension=0, tiled=False)
    gup, gdown = lax.psum((gup, gdown), "dp")

    gx, small_one, gwq, gwk, gwv, gb, gpw, gln, gtall, gwp = pl.pallas_call(
        bwd_kernel,
        grid=(GROUPS, PER),
        in_specs=[
            const((LENGTH, D)), const((8, D)), const((LENGTH, LANES)), const((LENGTH, D)), const((LENGTH, D)), *w_spec,
            const((3, 32, WIDE)), const((8, LANES)), const((PAIRS, LANES)), const((PAIRS, LANES)),
            const((LENGTH, PAIRS)), blocked((WIDE, D), lambda g, h: (g, 0)), blocked((SPOTS, 8, 3 * WIDE), lambda g, h: (0, 0, g), True),
            per_head(1, 3, LENGTH, LANES), per_head(1, LENGTH, LANES), per_head(1, KEYS, LANES),
            per_head(1, KEYS, LANES), per_head(1, LENGTH, KEYS), per_head(1, LENGTH, LANES), att_spec,
        ],
        out_specs=[
            const((LENGTH, D)), const((2, 8, D)),
            *[blocked((D, WIDE), lambda g, h: (0, g)) for _ in range(3)],
            blocked((8, 3 * WIDE), lambda g, h: (0, g)),
            blocked((3, TAPS, 8, WIDE), lambda g, h: (0, 0, 0, g)),
            const((6, 8, LANES)), const((PAIRS, LANES)), blocked((WIDE, D), lambda g, h: (g, 0)),
        ],
        out_shape=[
            sds((LENGTH, D), F32), sds((2, 8, D), F32), sds((D, D), BF16), sds((D, D), BF16), sds((D, D), BF16),
            sds((8, 3 * D), F32), sds((3, TAPS, 8, D), F32), sds((6, 8, LANES), F32), sds((PAIRS, LANES), F32),
            sds((D, D), BF16),
        ],
        scratch_shapes=[
            pltpu.VMEM((LENGTH, D), BF16),
            pltpu.VMEM((PER, LENGTH, LANES), F32),
            pltpu.VMEM((LENGTH, KEYS), BF16),
            pltpu.VMEM((PER, 3, LENGTH, LANES), F32),
            pltpu.VMEM((3, SPOTS + 2 * SIDE, 8, WIDE), F32),
            pltpu.VMEM((LENGTH, 3 * WIDE), BF16),
            pltpu.VMEM((LENGTH, 3 * WIDE), F32),
            pltpu.VMEM((LENGTH, D), F32),
        ],
        compiler_params=params,
        name="attend_back",
        cost_estimate=pl.CostEstimate(flops=2 * 7_000_000_000, bytes_accessed=60_000_000, transcendentals=0),
    )(
        x, vec, valid_rows, gm, gml, w_qkv, w_qkv, w_qkv, pw, ln, tall, cmp, jnp.asarray(select), w_proj,
        field, xh, qx, kx, vx, probs, outs, att,
    )

    gb = jnp.sum(gb, axis=0).reshape(GROUPS, 3, WIDE).transpose(1, 0, 2).reshape(-1)
    gpw = jnp.sum(gpw.reshape(3, TAPS, 8, HEADS, HEAD_DIM), axis=(2, 3))
    gln = jnp.sum(gln, axis=1)[:, :HEAD_DIM]
    grel = jnp.dot(pick.T, gtall[:, :HEAD_DIM], precision=lax.Precision.HIGHEST)
    small = jnp.sum(small, axis=1)
    small_one = jnp.sum(small_one, axis=1)
    gbu = lax.psum(jnp.sum(gbu, axis=1), ("dp", "tensor"))
    gbu = lax.dynamic_index_in_dim(gbu, lax.axis_index("tensor"), 0, False)
    gw = lax.psum((gwq, gwk, gwv, gwp), ("dp", "tensor"))
    gb, gpw, gln, grel, small, small_one = lax.psum((gb, gpw, gln, grel, small, small_one), ("dp", "tensor"))
    return (
        to_frames(out),
        to_frames(gx),
        small_one[0],
        small_one[1],
        jnp.concatenate(gw[:3], axis=1).astype(F32),
        gb,
        gpw,
        gln[:3],
        gln[3:],
        grel,
        gw[3].astype(F32),
        small[3],
        small[0],
        small[1],
        gup.astype(F32),
        gbu,
        gdown.astype(F32),
        small[2],
    )


def solution(mesh):
    rows = P(("dp", "tensor"), None)
    return jax.shard_map(
        per_device,
        mesh=mesh,
        in_specs=(
            rows, P(("dp", "tensor")), P(None, ("dp", "tensor"), None), *[P()] * 12,
            P(None, "tensor"), P("tensor"), P("tensor", None), P(), rows,
        ),
        out_specs=(rows, rows, *[P()] * 12, P(None, "tensor"), P("tensor"), P("tensor", None), P()),
        check_vma=False,
    )
```

```python
import functools

import jax
import jax.numpy as jnp
import numpy as np
from jax import lax
from jax.experimental import pallas as pl
from jax.experimental.pallas import tpu as pltpu
from jax.sharding import PartitionSpec as P

D = 768
HEADS = 8
HEAD_DIM = 96
FRAMES = 8
SIDE = 10
SMALL_SIDE = 7
SPOTS = SIDE * SIDE
LENGTH = FRAMES * SPOTS
MEM = 200
KEYS = 1024
OFFSETS = FRAMES + 2 * SIDE
REL_ROWS = 53
GROUPS = 2
PER = HEADS // GROUPS
WIDE = PER * HEAD_DIM
TAPS = 27
LANES = 128
BAND = SIDE * FRAMES
CHUNK = 160
PAIRS = 384
MASK_LANE = HEAD_DIM + OFFSETS
EPS = 1e-6
SCALE = HEAD_DIM**-0.5
F32 = jnp.float32
BF16 = jnp.bfloat16
NEG = -1e30
VMEM_LIMIT = 60 * 1024 * 1024


def nn(a, b):
    return jnp.dot(a, b, preferred_element_type=F32)


def nt(a, b):
    return lax.dot_general(a, b, (((1,), (1,)), ((), ())), preferred_element_type=F32)


def tn(a, b):
    return lax.dot_general(a, b, (((0,), (0,)), ((), ())), preferred_element_type=F32)


def lane_of(shape):
    return lax.broadcasted_iota(jnp.int32, shape, len(shape) - 1)


def to_heads(tiles):
    t0, t1, t2 = tiles
    lane = lane_of(t0.shape)
    own = lane < HEAD_DIM
    h1 = pltpu.roll(jnp.where(lane >= 96, t0, t1), 32, t0.ndim - 1)
    h2 = pltpu.roll(jnp.where(lane >= 64, t1, t2), 64, t0.ndim - 1)
    h3 = pltpu.roll(t2, 96, t0.ndim - 1)
    return [jnp.where(own, h, 0.0) for h in (t0, h1, h2, h3)]


def to_dense(heads):
    p0, p1, p2, p3 = heads
    lane = lane_of(p0.shape)
    r1 = pltpu.roll(p1, 96, p0.ndim - 1)
    r2 = pltpu.roll(p2, 64, p0.ndim - 1)
    r3 = pltpu.roll(p3, 32, p0.ndim - 1)
    return [jnp.where(lane < 96, p0, r1), jnp.where(lane < 64, r1, r2), jnp.where(lane < 32, r2, r3)]


def row_norm(x):
    mean = jnp.mean(x, axis=-1, keepdims=True)
    c = x - mean
    rstd = lax.rsqrt(jnp.mean(c * c, axis=-1, keepdims=True) + EPS)
    return c * rstd, rstd


def frame_shift(x, up):
    frame = lax.broadcasted_iota(jnp.int32, x.shape, 1)
    if up:
        return jnp.where(frame == 0, 0.0, pltpu.roll(x, 1, 1))
    return jnp.where(frame == FRAMES - 1, 0.0, pltpu.roll(x, FRAMES - 1, 1))


def fold8(x):
    return jnp.sum(x.reshape(x.shape[0] // 8, 8, x.shape[1]), axis=0)


def put_rows(ref, at, v):
    for j in range(v.shape[1] // LANES):
        ref[pl.ds(at + j, 1), :] = v[:, j * LANES : (j + 1) * LANES]


def put_tiles(ref, v):
    for j in range(v.shape[1] // LANES):
        ref[0, j] = v[:, j * LANES : (j + 1) * LANES].astype(BF16)


def total(x):
    return jnp.sum(x, axis=0, keepdims=True)


def alive(r, large, shape):
    inside = jnp.where(r < SMALL_SIDE, SMALL_SIDE * FRAMES, 0)
    return jnp.where(lax.broadcasted_iota(jnp.int32, shape, 0) < inside, 1.0, large)


def is_large(res_ref):
    return jnp.where(res_ref[0] == 1, 1.0, 0.0).astype(F32)


def put_spots(tiles, r, x):
    for c in range(SIDE):
        for j, (ref, at) in enumerate(tiles):
            to = pl.ds(r * SIDE + c, FRAMES, stride=SPOTS)
            ref[(*at, to, slice(None))] = x[c * FRAMES : (c + 1) * FRAMES, j * LANES : (j + 1) * LANES]


def get_spots(tiles, r):
    rows = [
        jnp.concatenate([ref[(*at, pl.ds(r * SIDE + c, FRAMES, stride=SPOTS), slice(None))] for ref, at in tiles], axis=1)
        for c in range(SIDE)
    ]
    return jnp.concatenate(rows)


def six(ref):
    return [(ref, (j,)) for j in range(D // LANES)]


def line(ref):
    return ref[...].reshape(1, ref.shape[0])


def tile_at(j):
    return pl.ds(pl.multiple_of(j * LANES, LANES), LANES)


def rows_at(r, size):
    return pl.ds(pl.multiple_of(r * size, size), size)


def fwd_kernel(
    res_ref, x_ref, gain_ref, bias_ref, bp_ref, wq_ref, wk_ref, wv_ref, bq_ref, bk_ref, bv_ref, pw_ref, ln_ref,
    tall_ref, cmp_ref, sel_ref, marks_ref, code_ref, mem_ref, wp_ref,
    mid_ref, xs_ref, field_ref, xh_ref, q_ref, k_ref, v_ref, p_ref, o_ref, att_ref,
    n_s, fld_s, pool_s, q_s, acc_s,
):
    g, h = pl.program_id(0), pl.program_id(1)
    large = is_large(res_ref)

    @pl.when((g == 0) & (h == 0))
    def _():
        for j in range(D // LANES):
            acc_s[j] = x_ref[:, j * LANES : (j + 1) * LANES].astype(F32)

        def body(i, _):
            rows = rows_at(i, BAND)
            x = get_spots(six(acc_s), i)
            mid_ref[rows, :] = x + line(bp_ref)
            xs_ref[rows, :] = x.astype(BF16)
            xh, _ = row_norm(x)
            n_s[rows, :] = (xh * line(gain_ref) + line(bias_ref)).astype(BF16)
            return 0

        lax.fori_loop(0, SIDE, body, 0)
        for a in range(3):
            fld_s[a, 0:SIDE] = jnp.zeros((SIDE, 8, WIDE), F32)
            fld_s[a, SPOTS + SIDE : SPOTS + 2 * SIDE] = jnp.zeros((SIDE, 8, WIDE), F32)

    @pl.when(h == 0)
    def _():
        for p, (w, b) in enumerate(((wq_ref, bq_ref), (wk_ref, bk_ref), (wv_ref, bv_ref))):
            y = nn(n_s[...], w[...]) + b[...]
            field_ref[:, :, p * WIDE : (p + 1) * WIDE] = y.reshape(SPOTS, 8, WIDE)

        def branch(p, _):
            def spread(r, _):
                spots = rows_at(r, SIDE)
                ok = alive(r, large, (BAND, LANES)).reshape(SIDE, 8, LANES)
                there = rows_at(r + 1, SIDE)
                for j in range(3):
                    lanes, own = tile_at(3 * p + j), slice(j * LANES, (j + 1) * LANES)
                    y = field_ref[spots, :, lanes] * ok
                    field_ref[spots, :, lanes] = y
                    fld_s[0, there, :, own] = frame_shift(y, True)
                    fld_s[1, there, :, own] = y
                    fld_s[2, there, :, own] = frame_shift(y, False)
                return 0

            lax.fori_loop(0, SIDE, spread, 0)

            def pool(j, _):
                lanes, own = tile_at(3 * p + j), tile_at(j)
                w = [jnp.broadcast_to(pw_ref[p, t : t + 1, own], (8, LANES)) for t in range(TAPS)]

                def row(r, _):
                    acc = [None] * SIDE
                    for c_in in range(SIDE):
                        for b in range(3):
                            for a in range(3):
                                x = fld_s[a, (r + b) * SIDE + c_in, :, own]
                                for e in range(3):
                                    c = c_in - e + 1
                                    if 0 <= c < SIDE:
                                        term = w[9 * a + 3 * b + e] * x
                                        acc[c] = term if acc[c] is None else acc[c] + term
                    for c in range(SIDE):
                        pool_s[r * SIDE + c, :, lanes] = acc[c]
                    return 0

                lax.fori_loop(0, SIDE, row, 0)
                return 0

            lax.fori_loop(0, 3, pool, 0)
            return 0

        lax.fori_loop(0, 3, branch, 0)
        lane = lane_of((BAND, LANES))

        def norm(r, _):
            spots, rows = rows_at(r, SIDE), rows_at(r, BAND)
            bar = jnp.where(lane == MASK_LANE, NEG, 0.0) * (1.0 - alive(r, large, (BAND, LANES)))
            for p in range(3):
                tiles = [
                    pool_s[spots, :, (3 * p + j) * LANES : (3 * p + j + 1) * LANES].reshape(BAND, LANES)
                    for j in range(3)
                ]
                for i, x in enumerate(to_heads(tiles)):
                    mean = jnp.sum(x, axis=-1, keepdims=True) * (1 / HEAD_DIM)
                    c = jnp.where(lane < HEAD_DIM, x - mean, 0.0)
                    var = jnp.sum(c * c, axis=-1, keepdims=True) * (1 / HEAD_DIM)
                    rstd = lax.rsqrt(var + EPS)
                    xh = c * rstd
                    xh_ref[i, p, rows, :] = jnp.where(lane == HEAD_DIM, rstd, xh)
                    y = xh * ln_ref[p : p + 1, :] + ln_ref[3 + p : 4 + p, :]
                    if p == 0:
                        q_s[i, rows, :] = y
                    elif p == 1:
                        k_ref[i, rows, :] = (y + marks_ref[rows, :] + bar).astype(BF16)
                    else:
                        one = (lane == HEAD_DIM) | (lane == HEAD_DIM + 1)
                        v_ref[i, rows, :] = jnp.where(one, 1.0, y).astype(BF16)
            return 0

        lax.fori_loop(0, SIDE, norm, 0)
        code = code_ref[...]
        out = 1.0 - jnp.where(code == 2.0, 1.0, code * large)
        lane_m = lane_of(code.shape)
        for a, ref in enumerate((k_ref, v_ref)):
            tiles = [mem_ref[a, :, j * LANES : (j + 1) * LANES].astype(F32) for j in range(3)]
            for i, m in enumerate(to_heads(tiles)):
                if a == 0:
                    m = jnp.where(lane_m == MASK_LANE, out * NEG, m)
                else:
                    m = jnp.where((lane_m == HEAD_DIM) | (lane_m == HEAD_DIM + 1), 1.0, m)
                ref[i, LENGTH:KEYS, :] = m.astype(BF16)

    def prepare(r, _):
        rows = rows_at(r, CHUNK)
        q = q_s[h, rows, :]
        near = (nt(q.astype(BF16), tall_ref[...]) * sel_ref[rows, :]).astype(BF16)
        lane = lane_of((CHUNK, LANES))
        ext = q * SCALE + nn(near, cmp_ref[...])
        q_ref[h, rows, :] = jnp.where(lane == MASK_LANE, 1.0, ext).astype(BF16)
        return 0

    lax.fori_loop(0, LENGTH // CHUNK, prepare, 0)

    def attend(r, _):
        rows = rows_at(r, CHUNK)
        lane = lane_of((CHUNK, LANES))
        s = nt(q_ref[h, rows, :], k_ref[h])
        e = jnp.exp(s - jnp.max(s, axis=-1, keepdims=True)).astype(BF16)
        p_ref[0, rows, :] = e
        o = nn(e, v_ref[h])
        total = o[:, HEAD_DIM : HEAD_DIM + 1]
        o = jnp.where(lane < HEAD_DIM, o * (1.0 / total), 0.0)
        o_ref[0, rows, :] = jnp.where(lane == HEAD_DIM, total, o)
        q_s[h, rows, :] += o
        return 0

    lax.fori_loop(0, LENGTH // CHUNK, attend, 0)

    @pl.when(h == PER - 1)
    def _():
        def join(r, _):
            rows = rows_at(r, BAND)
            for j, t in enumerate(to_dense([q_s[i, rows, :] for i in range(PER)])):
                att_ref[rows, j * LANES : (j + 1) * LANES] = t.astype(BF16)
            return 0

        lax.fori_loop(0, SIDE, join, 0)
        mid_ref[...] += nn(att_ref[...], wp_ref[...])


def mlp_kernel(
    res_ref, mid_ref, cot_ref, gain_ref, bias_ref, bd_ref, up_ref, bu_ref, down_ref,
    out_ref, gm_ref, gml_ref, small_ref, gup_ref, gdown_ref,
    n_s, nt_s, go_s, y_s, gn_s, wide_s, stage_s,
):
    step = pl.program_id(0)
    large = is_large(res_ref)

    @pl.when(step == 0)
    def _():
        for j in range(D // LANES):
            stage_s[j] = cot_ref[:, j * LANES : (j + 1) * LANES].astype(F32)

        def body(i, sums):
            rows = rows_at(i, BAND)
            xh, _ = row_norm(mid_ref[rows, :])
            n_s[rows, :] = (xh * line(gain_ref) + line(bias_ref)).astype(BF16)
            go = get_spots(six(stage_s), i) * alive(i, large, (BAND, D))
            wide_s[rows, :] = go
            go_s[rows, :] = go.astype(BF16)
            return sums + fold8(go)

        sums = lax.fori_loop(0, SIDE, body, jnp.zeros((8, D), F32))
        put_rows(small_ref, 12, total(sums))
        nt_s[...] = n_s[...].T

    pre = nn(n_s[...], up_ref[0]) + bu_ref[0].astype(F32)[0:1, :]
    cdf = 0.5 * (1.0 + lax.erf(pre * 0.7071067811865476))
    act = (pre * cdf).astype(BF16)
    slope = cdf + pre * jnp.exp(pre * pre * -0.5) * 0.3989422804014327
    ga = nt(go_s[...], down_ref[0])
    gh = ga * slope
    put_rows(small_ref, 24 + step * (gh.shape[1] // LANES), total(fold8(gh)))
    ghl = gh.astype(BF16)
    put_tiles(gdown_ref, tn(act, go_s[...]))
    put_tiles(gup_ref, nn(nt_s[...], ghl))
    y = nn(act, down_ref[0])
    gn = nt(ghl, up_ref[0])

    @pl.when(step == 0)
    def _():
        y_s[...] = y
        gn_s[...] = gn

    @pl.when(step > 0)
    def _():
        y_s[...] += y
        gn_s[...] += gn

    @pl.when(step == pl.num_programs(0) - 1)
    def _():
        def body(i, sums):
            rows = rows_at(i, BAND)
            mid = mid_ref[rows, :]
            put_spots(six(stage_s), i, (mid + y_s[rows, :] + line(bd_ref)) * alive(i, large, (BAND, D)))
            xh, rstd = row_norm(mid)
            gy = gn_s[rows, :]
            gx = gy * line(gain_ref)
            m1 = jnp.mean(gx, axis=-1, keepdims=True)
            m2 = jnp.mean(gx * xh, axis=-1, keepdims=True)
            gm = wide_s[rows, :] + (gx - m1 - xh * m2) * rstd
            gm_ref[rows, :] = gm
            gml_ref[rows, :] = gm.astype(BF16)
            return sums[0] + fold8(gy * xh), sums[1] + fold8(gy), sums[2] + fold8(gm)

        zero = jnp.zeros((8, D), F32)
        sums = lax.fori_loop(0, SIDE, body, (zero, zero, zero))
        for j in range(D // LANES):
            out_ref[:, j * LANES : (j + 1) * LANES] = stage_s[j].astype(BF16)
        for at, v in zip((0, 6, 18), sums):
            put_rows(small_ref, at, total(v))


def bwd_kernel(
    res_ref, x_ref, gain_ref, bias_ref, gm_ref, gml_ref, wq_ref, wk_ref, wv_ref, pw_ref, ln_ref,
    tall_ref, cmp_ref, sel_ref, pick_ref, wp_ref, field_ref, xh_ref, q_ref, k_ref, v_ref, p_ref, o_ref, att_ref,
    gx_ref, small_ref, gwq_ref, gwk_ref, gwv_ref, gwp_ref,
    gpw_s, gtall_s, n_s, do_s, ds_s, dpp_s, g_s, gq_s, gin_s, gn_s,
):
    g, h = pl.program_id(0), pl.program_id(1)
    large = is_large(res_ref)

    @pl.when((g == 0) & (h == 0))
    def _():
        def body(i, _):
            rows = rows_at(i, BAND)
            xh, _ = row_norm(x_ref[rows, :].astype(F32))
            n_s[rows, :] = (xh * line(gain_ref) + line(bias_ref)).astype(BF16)
            return 0

        lax.fori_loop(0, SIDE, body, 0)
        for a in range(3):
            g_s[a, 0:SIDE] = jnp.zeros((SIDE, 8, WIDE), F32)
            g_s[a, SPOTS + SIDE : SPOTS + 2 * SIDE] = jnp.zeros((SIDE, 8, WIDE), F32)
        gtall_s[...] = jnp.zeros(gtall_s.shape, F32)
        small_ref[...] = jnp.zeros(small_ref.shape, F32)
        gpw_s[...] = jnp.zeros(gpw_s.shape, F32)

    @pl.when(h == 0)
    def _():
        gin_s[:, 0:WIDE] = nt(gml_ref[...], wp_ref[...])

        def split(r, _):
            rows = rows_at(r, BAND)
            tiles = [gin_s[rows, j * LANES : (j + 1) * LANES] for j in range(3)]
            for i, t in enumerate(to_heads(tiles)):
                do_s[i, rows, :] = t
            return 0

        lax.fori_loop(0, SIDE, split, 0)
        gw = tn(att_ref[...], gml_ref[...])
        for j in range(D // LANES):
            gwp_ref[j] = gw[:, j * LANES : (j + 1) * LANES].astype(BF16)

    lane = lane_of((LENGTH, LANES))
    do = do_s[h]
    o = o_ref[0]
    inv = 1.0 / o[:, HEAD_DIM : HEAD_DIM + 1]
    delta = jnp.sum(do * o, axis=-1, keepdims=True) * inv
    high = delta.astype(BF16).astype(F32)
    doe = jnp.where(lane == HEAD_DIM, -high, jnp.where(lane == HEAD_DIM + 1, high - delta, do * inv)).astype(BF16)
    gq_s[:, 0:LANES] = doe

    def scores(r, _):
        rows = rows_at(r, CHUNK)
        dp = nt(gq_s[rows, 0:LANES], v_ref[0])
        ds_s[rows, :] = (p_ref[0, rows, :].astype(F32) * dp).astype(BF16)
        return 0

    lax.fori_loop(0, LENGTH // CHUNK, scores, 0)
    dqe = nn(ds_s[...], k_ref[0])
    dk = tn(q_ref[0], ds_s[...]).T[:LENGTH]
    dv = tn(doe, p_ref[0]).T[:LENGTH]
    far = (nt(dqe.astype(BF16), cmp_ref[...]) * sel_ref[...]).astype(BF16)
    xq = xh_ref[0, 0]
    query = (jnp.where(lane < HEAD_DIM, xq, 0.0) * ln_ref[0:1, :] + ln_ref[3:4, :]).astype(BF16)
    gtall_s[...] += tn(far, query)
    dq = dqe * SCALE + do + nn(far, tall_ref[...])
    for p, gy in enumerate((dq, dk, dv)):
        raw = xh_ref[0, p]
        rstd = raw[:, HEAD_DIM : HEAD_DIM + 1]
        gx = gy * ln_ref[p : p + 1, :]
        m1 = jnp.sum(gx, axis=-1, keepdims=True) * (1 / HEAD_DIM)
        m2 = jnp.sum(gx * raw, axis=-1, keepdims=True) * (1 / HEAD_DIM)
        dpp_s[h, p] = (gx - m1 - raw * m2) * rstd
        small_ref[96 + p : 97 + p, :] += total(fold8(gy * raw))
        small_ref[99 + p : 100 + p, :] += total(fold8(gy))

    @pl.when(h == PER - 1)
    def _():
        def branch(p, _):
            def spread(r, _):
                there, rows = rows_at(r + 1, SIDE), rows_at(r, BAND)
                for j, t in enumerate(to_dense([dpp_s[i, p, rows, :] for i in range(PER)])):
                    lanes = slice(j * LANES, (j + 1) * LANES)
                    t = t.reshape(SIDE, 8, LANES)
                    g_s[0, there, :, lanes] = frame_shift(t, False)
                    g_s[1, there, :, lanes] = t
                    g_s[2, there, :, lanes] = frame_shift(t, True)
                return 0

            lax.fori_loop(0, SIDE, spread, 0)

            def pool(j, _):
                lanes, own = tile_at(3 * p + j), tile_at(j)
                for a in range(3):
                    w = [
                        jnp.broadcast_to(pw_ref[p, t : t + 1, own], (8, LANES))
                        for t in range(9 * a, 9 * a + 9)
                    ]

                    def row(r, sums):
                        sums = list(sums)
                        x = [field_ref[r * SIDE + c, :, lanes] for c in range(SIDE)]
                        acc = [None] * SIDE
                        for c_in in range(SIDE):
                            for b in range(3):
                                t = g_s[a, (r + 2 - b) * SIDE + c_in, :, own]
                                for e in range(3):
                                    c = c_in + e - 1
                                    if 0 <= c < SIDE:
                                        term = w[3 * b + e] * t
                                        acc[c] = term if acc[c] is None else acc[c] + term
                                        sums[3 * b + e] = sums[3 * b + e] + x[c] * t
                        for c in range(SIDE):
                            at = pl.ds(pl.multiple_of(r * BAND + c * 8, 8), 8)
                            if a == 0:
                                gin_s[at, lanes] = acc[c]
                            else:
                                gin_s[at, lanes] += acc[c]
                        return tuple(sums)

                    sums = lax.fori_loop(0, SIDE, row, tuple(jnp.zeros((8, LANES), F32) for _ in range(9)))
                    for t in range(9):
                        gpw_s[9 * a + t : 9 * a + t + 1, own] = total(sums[t])
                return 0

            lax.fori_loop(0, 3, pool, 0)
            heads = to_heads([gpw_s[:, j * LANES : (j + 1) * LANES] for j in range(3)])
            small_ref[rows_at(p, 32), :] += heads[0] + heads[1] + heads[2] + heads[3]
            return 0

        lax.fori_loop(0, 3, branch, 0)

        def finish(r, sums):
            rows = rows_at(r, BAND)
            t = gin_s[rows, :] * alive(r, large, (BAND, 3 * WIDE))
            gq_s[rows, :] = t.astype(BF16)
            return sums + fold8(t)

        put_rows(small_ref, 168 + 9 * g, total(lax.fori_loop(0, SIDE, finish, jnp.zeros((8, 3 * WIDE), F32))))
        gn = None
        for p, (w, gw) in enumerate(((wq_ref, gwq_ref), (wk_ref, gwk_ref), (wv_ref, gwv_ref))):
            piece = gq_s[:, p * WIDE : (p + 1) * WIDE]
            value = tn(n_s[...], piece)
            for j in range(WIDE // LANES):
                gw[j] = value[:, j * LANES : (j + 1) * LANES].astype(BF16)
            term = nt(piece, w[...])
            gn = term if gn is None else gn + term

        @pl.when(g == 0)
        def _():
            gn_s[...] = gn

        @pl.when(g > 0)
        def _():
            gn_s[...] += gn

    @pl.when((h == PER - 1) & (g == GROUPS - 1))
    def _():
        stage = [(dpp_s, (j // 3, j % 3)) for j in range(D // LANES)]

        def body(i, sums):
            rows = rows_at(i, BAND)
            xh, rstd = row_norm(x_ref[rows, :].astype(F32))
            gy = gn_s[rows, :]
            gx = gy * line(gain_ref)
            m1 = jnp.mean(gx, axis=-1, keepdims=True)
            m2 = jnp.mean(gx * xh, axis=-1, keepdims=True)
            put_spots(stage, i, gm_ref[rows, :] + (gx - m1 - xh * m2) * rstd)
            return sums[0] + fold8(gy * xh), sums[1] + fold8(gy)

        zero = jnp.zeros((8, D), F32)
        sums = lax.fori_loop(0, SIDE, body, (zero, zero))
        for j, (ref, at) in enumerate(stage):
            gx_ref[:, j * LANES : (j + 1) * LANES] = ref[at]
        put_rows(small_ref, 186, total(sums[0]))
        put_rows(small_ref, 192, total(sums[1]))
        rest, rel = gtall_s[...], None
        for _ in range(3):
            part = rest.astype(BF16)
            rest = rest - part.astype(F32)
            term = nn(pick_ref[...], part)
            rel = term if rel is None else rel + term
        small_ref[104:168, :] = rel


def bit_of(axis, bit):
    return lax.axis_index(axis) // bit % 2


def partner_of(axis, bit):
    me = lax.axis_index(axis)
    return {axis: me + (1 - 2 * (me // bit % 2)) * bit}


def halvings(rows):
    count = 0
    while rows % (32 << count) == 0:
        count += 1
    return count


def reduce_kernel(parts, pieces, links, *refs):
    n = len(pieces)
    ins, one, two, out, small = refs[:n], refs[n], refs[n + 1], refs[n + 2], refs[n + 3]
    big, land, small_land, load_sem, send_sem, recv_sem, back_sem, home_sem, ssend_sem, srecv_sem = refs[n + 4 :]
    loads = [
        pltpu.make_async_copy(ref, big.at[pl.ds(first, rows)], load_sem.at[i])
        for i, (ref, (first, rows)) in enumerate(zip(ins, pieces))
    ]
    for copy in loads:
        copy.start()
    barrier = pltpu.get_barrier_semaphore()
    for link in links:
        pl.semaphore_signal(barrier, inc=1, device_id=partner_of(*link), device_id_type=pl.DeviceIdType.MESH)
    pl.semaphore_wait(barrier, len(links))
    small[0 : one.shape[0]] = one[...]
    small[one.shape[0] :] = two[...]
    for copy in loads:
        copy.wait()

    def send(src, dst, one, two, link):
        return pltpu.make_async_remote_copy(
            src_ref=src, dst_ref=dst, send_sem=one, recv_sem=two,
            device_id=partner_of(*link), device_id_type=pl.DeviceIdType.MESH,
        )

    spans = [[(first, rows)] for first, rows, _ in parts]
    for s in range(max(len(order) for _, _, order in parts)):
        flying = []
        for i, (first, rows, order) in enumerate(parts):
            if s >= len(order):
                continue
            off, size = spans[i][-1]
            half = size // 2
            bit = bit_of(*order[s])
            keep, give, at = off + bit * half, off + (1 - bit) * half, first + rows - size
            if halvings(rows) <= s:
                keep, give, half = off, off, size
            copy = send(
                big.at[pl.ds(pl.multiple_of(give, 16), half)], land.at[pl.ds(at, half)], send_sem.at[i, s], recv_sem.at[i, s], order[s]
            )
            copy.start()
            flying.append((copy, keep, half, at))
            spans[i].append((keep, half))
        extra = None
        if s < len(links):
            extra = send(small, small_land.at[s], ssend_sem.at[s], srecv_sem.at[s], links[s])
            extra.start()
        for copy, keep, half, at in flying:
            copy.wait()
            block = next(b for b in (512, 256, 128, 64, 48, 32, 16) if half % b == 0)

            def add(k, _):
                a = pl.ds(pl.multiple_of(keep + k * block, 16), block)
                b = pl.ds(pl.multiple_of(at + k * block, 16), block)
                big[a, :] = (big[a, :].astype(F32) + land[b, :].astype(F32)).astype(BF16)
                return 0

            lax.fori_loop(0, half // block, add, 0)
        if extra is not None:
            extra.wait()
            small[...] += small_land[s]
    for span in spans:
        off, size = span[-1]
        own = pl.ds(pl.multiple_of(off, 16), size)
        out[own, :] = big[own, :]
    depth = max(len(order) for _, _, order in parts)
    for s in reversed(range(depth)):
        flying = []
        for i, (first, rows, order) in enumerate(parts):
            if s >= min(len(order), halvings(rows)):
                continue
            off, size = spans[i][s + 1]
            here = out.at[pl.ds(pl.multiple_of(off, 16), size)]
            copy = send(here, here, back_sem.at[i, s], home_sem.at[i, s], order[s])
            copy.start()
            flying.append(copy)
        for copy in flying:
            copy.wait()


def bits(axis, size):
    return [(axis, 1 << k) for k in range(size.bit_length() - 1)]


def all_reduce(whole, over_dp, one, two, sizes):
    dp, tensor = bits("dp", sizes["dp"]), bits("tensor", sizes["tensor"])
    links = tensor + dp
    small = sds((one.shape[0] + two.shape[0], LANES), F32)
    pieces, at = [], 0
    for a in whole + over_dp:
        pieces.append((at, a.shape[0]))
        at += a.shape[0]
    cut = sum(a.shape[0] for a in whole)
    core, rest = tensor[:1], tensor[1:]
    third = cut // 3
    orders = (core + rest + dp, core + dp[:1] + dp[1:] + rest, core + dp[1:] + rest + dp[:1])
    parts = [(k * third, third, order) for k, order in enumerate(orders)]
    if over_dp:
        half = (at - cut) // 2
        parts += [(cut, half, dp), (cut + half, half, dp[1:] + dp[:1])]
    assert all(len(order) <= halvings(rows) + 1 for _, rows, order in parts)
    depth = max(len(order) for _, _, order in parts)
    dma = pltpu.SemaphoreType.DMA
    return pl.pallas_call(
        functools.partial(reduce_kernel, parts, pieces, links),
        in_specs=[pl.BlockSpec(memory_space=pl.ANY)] * len(pieces) + [pl.BlockSpec(memory_space=pltpu.VMEM)] * 2,
        out_specs=[pl.BlockSpec(memory_space=pltpu.VMEM)] * 2,
        out_shape=[sds((at, LANES), BF16), sds(small.shape, F32)],
        scratch_shapes=[
            pltpu.VMEM((at, LANES), BF16),
            pltpu.VMEM((at, LANES), BF16),
            pltpu.VMEM((len(links), *small.shape), F32),
            dma((len(pieces),)),
            dma((len(parts), depth)), dma((len(parts), depth)), dma((len(parts), depth)), dma((len(parts), depth)),
            dma((len(links),)), dma((len(links),)),
        ],
        compiler_params=pltpu.CompilerParams(
            vmem_limit_bytes=VMEM_LIMIT, collective_id=1, has_side_effects=True
        ),
        name="sum_all",
        cost_estimate=pl.CostEstimate(flops=10_000_000, bytes_accessed=20_000_000, transcendentals=0),
    )(*whole, *over_dp, one, two)


def unpack_kernel(big_ref, small_ref, *outs):
    squares, vectors, gb_ref, gpw_ref, gain_ref, bias_ref, rel_ref = outs[:4], outs[4:11], *outs[11:]
    for k, first, n in ((0, 0, 18), (1, 18, 6), (2, 24, 6), (3, 30, 6)):
        for j in range(n):
            squares[k][:, j * LANES : (j + 1) * LANES] = big_ref[first + j].astype(F32)

    @pl.when(pl.program_id(0) == 0)
    def _():
        own = 232 + 6 * lax.axis_index("tensor")
        for ref, at in zip(vectors, (186, 192, 226, 208, 214, 220, own)):
            for j in range(6):
                ref[j * LANES : (j + 1) * LANES] = small_ref[at + j, :]
        for g in range(GROUPS):
            for j in range(9):
                to = (j // 3) * D + g * WIDE + j % 3 * LANES
                gb_ref[to : to + LANES] = small_ref[168 + 9 * g + j, :]
        for p in range(3):
            gpw_ref[p] = small_ref[32 * p : 32 * p + TAPS, :HEAD_DIM]
        gain_ref[...] = small_ref[96:99, :HEAD_DIM]
        bias_ref[...] = small_ref[99:102, :HEAD_DIM]
        rel_ref[...] = small_ref[104 : 104 + REL_ROWS, :HEAD_DIM]


def unpack(big, small):
    def whole(*shape):
        return pl.BlockSpec(shape, lambda i: (0,) * len(shape))

    def band(width):
        return pl.BlockSpec((LANES, width), lambda i: (i, 0))

    shapes = [(D,)] * 7 + [(3 * D,), (3, TAPS, HEAD_DIM), (3, HEAD_DIM), (3, HEAD_DIM), (REL_ROWS, HEAD_DIM)]
    return pl.pallas_call(
        unpack_kernel,
        grid=(D // LANES,),
        in_specs=[pl.BlockSpec((36, LANES, LANES), lambda i: (0, i, 0)), whole(*small.shape)],
        out_specs=[band(3 * D), band(D), band(D), band(D), *[whole(*shape) for shape in shapes]],
        out_shape=[sds((D, 3 * D), F32), *[sds((D, D), F32)] * 3, *[sds(shape, F32) for shape in shapes]],
        name="unpack",
        cost_estimate=pl.CostEstimate(flops=0, bytes_accessed=22_000_000, transcendentals=0),
    )(big, small)


def position_tables():
    spot = np.arange(LENGTH) // FRAMES
    frame, row, column = np.arange(LENGTH) % FRAMES, spot // SIDE, spot % SIDE
    kinds = ((frame, FRAMES, 0), (row, SIDE, FRAMES), (column, SIDE, FRAMES + SIDE))
    bases = (FRAMES - 1, 2 * FRAMES - 1 + SIDE - 1, 2 * FRAMES - 1 + 2 * SIDE - 1 + SIDE - 1)
    pick = np.zeros((PAIRS, REL_ROWS), np.float32)
    squeeze = np.zeros((PAIRS, LANES), np.float32)
    select = np.zeros((LENGTH, PAIRS), np.float32)
    marks = np.zeros((LENGTH, LANES), np.float32)
    for tile, ((where, size, first), base) in enumerate(zip(kinds, bases)):
        for at in range(size):
            for m in range(size):
                col = tile * LANES + at * size + m
                pick[col, base + at - m] = 1.0
                squeeze[col, HEAD_DIM + first + m] = 1.0
                select[:, col] = where == at
        marks[np.arange(LENGTH), HEAD_DIM + first + where] = 1.0
    memory_at = np.arange(KEYS - LENGTH) % (MEM // 2)
    half, small = (SIDE + 1) // 2, (SMALL_SIDE + 1) // 2
    memory_inside = (memory_at // half % half < small) & (memory_at % half < small)
    exists = np.arange(KEYS - LENGTH) < MEM
    code = np.where(exists, 1.0 + memory_inside, 0.0).astype(np.float32)
    return pick, squeeze, select, marks, np.repeat(code[:, None], LANES, 1)


def blocked(shape, index, single=False):
    if single:
        return pl.BlockSpec(shape, index, pipeline_mode=pl.Buffered(1))
    return pl.BlockSpec(shape, index)


def const(shape):
    return blocked(shape, lambda *_: (0,) * len(shape), True)


def sds(shape, dtype):
    return jax.ShapeDtypeStruct(shape, dtype)


def per_device(
    inputs, res_ids, memory, gain_one, bias_one, w_qkv, b_qkv, pool_weight, pool_gain, pool_bias, rel_table,
    w_proj, b_proj, gain_two, bias_two, w_up, b_up, w_down, b_down, cotangent,
):
    split = lax.axis_size("tensor")
    pick, squeeze, select, marks, code = position_tables()
    up_all = lax.all_gather(jnp.concatenate([w_up, jnp.broadcast_to(b_up, (16, b_up.shape[0]))]), "tensor")
    down_all = lax.all_gather(w_down, "tensor")
    pw = jnp.pad(jnp.tile(pool_weight, (1, 1, PER)), ((0, 0), (0, 5), (0, 0)))
    ln = jnp.pad(jnp.concatenate([pool_gain, pool_bias]), ((0, 2), (0, LANES - HEAD_DIM)))
    tall = jnp.dot(pick, rel_table, precision=lax.Precision.HIGHEST)
    tall = jnp.pad(tall, ((0, 0), (0, LANES - HEAD_DIM))).astype(BF16)
    cmp = jnp.asarray(squeeze, BF16)
    mem = jnp.pad(memory, ((0, 0), (0, KEYS - LENGTH - MEM), (0, 0)))
    bq = b_qkv.reshape(1, -1)

    params = pltpu.CompilerParams(vmem_limit_bytes=VMEM_LIMIT)
    w_spec = [blocked((D, WIDE), lambda g, h, p=p: (0, GROUPS * p + g)) for p in range(3)]
    b_spec = [blocked((1, WIDE), lambda g, h, p=p: (0, GROUPS * p + g)) for p in range(3)]

    scalar = pl.BlockSpec(memory_space=pltpu.SMEM)
    row = const((D,))

    def per_group(*shape):
        return blocked(shape, lambda g, h: (g,) + (0,) * (len(shape) - 1))

    def per_head(*shape):
        return blocked(shape, lambda g, h: (PER * g + h,) + (0,) * (len(shape) - 1))

    field_spec = blocked((SPOTS, 8, 3 * WIDE), lambda g, h: (0, 0, g))
    att_spec = blocked((LENGTH, WIDE), lambda g, h: (0, g))
    mid, xs, field, xh, qx, kx, vx, probs, outs, att = pl.pallas_call(
        fwd_kernel,
        grid=(GROUPS, PER),
        in_specs=[
            scalar, const((LENGTH, D)), row, row, row, *w_spec, *b_spec,
            const((3, 32, WIDE)), const((8, LANES)), const((PAIRS, LANES)), const((PAIRS, LANES)),
            const((LENGTH, PAIRS)), const((LENGTH, LANES)), const((KEYS - LENGTH, LANES)),
            blocked((2, KEYS - LENGTH, WIDE), lambda g, h: (0, 0, g)),
            blocked((WIDE, D), lambda g, h: (g, 0)),
        ],
        out_specs=[
            const((LENGTH, D)), const((LENGTH, D)), field_spec, per_group(PER, 3, LENGTH, LANES), per_group(PER, LENGTH, LANES),
            per_group(PER, KEYS, LANES), per_group(PER, KEYS, LANES), per_head(1, LENGTH, KEYS),
            per_head(1, LENGTH, LANES), att_spec,
        ],
        out_shape=[
            sds((LENGTH, D), F32), sds((LENGTH, D), BF16), sds((SPOTS, 8, 3 * D), F32), sds((HEADS, 3, LENGTH, LANES), F32),
            sds((HEADS, LENGTH, LANES), BF16), sds((HEADS, KEYS, LANES), BF16), sds((HEADS, KEYS, LANES), BF16),
            sds((HEADS, LENGTH, KEYS), BF16), sds((HEADS, LENGTH, LANES), F32), sds((LENGTH, D), BF16),
        ],
        scratch_shapes=[
            pltpu.VMEM((LENGTH, D), BF16),
            pltpu.VMEM((3, SPOTS + 2 * SIDE, 8, WIDE), F32),
            pltpu.VMEM((SPOTS, 8, 3 * WIDE), F32),
            pltpu.VMEM((PER, LENGTH, LANES), F32),
            pltpu.VMEM((D // LANES, LENGTH, LANES), F32),
        ],
        compiler_params=params,
        name="attend",
        cost_estimate=pl.CostEstimate(flops=2 * 3_500_000_000, bytes_accessed=60_000_000, transcendentals=6_500_000),
    )(
        res_ids, inputs, gain_one, bias_one, b_proj, w_qkv, w_qkv, w_qkv, bq, bq, bq, pw, ln,
        tall, cmp, jnp.asarray(select), jnp.asarray(marks), jnp.asarray(code), mem, w_proj,
    )

    hidden = w_up.shape[1]
    piece = 384
    parts = hidden // piece
    tiles = hidden // LANES
    out, gm, gml, small, gup, gdown = pl.pallas_call(
        mlp_kernel,
        grid=(split * parts,),
        in_specs=[
            scalar, const((LENGTH, D)), const((LENGTH, D)), row, row, row,
            blocked((1, D, piece), lambda i: (i // parts, 0, i % parts)),
            blocked((1, 16, piece), lambda i: (i // parts, D // 16, i % parts)),
            blocked((1, piece, D), lambda i: (i // parts, i % parts, 0)),
        ],
        out_specs=[
            const((LENGTH, D)), const((LENGTH, D)), const((LENGTH, D)), const((24 + split * tiles, LANES)),
            blocked((1, piece // LANES, D, LANES), lambda i: (i // parts, i % parts, 0, 0)),
            blocked((1, D // LANES, piece, LANES), lambda i: (i // parts, 0, i % parts, 0)),
        ],
        out_shape=[
            sds((LENGTH, D), BF16), sds((LENGTH, D), F32), sds((LENGTH, D), BF16), sds((24 + split * tiles, LANES), F32),
            sds((split, tiles, D, LANES), BF16), sds((split, D // LANES, hidden, LANES), BF16),
        ],
        scratch_shapes=[
            pltpu.VMEM((LENGTH, D), BF16),
            pltpu.VMEM((D, LENGTH), BF16),
            pltpu.VMEM((LENGTH, D), BF16),
            *[pltpu.VMEM((LENGTH, D), F32)] * 3,
            pltpu.VMEM((D // LANES, LENGTH, LANES), F32),
        ],
        compiler_params=params,
        name="mlp",
        cost_estimate=pl.CostEstimate(flops=2 * 11_300_000_000, bytes_accessed=40_000_000, transcendentals=5_000_000),
    )(res_ids, mid, cotangent, gain_two, bias_two, b_down, up_all, up_all, down_all)

    gup = lax.psum_scatter(gup, "tensor", scatter_dimension=0, tiled=False)
    gdown = lax.psum_scatter(gdown, "tensor", scatter_dimension=0, tiled=False)

    gx, small_one, gwq, gwk, gwv, gwp = pl.pallas_call(
        bwd_kernel,
        grid=(GROUPS, PER),
        in_specs=[
            scalar, const((LENGTH, D)), row, row, const((LENGTH, D)), const((LENGTH, D)), *w_spec,
            const((3, 32, WIDE)), const((8, LANES)), const((PAIRS, LANES)), const((PAIRS, LANES)),
            const((LENGTH, PAIRS)), const((64, PAIRS)), blocked((WIDE, D), lambda g, h: (g, 0)),
            blocked((SPOTS, 8, 3 * WIDE), lambda g, h: (0, 0, g), True),
            per_head(1, 3, LENGTH, LANES), per_head(1, LENGTH, LANES), per_head(1, KEYS, LANES),
            per_head(1, KEYS, LANES), per_head(1, LENGTH, KEYS), per_head(1, LENGTH, LANES), att_spec,
        ],
        out_specs=[
            const((LENGTH, D)), const((208, LANES)),
            *[blocked((3, D, LANES), lambda g, h: (g, 0, 0)) for _ in range(3)],
            blocked((6, WIDE, LANES), lambda g, h: (0, g, 0)),
        ],
        out_shape=[
            sds((LENGTH, D), F32), sds((208, LANES), F32), *[sds((6, D, LANES), BF16)] * 4,
        ],
        scratch_shapes=[
            pltpu.VMEM((32, WIDE), F32),
            pltpu.VMEM((PAIRS, LANES), F32),
            pltpu.VMEM((LENGTH, D), BF16),
            pltpu.VMEM((PER, LENGTH, LANES), F32),
            pltpu.VMEM((LENGTH, KEYS), BF16),
            pltpu.VMEM((PER, 3, LENGTH, LANES), F32),
            pltpu.VMEM((3, SPOTS + 2 * SIDE, 8, WIDE), F32),
            pltpu.VMEM((LENGTH, 3 * WIDE), BF16),
            pltpu.VMEM((LENGTH, 3 * WIDE), F32),
            pltpu.VMEM((LENGTH, D), F32),
        ],
        compiler_params=params,
        name="attend_back",
        cost_estimate=pl.CostEstimate(flops=2 * 7_000_000_000, bytes_accessed=60_000_000, transcendentals=0),
    )(
        res_ids, xs, gain_one, bias_one, gm, gml, w_qkv, w_qkv, w_qkv, pw, ln, tall, cmp, jnp.asarray(select), jnp.asarray(np.pad(pick.T, ((0, 11), (0, 0))), BF16), w_proj,
        field, xh, qx, kx, vx, probs, outs, att,
    )

    flat = [a.reshape(-1, LANES) for a in (gwq, gwk, gwv, gwp, gup, gdown)]
    sizes = {axis: lax.axis_size(axis) for axis in ("dp", "tensor")}
    big, small = all_reduce(flat[:4], flat[4:], small_one, small, sizes)
    outs = unpack(big.reshape(-1, D, LANES), small)
    squares, (gain1, bias1, bp, gain2, bias2, bd, bu), (gb, gpw, pg, pb, rel) = outs[:4], outs[4:11], outs[11:]

    return (
        out, gx, gain1, bias1, squares[0], gb, gpw, pg, pb, rel, squares[1], bp, gain2, bias2, squares[2], bu, squares[3], bd,
    )


def solution(mesh):
    rows = P(("dp", "tensor"), None)
    return jax.shard_map(
        per_device,
        mesh=mesh,
        in_specs=(
            rows, P(("dp", "tensor")), P(None, ("dp", "tensor"), None), *[P()] * 12,
            P(None, "tensor"), P("tensor"), P("tensor", None), P(), rows,
        ),
        out_specs=(rows, rows, *[P()] * 12, P(None, "tensor"), P("tensor"), P("tensor", None), P()),
        check_vma=False,
    )
```

```python
import functools

import jax
import jax.numpy as jnp
import numpy as np
from jax import lax
from jax.experimental import pallas as pl
from jax.experimental.pallas import tpu as pltpu
from jax.sharding import PartitionSpec as P

D = 768
HEADS = 8
HEAD_DIM = 96
FRAMES = 8
SIDE = 10
SMALL_SIDE = 7
SPOTS = SIDE * SIDE
LENGTH = FRAMES * SPOTS
MEM = 200
KEYS = 1024
OFFSETS = FRAMES + 2 * SIDE
REL_ROWS = 53
GROUPS = 2
PER = HEADS // GROUPS
WIDE = PER * HEAD_DIM
TAPS = 27
LANES = 128
BAND = SIDE * FRAMES
CHUNK = 160
PAIRS = 384
MASK_LANE = HEAD_DIM + OFFSETS
EPS = 1e-6
SCALE = HEAD_DIM**-0.5
F32 = jnp.float32
BF16 = jnp.bfloat16
NEG = -1e30
UP_TICKS = (0, 2, 3, 4, 5, 7, 9)
DOWN_TICKS = (2, 4, 7, 8, 9, 10, 11, 14)
VMEM_LIMIT = 60 * 1024 * 1024


def nn(a, b):
    return jnp.dot(a, b, preferred_element_type=F32)


def nt(a, b):
    return lax.dot_general(a, b, (((1,), (1,)), ((), ())), preferred_element_type=F32)


def tn(a, b):
    return lax.dot_general(a, b, (((0,), (0,)), ((), ())), preferred_element_type=F32)


def lane_of(shape):
    return lax.broadcasted_iota(jnp.int32, shape, len(shape) - 1)


def to_heads(tiles):
    t0, t1, t2 = tiles
    lane = lane_of(t0.shape)
    own = lane < HEAD_DIM
    h1 = pltpu.roll(jnp.where(lane >= 96, t0, t1), 32, t0.ndim - 1)
    h2 = pltpu.roll(jnp.where(lane >= 64, t1, t2), 64, t0.ndim - 1)
    h3 = pltpu.roll(t2, 96, t0.ndim - 1)
    return [jnp.where(own, h, 0.0) for h in (t0, h1, h2, h3)]


def to_dense(heads):
    p0, p1, p2, p3 = heads
    lane = lane_of(p0.shape)
    r1 = pltpu.roll(p1, 96, p0.ndim - 1)
    r2 = pltpu.roll(p2, 64, p0.ndim - 1)
    r3 = pltpu.roll(p3, 32, p0.ndim - 1)
    return [jnp.where(lane < 96, p0, r1), jnp.where(lane < 64, r1, r2), jnp.where(lane < 32, r2, r3)]


def row_norm(x):
    mean = jnp.mean(x, axis=-1, keepdims=True)
    c = x - mean
    rstd = lax.rsqrt(jnp.mean(c * c, axis=-1, keepdims=True) + EPS)
    return c * rstd, rstd


def frame_shift(x, up):
    frame = lax.broadcasted_iota(jnp.int32, x.shape, 1)
    if up:
        return jnp.where(frame == 0, 0.0, pltpu.roll(x, 1, 1))
    return jnp.where(frame == FRAMES - 1, 0.0, pltpu.roll(x, FRAMES - 1, 1))


def fold8(x):
    return jnp.sum(x.reshape(x.shape[0] // 8, 8, x.shape[1]), axis=0)


def put_rows(ref, at, v):
    for j in range(v.shape[1] // LANES):
        ref[pl.ds(at + j, 1), :] = v[:, j * LANES : (j + 1) * LANES]


def total(x):
    return jnp.sum(x, axis=0, keepdims=True)


def alive(r, large, shape):
    inside = jnp.where(r < SMALL_SIDE, SMALL_SIDE * FRAMES, 0)
    return jnp.where(lax.broadcasted_iota(jnp.int32, shape, 0) < inside, 1.0, large)


def is_large(res_ref):
    return jnp.where(res_ref[0] == 1, 1.0, 0.0).astype(F32)


def put_spots(tiles, r, x):
    for c in range(SIDE):
        for j, (ref, at) in enumerate(tiles):
            to = pl.ds(r * SIDE + c, FRAMES, stride=SPOTS)
            ref[(*at, to, slice(None))] = x[c * FRAMES : (c + 1) * FRAMES, j * LANES : (j + 1) * LANES]


def get_spots(tiles, r):
    rows = [
        jnp.concatenate([ref[(*at, pl.ds(r * SIDE + c, FRAMES, stride=SPOTS), slice(None))] for ref, at in tiles], axis=1)
        for c in range(SIDE)
    ]
    return jnp.concatenate(rows)


def six(ref):
    return [(ref, (j,)) for j in range(D // LANES)]


def line(ref):
    return ref[...].reshape(1, ref.shape[0])


def tile_at(j):
    return pl.ds(pl.multiple_of(j * LANES, LANES), LANES)


def rows_at(r, size):
    return pl.ds(pl.multiple_of(r * size, size), size)


def bit_of(axis, bit):
    return lax.axis_index(axis) // bit % 2


def partner_of(axis, bit):
    me = lax.axis_index(axis)
    return {axis: me + (1 - 2 * (me // bit % 2)) * bit}


def halvings(rows):
    count = 0
    while rows % (32 << count) == 0:
        count += 1
    return count


def bits(axis, size):
    return [(axis, 1 << k) for k in range(size.bit_length() - 1)]


def send(src, dst, one, two, link):
    return pltpu.make_async_remote_copy(
        src_ref=src, dst_ref=dst, send_sem=one, recv_sem=two,
        device_id=partner_of(*link), device_id_type=pl.DeviceIdType.MESH,
    )


def greet(links):
    barrier = pltpu.get_barrier_semaphore()
    for link in links:
        pl.semaphore_signal(barrier, inc=1, device_id=partner_of(*link), device_id_type=pl.DeviceIdType.MESH)
    pl.semaphore_wait(barrier, len(links))


def some(start, rows):
    return pl.ds(pl.multiple_of(start, 16), rows)


def add_rows(dst, at, src, start, rows):
    block = next(b for b in (512, 256, 128, 64, 48, 32, 16) if rows % b == 0)

    def add(k, _):
        a, b = some(at + k * block, block), some(start + k * block, block)
        dst[a, :] = (dst[a, :].astype(F32) + src[b, :].astype(F32)).astype(BF16)
        return 0

    lax.fori_loop(0, rows // block, add, 0)


def chain(work, land, out, send_sem, recv_sem, own_sem, order, merge=None):
    rows, count = work.shape[0], halvings(work.shape[0])

    def span(s):
        off, size = 0, rows
        for k in range(min(s, count)):
            size //= 2
            off = off + bit_of(*order[k]) * size
        return off, size

    def halve(s, k):
        off, size = span(s)
        half, bit, at = size // 2, bit_of(*order[s]), rows - size
        keep, give = off + bit * half, off + (1 - bit) * half
        if s >= count:
            keep, give, half = off, off, size
        copy = send(work.at[some(give, half)], land.at[some(at, half)], send_sem.at[k], recv_sem.at[k], order[s])
        return copy, (work, keep, land, at, half)

    def join(k):
        ref, landing, link = merge
        return send(ref, landing, send_sem.at[k], recv_sem.at[k], link), (work, span(1)[0], landing, 0, ref.shape[0])

    def double(s, k):
        off, size = span(s + 1)
        here = out.at[some(off, size)]
        return send(here, here, send_sem.at[k], recv_sem.at[k], order[s]), None

    def own():
        off, size = span(len(order))
        copy = pltpu.make_async_copy(work.at[some(off, size)], out.at[some(off, size)], own_sem)
        copy.start()
        copy.wait()

    plans = [functools.partial(halve, s) for s in range(len(order))]
    if merge is not None:
        plans.insert(1, join)
    gather = len(plans)
    plans += [functools.partial(double, s) for s in reversed(range(min(len(order), count)))]

    def start(k):
        if k == gather:
            own()
        plans[k](k)[0].start()

    def finish(k):
        copy, todo = plans[k](k)
        copy.wait()
        if todo is not None:
            add_rows(*todo)

    def step(k):
        if k > 0:
            finish(k - 1)
        if k < len(plans):
            start(k)

    return [functools.partial(step, k) for k in range(len(plans) + 1)]


def at_ticks(tick, table, steps):
    for n in sorted(set(table)):
        due = [k for k in range(len(steps)) if table[min(k, len(table) - 1)] == n]

        @pl.when(tick == n)
        def _():
            for k in due:
                steps[k]()


def fwd_kernel(
    res_ref, x_ref, gain_ref, bias_ref, bp_ref, wq_ref, wk_ref, wv_ref, bq_ref, bk_ref, bv_ref, pw_ref, ln_ref,
    tall_ref, cmp_ref, sel_ref, marks_ref, code_ref, mem_ref, wp_ref,
    mid_ref, xs_ref, field_ref, xh_ref, q_ref, k_ref, v_ref, p_ref, o_ref, att_ref,
    n_s, fld_s, pool_s, q_s, acc_s,
):
    g, h = pl.program_id(0), pl.program_id(1)
    large = is_large(res_ref)

    @pl.when((g == 0) & (h == 0))
    def _():
        for j in range(D // LANES):
            acc_s[j] = x_ref[:, j * LANES : (j + 1) * LANES].astype(F32)

        def body(i, _):
            rows = rows_at(i, BAND)
            x = get_spots(six(acc_s), i)
            mid_ref[rows, :] = x + line(bp_ref)
            xs_ref[rows, :] = x.astype(BF16)
            xh, _ = row_norm(x)
            n_s[rows, :] = (xh * line(gain_ref) + line(bias_ref)).astype(BF16)
            return 0

        lax.fori_loop(0, SIDE, body, 0)
        for a in range(3):
            fld_s[a, 0:SIDE] = jnp.zeros((SIDE, 8, WIDE), F32)
            fld_s[a, SPOTS + SIDE : SPOTS + 2 * SIDE] = jnp.zeros((SIDE, 8, WIDE), F32)

    @pl.when(h == 0)
    def _():
        for p, (w, b) in enumerate(((wq_ref, bq_ref), (wk_ref, bk_ref), (wv_ref, bv_ref))):
            y = nn(n_s[...], w[...]) + b[...]
            field_ref[:, :, p * WIDE : (p + 1) * WIDE] = y.reshape(SPOTS, 8, WIDE)

        def branch(p, _):
            def spread(r, _):
                spots = rows_at(r, SIDE)
                ok = alive(r, large, (BAND, LANES)).reshape(SIDE, 8, LANES)
                there = rows_at(r + 1, SIDE)
                for j in range(3):
                    lanes, own = tile_at(3 * p + j), slice(j * LANES, (j + 1) * LANES)
                    y = field_ref[spots, :, lanes] * ok
                    field_ref[spots, :, lanes] = y
                    fld_s[0, there, :, own] = frame_shift(y, True)
                    fld_s[1, there, :, own] = y
                    fld_s[2, there, :, own] = frame_shift(y, False)
                return 0

            lax.fori_loop(0, SIDE, spread, 0)

            def pool(j, _):
                lanes, own = tile_at(3 * p + j), tile_at(j)
                w = [jnp.broadcast_to(pw_ref[p, t : t + 1, own], (8, LANES)) for t in range(TAPS)]

                def row(r, _):
                    acc = [None] * SIDE
                    for c_in in range(SIDE):
                        for b in range(3):
                            for a in range(3):
                                x = fld_s[a, (r + b) * SIDE + c_in, :, own]
                                for e in range(3):
                                    c = c_in - e + 1
                                    if 0 <= c < SIDE:
                                        term = w[9 * a + 3 * b + e] * x
                                        acc[c] = term if acc[c] is None else acc[c] + term
                    for c in range(SIDE):
                        pool_s[r * SIDE + c, :, lanes] = acc[c]
                    return 0

                lax.fori_loop(0, SIDE, row, 0)
                return 0

            lax.fori_loop(0, 3, pool, 0)
            return 0

        lax.fori_loop(0, 3, branch, 0)
        lane = lane_of((BAND, LANES))

        def norm(r, _):
            spots, rows = rows_at(r, SIDE), rows_at(r, BAND)
            bar = jnp.where(lane == MASK_LANE, NEG, 0.0) * (1.0 - alive(r, large, (BAND, LANES)))
            for p in range(3):
                tiles = [
                    pool_s[spots, :, (3 * p + j) * LANES : (3 * p + j + 1) * LANES].reshape(BAND, LANES)
                    for j in range(3)
                ]
                for i, x in enumerate(to_heads(tiles)):
                    mean = jnp.sum(x, axis=-1, keepdims=True) * (1 / HEAD_DIM)
                    c = jnp.where(lane < HEAD_DIM, x - mean, 0.0)
                    var = jnp.sum(c * c, axis=-1, keepdims=True) * (1 / HEAD_DIM)
                    rstd = lax.rsqrt(var + EPS)
                    xh = c * rstd
                    xh_ref[i, p, rows, :] = jnp.where(lane == HEAD_DIM, rstd, xh)
                    y = xh * ln_ref[p : p + 1, :] + ln_ref[3 + p : 4 + p, :]
                    if p == 0:
                        q_s[i, rows, :] = y
                    elif p == 1:
                        k_ref[i, rows, :] = (y + marks_ref[rows, :] + bar).astype(BF16)
                    else:
                        one = (lane == HEAD_DIM) | (lane == HEAD_DIM + 1)
                        v_ref[i, rows, :] = jnp.where(one, 1.0, y).astype(BF16)
            return 0

        lax.fori_loop(0, SIDE, norm, 0)
        code = code_ref[...]
        out = 1.0 - jnp.where(code == 2.0, 1.0, code * large)
        lane_m = lane_of(code.shape)
        for a, ref in enumerate((k_ref, v_ref)):
            tiles = [mem_ref[a, :, j * LANES : (j + 1) * LANES].astype(F32) for j in range(3)]
            for i, m in enumerate(to_heads(tiles)):
                if a == 0:
                    m = jnp.where(lane_m == MASK_LANE, out * NEG, m)
                else:
                    m = jnp.where((lane_m == HEAD_DIM) | (lane_m == HEAD_DIM + 1), 1.0, m)
                ref[i, LENGTH:KEYS, :] = m.astype(BF16)

    def prepare(r, _):
        rows = rows_at(r, CHUNK)
        q = q_s[h, rows, :]
        near = (nt(q.astype(BF16), tall_ref[...]) * sel_ref[rows, :]).astype(BF16)
        lane = lane_of((CHUNK, LANES))
        ext = q * SCALE + nn(near, cmp_ref[...])
        q_ref[h, rows, :] = jnp.where(lane == MASK_LANE, 1.0, ext).astype(BF16)
        return 0

    lax.fori_loop(0, LENGTH // CHUNK, prepare, 0)

    def attend(r, _):
        rows = rows_at(r, CHUNK)
        lane = lane_of((CHUNK, LANES))
        s = nt(q_ref[h, rows, :], k_ref[h])
        e = jnp.exp(s - jnp.max(s, axis=-1, keepdims=True)).astype(BF16)
        p_ref[0, rows, :] = e
        o = nn(e, v_ref[h])
        total = o[:, HEAD_DIM : HEAD_DIM + 1]
        o = jnp.where(lane < HEAD_DIM, o * (1.0 / total), 0.0)
        o_ref[0, rows, :] = jnp.where(lane == HEAD_DIM, total, o)
        q_s[h, rows, :] += o
        return 0

    lax.fori_loop(0, LENGTH // CHUNK, attend, 0)

    @pl.when(h == PER - 1)
    def _():
        def join(r, _):
            rows = rows_at(r, BAND)
            for j, t in enumerate(to_dense([q_s[i, rows, :] for i in range(PER)])):
                att_ref[rows, j * LANES : (j + 1) * LANES] = t.astype(BF16)
            return 0

        lax.fori_loop(0, SIDE, join, 0)
        mid_ref[...] += nn(att_ref[...], wp_ref[...])


def mlp_kernel(
    parts, res_ref, mid_ref, cot_ref, gain_ref, bias_ref, bd_ref, up_all, down_all,
    out_ref, gm_ref, gml_ref, small_ref, gup_ref, gdown_ref, gfar_ref,
    n_s, nt_s, go_s, y_s, gn_s, wide_s, stage_s, up_s, bu_s, down_s, grad_s, land_s, side_s, load_sem, send_sem, recv_sem,
):
    step = pl.program_id(0)
    large = is_large(res_ref)
    tiles, width = D // LANES, up_s.shape[2]
    cut, half = tiles * D, tiles * D // 2
    core, other, near = ("tensor", 1), ("tensor", 2), ("dp", 1)

    def slice_of(k):
        k = k // parts
        return (bit_of(*core) + 1 - k % 2) % 2 + 2 * ((bit_of(*other) + 1 - k // 2) % 2)

    def loads(k):
        t, c = slice_of(k), k % parts
        lanes = pl.ds(pl.multiple_of(c * width, LANES), width)
        return [
            pltpu.make_async_copy(up_all.at[t, pl.ds(0, D), lanes], up_s.at[k], load_sem.at[0, k]),
            pltpu.make_async_copy(up_all.at[t, pl.ds(D, 16), lanes], bu_s.at[k], load_sem.at[1, k]),
            pltpu.make_async_copy(down_all.at[t, some(c * width, width)], down_s.at[k], load_sem.at[2, k]),
        ]

    def to_core(k):
        return send(grad_s.at[2 * k], land_s.at[k], send_sem.at[k], recv_sem.at[k], core)

    def to_side():
        return send(grad_s.at[1, pl.ds(0, cut)], side_s.at[pl.ds(0, cut)], send_sem.at[2], recv_sem.at[2], other)

    def to_near():
        give = cut + (1 - bit_of(*near)) * half
        return send(grad_s.at[1, some(give, half)], side_s.at[pl.ds(cut, half)], send_sem.at[3], recv_sem.at[3], near)

    @pl.when(step == 0)
    def _():
        for k in range(parts * 4):
            for copy in loads(k):
                copy.start()
        greet((core, other, near))

    @pl.when(step == 2 * parts)
    def _():
        to_core(0).wait()
        add_rows(grad_s.at[1], 0, land_s.at[0], 0, 2 * cut)
        to_side().start()
        to_near().start()

    for k in range(2):

        @pl.when(step == (2 * k + 1) * parts)
        def _():
            to_core(k).start()

    @pl.when(step == 0)
    def _():
        for j in range(D // LANES):
            stage_s[j] = cot_ref[:, j * LANES : (j + 1) * LANES].astype(F32)

        def body(i, sums):
            rows = rows_at(i, BAND)
            xh, _ = row_norm(mid_ref[rows, :])
            n_s[rows, :] = (xh * line(gain_ref) + line(bias_ref)).astype(BF16)
            go = get_spots(six(stage_s), i) * alive(i, large, (BAND, D))
            wide_s[rows, :] = go
            go_s[rows, :] = go.astype(BF16)
            return sums + fold8(go)

        sums = lax.fori_loop(0, SIDE, body, jnp.zeros((8, D), F32))
        put_rows(small_ref, 12, total(sums))
        nt_s[...] = n_s[...].T

    for copy in loads(step):
        copy.wait()
    pre = nn(n_s[...], up_s[step]) + bu_s[step].astype(F32)[0:1, :]
    cdf = 0.5 * (1.0 + lax.erf(pre * 0.7071067811865476))
    act = (pre * cdf).astype(BF16)
    slope = cdf + pre * jnp.exp(pre * pre * -0.5) * 0.3989422804014327
    ga = nt(go_s[...], down_s[step])
    gh = ga * slope
    own, part = step // parts, step % parts
    put_rows(small_ref, 24 + slice_of(step) * tiles + part * (width // LANES), total(fold8(gh)))
    ghl = gh.astype(BF16)
    value = tn(act, go_s[...]).astype(BF16)
    for j in range(tiles):
        grad_s[own, some(cut + j * D + part * width, width), :] = value[:, j * LANES : (j + 1) * LANES]
    value = nn(nt_s[...], ghl).astype(BF16)
    for j in range(width // LANES):
        grad_s[own, some((part * (width // LANES) + j) * D, D), :] = value[:, j * LANES : (j + 1) * LANES]
    y = nn(act, down_s[step])
    gn = nt(ghl, up_s[step])

    @pl.when(step == 0)
    def _():
        y_s[...] = y
        gn_s[...] = gn

    @pl.when(step > 0)
    def _():
        y_s[...] += y
        gn_s[...] += gn

    @pl.when(step == pl.num_programs(0) - 1)
    def _():
        def body(i, sums):
            rows = rows_at(i, BAND)
            mid = mid_ref[rows, :]
            put_spots(six(stage_s), i, (mid + y_s[rows, :] + line(bd_ref)) * alive(i, large, (BAND, D)))
            xh, rstd = row_norm(mid)
            gy = gn_s[rows, :]
            gx = gy * line(gain_ref)
            m1 = jnp.mean(gx, axis=-1, keepdims=True)
            m2 = jnp.mean(gx * xh, axis=-1, keepdims=True)
            gm = wide_s[rows, :] + (gx - m1 - xh * m2) * rstd
            gm_ref[rows, :] = gm
            gml_ref[rows, :] = gm.astype(BF16)
            return sums[0] + fold8(gy * xh), sums[1] + fold8(gy), sums[2] + fold8(gm)

        zero = jnp.zeros((8, D), F32)
        sums = lax.fori_loop(0, SIDE, body, (zero, zero, zero))
        for j in range(D // LANES):
            out_ref[:, j * LANES : (j + 1) * LANES] = stage_s[j].astype(BF16)
        for at, v in zip((0, 6, 18), sums):
            put_rows(small_ref, at, total(v))
        to_core(1).wait()
        add_rows(grad_s.at[3], 0, land_s.at[1], 0, 2 * cut)
        to_side().wait()
        add_rows(grad_s.at[3], 0, side_s, 0, cut)
        to_near().wait()
        keep = cut + bit_of(*near) * half
        add_rows(grad_s.at[1], keep, side_s, cut, half)
        gup_ref[...] = grad_s[3, 0:cut, :]
        gdown_ref[...] = grad_s[3, cut : 2 * cut, :]
        gfar_ref[...] = grad_s[1, some(keep, half), :]


def bwd_kernel(
    order, res_ref, x_ref, gain_ref, bias_ref, gm_any, gml_ref, wq_ref, wk_ref, wv_ref, pw_ref, ln_ref,
    tall_ref, cmp_ref, sel_ref, pick_ref, wp_ref, field_ref, xh_ref, q_ref, k_ref, v_ref, p_ref, o_ref, att_ref,
    gup_any, gdown_any, gfar_any,
    gx_ref, small_ref, gwq_ref, gwk_ref, gwv_ref, gwp_ref, gup_out, gdown_out,
    gpw_s, gtall_s, n_s, do_s, ds_s, dpp_s, g_s, gq_s, gin_s,
    up_s, down_s, far_s, up_land, down_land, far_land, load_sem, own_sem, send_sem, recv_sem,
):
    g, h = pl.program_id(0), pl.program_id(1)
    large = is_large(res_ref)
    up_steps = chain(up_s, up_land, gup_out, send_sem.at[0], recv_sem.at[0], own_sem.at[0], order)
    side = (far_s, far_land, ("tensor", 2))
    down_steps = chain(down_s, down_land, gdown_out, send_sem.at[1], recv_sem.at[1], own_sem.at[1], order, side)

    def travel(tick):
        at_ticks(tick, UP_TICKS, up_steps)
        at_ticks(tick, DOWN_TICKS, down_steps)

    @pl.when((g == 0) & (h == 0))
    def _():
        loads = [
            pltpu.make_async_copy(src, dst, load_sem.at[k])
            for k, (src, dst) in enumerate(((gup_any, up_s), (gdown_any, down_s), (gfar_any, far_s)))
        ]
        for copy in loads:
            copy.start()
        greet((("tensor", 2), *order))
        for copy in loads:
            copy.wait()

    travel((PER + 3) * g + h)

    @pl.when((g == 0) & (h == 0))
    def _():
        def body(i, _):
            rows = rows_at(i, BAND)
            xh, _ = row_norm(x_ref[rows, :].astype(F32))
            n_s[rows, :] = (xh * line(gain_ref) + line(bias_ref)).astype(BF16)
            return 0

        lax.fori_loop(0, SIDE, body, 0)
        for a in range(3):
            g_s[a, 0:SIDE] = jnp.zeros((SIDE, 8, WIDE), F32)
            g_s[a, SPOTS + SIDE : SPOTS + 2 * SIDE] = jnp.zeros((SIDE, 8, WIDE), F32)
        gtall_s[...] = jnp.zeros(gtall_s.shape, F32)
        small_ref[...] = jnp.zeros(small_ref.shape, F32)
        gpw_s[...] = jnp.zeros(gpw_s.shape, F32)

    @pl.when(h == 0)
    def _():
        gin_s[:, 0:WIDE] = nt(gml_ref[...], wp_ref[...])

        def split(r, _):
            rows = rows_at(r, BAND)
            tiles = [gin_s[rows, j * LANES : (j + 1) * LANES] for j in range(3)]
            for i, t in enumerate(to_heads(tiles)):
                do_s[i, rows, :] = t
            return 0

        lax.fori_loop(0, SIDE, split, 0)
        gw = tn(att_ref[...], gml_ref[...])
        for j in range(D // LANES):
            gwp_ref[j] = gw[:, j * LANES : (j + 1) * LANES].astype(BF16)

    lane = lane_of((LENGTH, LANES))
    do = do_s[h]
    o = o_ref[0]
    inv = 1.0 / o[:, HEAD_DIM : HEAD_DIM + 1]
    delta = jnp.sum(do * o, axis=-1, keepdims=True) * inv
    high = delta.astype(BF16).astype(F32)
    doe = jnp.where(lane == HEAD_DIM, -high, jnp.where(lane == HEAD_DIM + 1, high - delta, do * inv)).astype(BF16)
    gq_s[:, 0:LANES] = doe

    def scores(r, _):
        rows = rows_at(r, CHUNK)
        dp = nt(gq_s[rows, 0:LANES], v_ref[0])
        ds_s[rows, :] = (p_ref[0, rows, :].astype(F32) * dp).astype(BF16)
        return 0

    lax.fori_loop(0, LENGTH // CHUNK, scores, 0)
    dqe = nn(ds_s[...], k_ref[0])
    dk = tn(q_ref[0], ds_s[...]).T[:LENGTH]
    dv = tn(doe, p_ref[0]).T[:LENGTH]
    far = (nt(dqe.astype(BF16), cmp_ref[...]) * sel_ref[...]).astype(BF16)
    xq = xh_ref[0, 0]
    query = (jnp.where(lane < HEAD_DIM, xq, 0.0) * ln_ref[0:1, :] + ln_ref[3:4, :]).astype(BF16)
    gtall_s[...] += tn(far, query)
    dq = dqe * SCALE + do + nn(far, tall_ref[...])
    for p, gy in enumerate((dq, dk, dv)):
        raw = xh_ref[0, p]
        rstd = raw[:, HEAD_DIM : HEAD_DIM + 1]
        gx = gy * ln_ref[p : p + 1, :]
        m1 = jnp.sum(gx, axis=-1, keepdims=True) * (1 / HEAD_DIM)
        m2 = jnp.sum(gx * raw, axis=-1, keepdims=True) * (1 / HEAD_DIM)
        dpp_s[h, p] = (gx - m1 - raw * m2) * rstd
        small_ref[96 + p : 97 + p, :] += total(fold8(gy * raw))
        small_ref[99 + p : 100 + p, :] += total(fold8(gy))

    @pl.when(h == PER - 1)
    def _():
        def branch(p, _):
            def spread(r, _):
                there, rows = rows_at(r + 1, SIDE), rows_at(r, BAND)
                for j, t in enumerate(to_dense([dpp_s[i, p, rows, :] for i in range(PER)])):
                    lanes = slice(j * LANES, (j + 1) * LANES)
                    t = t.reshape(SIDE, 8, LANES)
                    g_s[0, there, :, lanes] = frame_shift(t, False)
                    g_s[1, there, :, lanes] = t
                    g_s[2, there, :, lanes] = frame_shift(t, True)
                return 0

            lax.fori_loop(0, SIDE, spread, 0)

            def pool(j, _):
                lanes, own = tile_at(3 * p + j), tile_at(j)
                for a in range(3):
                    w = [
                        jnp.broadcast_to(pw_ref[p, t : t + 1, own], (8, LANES))
                        for t in range(9 * a, 9 * a + 9)
                    ]

                    def row(r, sums):
                        sums = list(sums)
                        x = [field_ref[r * SIDE + c, :, lanes] for c in range(SIDE)]
                        acc = [None] * SIDE
                        for c_in in range(SIDE):
                            for b in range(3):
                                t = g_s[a, (r + 2 - b) * SIDE + c_in, :, own]
                                for e in range(3):
                                    c = c_in + e - 1
                                    if 0 <= c < SIDE:
                                        term = w[3 * b + e] * t
                                        acc[c] = term if acc[c] is None else acc[c] + term
                                        sums[3 * b + e] = sums[3 * b + e] + x[c] * t
                        for c in range(SIDE):
                            at = pl.ds(pl.multiple_of(r * BAND + c * 8, 8), 8)
                            if a == 0:
                                gin_s[at, lanes] = acc[c]
                            else:
                                gin_s[at, lanes] += acc[c]
                        return tuple(sums)

                    sums = lax.fori_loop(0, SIDE, row, tuple(jnp.zeros((8, LANES), F32) for _ in range(9)))
                    for t in range(9):
                        gpw_s[9 * a + t : 9 * a + t + 1, own] = total(sums[t])
                return 0

            lax.fori_loop(0, 3, pool, 0)
            travel((PER + 3) * g + PER + p)
            heads = to_heads([gpw_s[:, j * LANES : (j + 1) * LANES] for j in range(3)])
            small_ref[rows_at(p, 32), :] += heads[0] + heads[1] + heads[2] + heads[3]
            return 0

        lax.fori_loop(0, 3, branch, 0)

        def finish(r, sums):
            rows = rows_at(r, BAND)
            t = gin_s[rows, :] * alive(r, large, (BAND, 3 * WIDE))
            gq_s[rows, :] = t.astype(BF16)
            return sums + fold8(t)

        put_rows(small_ref, 168 + 9 * g, total(lax.fori_loop(0, SIDE, finish, jnp.zeros((8, 3 * WIDE), F32))))
        gm_load = pltpu.make_async_copy(gm_any, gin_s.at[:, pl.ds(0, D)], load_sem.at[3])

        @pl.when(g == GROUPS - 1)
        def _():
            gm_load.start()

        gn = None
        for p, (w, gw) in enumerate(((wq_ref, gwq_ref), (wk_ref, gwk_ref), (wv_ref, gwv_ref))):
            piece = gq_s[:, p * WIDE : (p + 1) * WIDE]
            value = tn(n_s[...], piece)
            for j in range(WIDE // LANES):
                gw[j] = value[:, j * LANES : (j + 1) * LANES].astype(BF16)
            term = nt(piece, w[...])
            gn = term if gn is None else gn + term

        @pl.when(g == 0)
        def _():
            gx_ref[...] = gn

        @pl.when(g > 0)
        def _():
            gx_ref[...] += gn

    @pl.when((h == PER - 1) & (g == GROUPS - 1))
    def _():
        pltpu.make_async_copy(gm_any, gin_s.at[:, pl.ds(0, D)], load_sem.at[3]).wait()
        stage = [(dpp_s, (j // 3, j % 3)) for j in range(D // LANES)]

        def body(i, sums):
            rows = rows_at(i, BAND)
            xh, rstd = row_norm(x_ref[rows, :].astype(F32))
            gy = gx_ref[rows, :]
            gx = gy * line(gain_ref)
            m1 = jnp.mean(gx, axis=-1, keepdims=True)
            m2 = jnp.mean(gx * xh, axis=-1, keepdims=True)
            put_spots(stage, i, gin_s[rows, 0:D] + (gx - m1 - xh * m2) * rstd)
            return sums[0] + fold8(gy * xh), sums[1] + fold8(gy)

        zero = jnp.zeros((8, D), F32)
        sums = lax.fori_loop(0, SIDE, body, (zero, zero))
        for j, (ref, at) in enumerate(stage):
            gx_ref[:, j * LANES : (j + 1) * LANES] = ref[at]
        put_rows(small_ref, 186, total(sums[0]))
        put_rows(small_ref, 192, total(sums[1]))
        rest, rel = gtall_s[...], None
        for _ in range(3):
            part = rest.astype(BF16)
            rest = rest - part.astype(F32)
            term = nn(pick_ref[...], part)
            rel = term if rel is None else rel + term
        small_ref[104:168, :] = rel
        travel(2 * (PER + 3))


def reduce_kernel(parts, pieces, links, *refs):
    n = len(pieces)
    ins, one, two, out, small = refs[:n], refs[n], refs[n + 1], refs[n + 2], refs[n + 3]
    big, land, small_land, load_sem, send_sem, recv_sem, back_sem, home_sem, ssend_sem, srecv_sem = refs[n + 4 :]
    loads = [
        pltpu.make_async_copy(ref, big.at[pl.ds(first, rows)], load_sem.at[i])
        for i, (ref, (first, rows)) in enumerate(zip(ins, pieces))
    ]
    for copy in loads:
        copy.start()
    greet(links)
    small[0 : one.shape[0]] = one[...]
    small[one.shape[0] :] = two[...]
    for copy in loads:
        copy.wait()

    spans = [[(first, rows)] for first, rows, _ in parts]
    for s in range(max(len(order) for _, _, order in parts)):
        flying = []
        for i, (first, rows, order) in enumerate(parts):
            if s >= len(order):
                continue
            off, size = spans[i][-1]
            half = size // 2
            bit = bit_of(*order[s])
            keep, give, at = off + bit * half, off + (1 - bit) * half, first + rows - size
            if halvings(rows) <= s:
                keep, give, half = off, off, size
            copy = send(
                big.at[pl.ds(pl.multiple_of(give, 16), half)], land.at[pl.ds(at, half)], send_sem.at[i, s], recv_sem.at[i, s], order[s]
            )
            copy.start()
            flying.append((copy, keep, half, at))
            spans[i].append((keep, half))
        extra = None
        if s < len(links):
            extra = send(small, small_land.at[s], ssend_sem.at[s], srecv_sem.at[s], links[s])
            extra.start()
        for copy, keep, half, at in flying:
            copy.wait()
            add_rows(big, keep, land, at, half)
        if extra is not None:
            extra.wait()
            small[...] += small_land[s]
    for span in spans:
        off, size = span[-1]
        own = pl.ds(pl.multiple_of(off, 16), size)
        out[own, :] = big[own, :]
    depth = max(len(order) for _, _, order in parts)
    for s in reversed(range(depth)):
        flying = []
        for i, (first, rows, order) in enumerate(parts):
            if s >= min(len(order), halvings(rows)):
                continue
            off, size = spans[i][s + 1]
            here = out.at[pl.ds(pl.multiple_of(off, 16), size)]
            copy = send(here, here, back_sem.at[i, s], home_sem.at[i, s], order[s])
            copy.start()
            flying.append(copy)
        for copy in flying:
            copy.wait()


def all_reduce(whole, over_dp, one, two, sizes):
    dp, tensor = bits("dp", sizes["dp"]), bits("tensor", sizes["tensor"])
    links = tensor + dp
    small = sds((one.shape[0] + two.shape[0], LANES), F32)
    pieces, at = [], 0
    for a in whole + over_dp:
        pieces.append((at, a.shape[0]))
        at += a.shape[0]
    cut = sum(a.shape[0] for a in whole)
    core, rest = tensor[:1], tensor[1:]
    third = cut // 3
    orders = (core + rest + dp, core + dp[:1] + dp[1:] + rest, core + dp[1:] + rest + dp[:1])
    parts = [(k * third, third, order) for k, order in enumerate(orders)]
    if over_dp:
        half = (at - cut) // 2
        parts += [(cut, half, dp), (cut + half, half, dp[1:] + dp[:1])]
    assert all(len(order) <= halvings(rows) + 1 for _, rows, order in parts)
    depth = max(len(order) for _, _, order in parts)
    dma = pltpu.SemaphoreType.DMA
    return pl.pallas_call(
        functools.partial(reduce_kernel, parts, pieces, links),
        in_specs=[pl.BlockSpec(memory_space=pl.ANY)] * len(pieces) + [pl.BlockSpec(memory_space=pltpu.VMEM)] * 2,
        out_specs=[pl.BlockSpec(memory_space=pltpu.VMEM)] * 2,
        out_shape=[sds((at, LANES), BF16), sds(small.shape, F32)],
        scratch_shapes=[
            pltpu.VMEM((at, LANES), BF16),
            pltpu.VMEM((at, LANES), BF16),
            pltpu.VMEM((len(links), *small.shape), F32),
            dma((len(pieces),)),
            dma((len(parts), depth)), dma((len(parts), depth)), dma((len(parts), depth)), dma((len(parts), depth)),
            dma((len(links),)), dma((len(links),)),
        ],
        compiler_params=pltpu.CompilerParams(
            vmem_limit_bytes=VMEM_LIMIT, collective_id=1, has_side_effects=True
        ),
        name="sum_all",
        cost_estimate=pl.CostEstimate(flops=10_000_000, bytes_accessed=20_000_000, transcendentals=0),
    )(*whole, *over_dp, one, two)


def unpack_kernel(big_ref, up_ref, down_ref, small_ref, *outs):
    squares, vectors, gb_ref, gpw_ref, gain_ref, bias_ref, rel_ref = outs[:4], outs[4:11], *outs[11:]
    for out, ref, first, n in zip(squares, (big_ref, big_ref, up_ref, down_ref), (0, 18, 0, 0), (18, 6, 6, 6)):
        for j in range(n):
            out[:, j * LANES : (j + 1) * LANES] = ref[first + j].astype(F32)

    @pl.when(pl.program_id(0) == 0)
    def _():
        own = 232 + 6 * lax.axis_index("tensor")
        for ref, at in zip(vectors, (186, 192, 226, 208, 214, 220, own)):
            for j in range(6):
                ref[j * LANES : (j + 1) * LANES] = small_ref[at + j, :]
        for g in range(GROUPS):
            for j in range(9):
                to = (j // 3) * D + g * WIDE + j % 3 * LANES
                gb_ref[to : to + LANES] = small_ref[168 + 9 * g + j, :]
        for p in range(3):
            gpw_ref[p] = small_ref[32 * p : 32 * p + TAPS, :HEAD_DIM]
        gain_ref[...] = small_ref[96:99, :HEAD_DIM]
        bias_ref[...] = small_ref[99:102, :HEAD_DIM]
        rel_ref[...] = small_ref[104 : 104 + REL_ROWS, :HEAD_DIM]


def unpack(big, up, down, small):
    def whole(*shape):
        return pl.BlockSpec(shape, lambda i: (0,) * len(shape))

    def band(width):
        return pl.BlockSpec((LANES, width), lambda i: (i, 0))

    shapes = [(D,)] * 7 + [(3 * D,), (3, TAPS, HEAD_DIM), (3, HEAD_DIM), (3, HEAD_DIM), (REL_ROWS, HEAD_DIM)]
    return pl.pallas_call(
        unpack_kernel,
        grid=(D // LANES,),
        in_specs=[
            *[pl.BlockSpec((n, LANES, LANES), lambda i: (0, i, 0)) for n in (24, 6, 6)], whole(*small.shape),
        ],
        out_specs=[band(3 * D), band(D), band(D), band(D), *[whole(*shape) for shape in shapes]],
        out_shape=[sds((D, 3 * D), F32), *[sds((D, D), F32)] * 3, *[sds(shape, F32) for shape in shapes]],
        name="unpack",
        cost_estimate=pl.CostEstimate(flops=0, bytes_accessed=22_000_000, transcendentals=0),
    )(big, up, down, small)


def position_tables():
    spot = np.arange(LENGTH) // FRAMES
    frame, row, column = np.arange(LENGTH) % FRAMES, spot // SIDE, spot % SIDE
    kinds = ((frame, FRAMES, 0), (row, SIDE, FRAMES), (column, SIDE, FRAMES + SIDE))
    bases = (FRAMES - 1, 2 * FRAMES - 1 + SIDE - 1, 2 * FRAMES - 1 + 2 * SIDE - 1 + SIDE - 1)
    pick = np.zeros((PAIRS, REL_ROWS), np.float32)
    squeeze = np.zeros((PAIRS, LANES), np.float32)
    select = np.zeros((LENGTH, PAIRS), np.float32)
    marks = np.zeros((LENGTH, LANES), np.float32)
    for tile, ((where, size, first), base) in enumerate(zip(kinds, bases)):
        for at in range(size):
            for m in range(size):
                col = tile * LANES + at * size + m
                pick[col, base + at - m] = 1.0
                squeeze[col, HEAD_DIM + first + m] = 1.0
                select[:, col] = where == at
        marks[np.arange(LENGTH), HEAD_DIM + first + where] = 1.0
    memory_at = np.arange(KEYS - LENGTH) % (MEM // 2)
    half, small = (SIDE + 1) // 2, (SMALL_SIDE + 1) // 2
    memory_inside = (memory_at // half % half < small) & (memory_at % half < small)
    exists = np.arange(KEYS - LENGTH) < MEM
    code = np.where(exists, 1.0 + memory_inside, 0.0).astype(np.float32)
    return pick, squeeze, select, marks, np.repeat(code[:, None], LANES, 1)


def blocked(shape, index, single=False):
    if single:
        return pl.BlockSpec(shape, index, pipeline_mode=pl.Buffered(1))
    return pl.BlockSpec(shape, index)


def const(shape):
    return blocked(shape, lambda *_: (0,) * len(shape), True)


def sds(shape, dtype):
    return jax.ShapeDtypeStruct(shape, dtype)


def per_device(
    inputs, res_ids, memory, gain_one, bias_one, w_qkv, b_qkv, pool_weight, pool_gain, pool_bias, rel_table,
    w_proj, b_proj, gain_two, bias_two, w_up, b_up, w_down, b_down, cotangent,
):
    split = lax.axis_size("tensor")
    pick, squeeze, select, marks, code = position_tables()
    up_all = lax.all_gather(jnp.concatenate([w_up, jnp.broadcast_to(b_up, (16, b_up.shape[0]))]), "tensor")
    down_all = lax.all_gather(w_down, "tensor")
    pw = jnp.pad(jnp.tile(pool_weight, (1, 1, PER)), ((0, 0), (0, 5), (0, 0)))
    ln = jnp.pad(jnp.concatenate([pool_gain, pool_bias]), ((0, 2), (0, LANES - HEAD_DIM)))
    tall = jnp.dot(pick, rel_table, precision=lax.Precision.HIGHEST)
    tall = jnp.pad(tall, ((0, 0), (0, LANES - HEAD_DIM))).astype(BF16)
    cmp = jnp.asarray(squeeze, BF16)
    mem = jnp.pad(memory, ((0, 0), (0, KEYS - LENGTH - MEM), (0, 0)))
    bq = b_qkv.reshape(1, -1)

    params = pltpu.CompilerParams(vmem_limit_bytes=VMEM_LIMIT)
    w_spec = [blocked((D, WIDE), lambda g, h, p=p: (0, GROUPS * p + g)) for p in range(3)]
    b_spec = [blocked((1, WIDE), lambda g, h, p=p: (0, GROUPS * p + g)) for p in range(3)]

    scalar = pl.BlockSpec(memory_space=pltpu.SMEM)
    row = const((D,))

    def per_group(*shape):
        return blocked(shape, lambda g, h: (g,) + (0,) * (len(shape) - 1))

    def per_head(*shape):
        return blocked(shape, lambda g, h: (PER * g + h,) + (0,) * (len(shape) - 1))

    field_spec = blocked((SPOTS, 8, 3 * WIDE), lambda g, h: (0, 0, g))
    att_spec = blocked((LENGTH, WIDE), lambda g, h: (0, g))
    mid, xs, field, xh, qx, kx, vx, probs, outs, att = pl.pallas_call(
        fwd_kernel,
        grid=(GROUPS, PER),
        in_specs=[
            scalar, const((LENGTH, D)), row, row, row, *w_spec, *b_spec,
            const((3, 32, WIDE)), const((8, LANES)), const((PAIRS, LANES)), const((PAIRS, LANES)),
            const((LENGTH, PAIRS)), const((LENGTH, LANES)), const((KEYS - LENGTH, LANES)),
            blocked((2, KEYS - LENGTH, WIDE), lambda g, h: (0, 0, g)),
            blocked((WIDE, D), lambda g, h: (g, 0)),
        ],
        out_specs=[
            const((LENGTH, D)), const((LENGTH, D)), field_spec, per_group(PER, 3, LENGTH, LANES), per_group(PER, LENGTH, LANES),
            per_group(PER, KEYS, LANES), per_group(PER, KEYS, LANES), per_head(1, LENGTH, KEYS),
            per_head(1, LENGTH, LANES), att_spec,
        ],
        out_shape=[
            sds((LENGTH, D), F32), sds((LENGTH, D), BF16), sds((SPOTS, 8, 3 * D), F32), sds((HEADS, 3, LENGTH, LANES), F32),
            sds((HEADS, LENGTH, LANES), BF16), sds((HEADS, KEYS, LANES), BF16), sds((HEADS, KEYS, LANES), BF16),
            sds((HEADS, LENGTH, KEYS), BF16), sds((HEADS, LENGTH, LANES), F32), sds((LENGTH, D), BF16),
        ],
        scratch_shapes=[
            pltpu.VMEM((LENGTH, D), BF16),
            pltpu.VMEM((3, SPOTS + 2 * SIDE, 8, WIDE), F32),
            pltpu.VMEM((SPOTS, 8, 3 * WIDE), F32),
            pltpu.VMEM((PER, LENGTH, LANES), F32),
            pltpu.VMEM((D // LANES, LENGTH, LANES), F32),
        ],
        compiler_params=params,
        name="attend",
        cost_estimate=pl.CostEstimate(flops=2 * 3_500_000_000, bytes_accessed=60_000_000, transcendentals=6_500_000),
    )(
        res_ids, inputs, gain_one, bias_one, b_proj, w_qkv, w_qkv, w_qkv, bq, bq, bq, pw, ln,
        tall, cmp, jnp.asarray(select), jnp.asarray(marks), jnp.asarray(code), mem, w_proj,
    )

    hidden = w_up.shape[1]
    piece = 384
    parts = hidden // piece
    tiles = hidden // LANES
    chunks, cut = split * parts, D // LANES * D
    dma = pltpu.SemaphoreType.DMA
    anywhere = pl.BlockSpec(memory_space=pl.ANY)
    out, gm, gml, small, gup, gdown, gfar = pl.pallas_call(
        functools.partial(mlp_kernel, parts),
        grid=(chunks,),
        in_specs=[scalar, const((LENGTH, D)), const((LENGTH, D)), row, row, row, anywhere, anywhere],
        out_specs=[
            const((LENGTH, D)), const((LENGTH, D)), const((LENGTH, D)), const((24 + split * tiles, LANES)),
            const((cut, LANES)), const((cut, LANES)), const((cut // 2, LANES)),
        ],
        out_shape=[
            sds((LENGTH, D), BF16), sds((LENGTH, D), F32), sds((LENGTH, D), BF16), sds((24 + split * tiles, LANES), F32),
            sds((cut, LANES), BF16), sds((cut, LANES), BF16), sds((cut // 2, LANES), BF16),
        ],
        scratch_shapes=[
            pltpu.VMEM((LENGTH, D), BF16),
            pltpu.VMEM((D, LENGTH), BF16),
            pltpu.VMEM((LENGTH, D), BF16),
            *[pltpu.VMEM((LENGTH, D), F32)] * 3,
            pltpu.VMEM((D // LANES, LENGTH, LANES), F32),
            pltpu.VMEM((chunks, D, piece), BF16),
            pltpu.VMEM((chunks, 16, piece), BF16),
            pltpu.VMEM((chunks, piece, D), BF16),
            pltpu.VMEM((split, 2 * cut, LANES), BF16),
            pltpu.VMEM((2, 2 * cut, LANES), BF16),
            pltpu.VMEM((cut + cut // 2, LANES), BF16),
            dma((3, chunks)), dma((4,)), dma((4,)),
        ],
        compiler_params=pltpu.CompilerParams(vmem_limit_bytes=VMEM_LIMIT, collective_id=2, has_side_effects=True),
        name="mlp",
        cost_estimate=pl.CostEstimate(flops=2 * 11_300_000_000, bytes_accessed=40_000_000, transcendentals=5_000_000),
    )(res_ids, mid, cotangent, gain_two, bias_two, b_down, up_all, down_all)

    links = bits("dp", lax.axis_size("dp"))
    gx, small_one, gwq, gwk, gwv, gwp, gup, gdown = pl.pallas_call(
        functools.partial(bwd_kernel, links),
        grid=(GROUPS, PER),
        in_specs=[
            scalar, const((LENGTH, D)), row, row, anywhere, const((LENGTH, D)), *w_spec,
            const((3, 32, WIDE)), const((8, LANES)), const((PAIRS, LANES)), const((PAIRS, LANES)),
            const((LENGTH, PAIRS)), const((64, PAIRS)), blocked((WIDE, D), lambda g, h: (g, 0)),
            blocked((SPOTS, 8, 3 * WIDE), lambda g, h: (0, 0, g), True),
            per_head(1, 3, LENGTH, LANES), per_head(1, LENGTH, LANES), per_head(1, KEYS, LANES),
            per_head(1, KEYS, LANES), per_head(1, LENGTH, KEYS), per_head(1, LENGTH, LANES), att_spec,
            anywhere, anywhere, anywhere,
        ],
        out_specs=[
            const((LENGTH, D)), const((208, LANES)),
            *[blocked((3, D, LANES), lambda g, h: (g, 0, 0)) for _ in range(3)],
            blocked((6, WIDE, LANES), lambda g, h: (0, g, 0)), anywhere, anywhere,
        ],
        out_shape=[
            sds((LENGTH, D), F32), sds((208, LANES), F32), *[sds((6, D, LANES), BF16)] * 4,
            sds((cut, LANES), BF16), sds((cut, LANES), BF16),
        ],
        scratch_shapes=[
            pltpu.VMEM((32, WIDE), F32),
            pltpu.VMEM((PAIRS, LANES), F32),
            pltpu.VMEM((LENGTH, D), BF16),
            pltpu.VMEM((PER, LENGTH, LANES), F32),
            pltpu.VMEM((LENGTH, KEYS), BF16),
            pltpu.VMEM((PER, 3, LENGTH, LANES), F32),
            pltpu.VMEM((3, SPOTS + 2 * SIDE, 8, WIDE), F32),
            pltpu.VMEM((LENGTH, 3 * WIDE), BF16),
            pltpu.VMEM((LENGTH, 3 * WIDE), F32),
            pltpu.VMEM((cut, LANES), BF16), pltpu.VMEM((cut, LANES), BF16), pltpu.VMEM((cut // 2, LANES), BF16),
            pltpu.VMEM((cut, LANES), BF16), pltpu.VMEM((cut, LANES), BF16), pltpu.VMEM((cut // 2, LANES), BF16),
            dma((4,)), dma((2,)), dma((2, 2 * len(links) + 1)), dma((2, 2 * len(links) + 1)),
        ],
        compiler_params=pltpu.CompilerParams(vmem_limit_bytes=VMEM_LIMIT, collective_id=3, has_side_effects=True),
        name="attend_back",
        cost_estimate=pl.CostEstimate(flops=2 * 7_000_000_000, bytes_accessed=60_000_000, transcendentals=0),
    )(
        res_ids, xs, gain_one, bias_one, gm, gml, w_qkv, w_qkv, w_qkv, pw, ln, tall, cmp, jnp.asarray(select), jnp.asarray(np.pad(pick.T, ((0, 11), (0, 0))), BF16), w_proj,
        field, xh, qx, kx, vx, probs, outs, att, gup, gdown, gfar,
    )

    flat = [a.reshape(-1, LANES) for a in (gwq, gwk, gwv, gwp)]
    sizes = {axis: lax.axis_size(axis) for axis in ("dp", "tensor")}
    big, small = all_reduce(flat, [], small_one, small, sizes)
    outs = unpack(*[a.reshape(-1, D, LANES) for a in (big, gup, gdown)], small)
    squares, (gain1, bias1, bp, gain2, bias2, bd, bu), (gb, gpw, pg, pb, rel) = outs[:4], outs[4:11], outs[11:]

    return (
        out, gx, gain1, bias1, squares[0], gb, gpw, pg, pb, rel, squares[1], bp, gain2, bias2, squares[2], bu, squares[3], bd,
    )


def solution(mesh):
    rows = P(("dp", "tensor"), None)
    return jax.shard_map(
        per_device,
        mesh=mesh,
        in_specs=(
            rows, P(("dp", "tensor")), P(None, ("dp", "tensor"), None), *[P()] * 12,
            P(None, "tensor"), P("tensor"), P("tensor", None), P(), rows,
        ),
        out_specs=(rows, rows, *[P()] * 12, P(None, "tensor"), P("tensor"), P("tensor", None), P()),
        check_vma=False,
    )
```

```python
import functools

import jax
import jax.numpy as jnp
import numpy as np
from jax import lax
from jax.experimental import pallas as pl
from jax.experimental.pallas import tpu as pltpu
from jax.sharding import PartitionSpec as P

D = 768
HEADS = 8
HEAD_DIM = 96
FRAMES = 8
SIDE = 10
SMALL_SIDE = 7
SPOTS = SIDE * SIDE
LENGTH = FRAMES * SPOTS
MEM = 200
KEYS = 1024
OFFSETS = FRAMES + 2 * SIDE
REL_ROWS = 53
GROUPS = 2
PER = HEADS // GROUPS
WIDE = PER * HEAD_DIM
TAPS = 27
LANES = 128
BAND = SIDE * FRAMES
PAIRS = 384
MASK_LANE = HEAD_DIM + OFFSETS
EPS = 1e-6
SCALE = HEAD_DIM**-0.5
F32 = jnp.float32
BF16 = jnp.bfloat16
NEG = -1e30
UP_TICKS = (0, 3, 4, 5, 6, 8, 11)
DOWN_TICKS = (3, 5, 7, 9, 10, 11, 12, 14)
VMEM_LIMIT = 60 * 1024 * 1024


def nn(a, b):
    return jnp.dot(a, b, preferred_element_type=F32)


def nt(a, b):
    return lax.dot_general(a, b, (((1,), (1,)), ((), ())), preferred_element_type=F32)


def tn(a, b):
    return lax.dot_general(a, b, (((0,), (0,)), ((), ())), preferred_element_type=F32)


def lane_of(shape):
    return lax.broadcasted_iota(jnp.int32, shape, len(shape) - 1)


def to_heads(tiles):
    t0, t1, t2 = tiles
    lane = lane_of(t0.shape)
    own = lane < HEAD_DIM
    h1 = pltpu.roll(jnp.where(lane >= 96, t0, t1), 32, t0.ndim - 1)
    h2 = pltpu.roll(jnp.where(lane >= 64, t1, t2), 64, t0.ndim - 1)
    h3 = pltpu.roll(t2, 96, t0.ndim - 1)
    return [jnp.where(own, h, 0.0) for h in (t0, h1, h2, h3)]


def to_dense(heads):
    p0, p1, p2, p3 = heads
    lane = lane_of(p0.shape)
    r1 = pltpu.roll(p1, 96, p0.ndim - 1)
    r2 = pltpu.roll(p2, 64, p0.ndim - 1)
    r3 = pltpu.roll(p3, 32, p0.ndim - 1)
    return [jnp.where(lane < 96, p0, r1), jnp.where(lane < 64, r1, r2), jnp.where(lane < 32, r2, r3)]


def row_norm(x):
    mean = jnp.mean(x, axis=-1, keepdims=True)
    c = x - mean
    rstd = lax.rsqrt(jnp.mean(c * c, axis=-1, keepdims=True) + EPS)
    return c * rstd, rstd


def ones_matrix():
    return jnp.where(lax.broadcasted_iota(jnp.int32, (LANES, LANES), 0) < HEAD_DIM, 1.0, 0.0).astype(BF16)


def lane_mean(x, ones):
    return nn(x.astype(BF16), ones) * (1 / HEAD_DIM)


def fine_mean(x, ones):
    high = x.astype(BF16)
    low = (x - high.astype(F32)).astype(BF16)
    return nn(jnp.concatenate([high, low], axis=1), jnp.concatenate([ones, ones])) * (1 / HEAD_DIM)


def frame_shift(x, up):
    frame = lax.broadcasted_iota(jnp.int32, x.shape, 1)
    if up:
        return jnp.where(frame == 0, 0.0, pltpu.roll(x, 1, 1))
    return jnp.where(frame == FRAMES - 1, 0.0, pltpu.roll(x, FRAMES - 1, 1))


def fold8(x):
    return jnp.sum(x.reshape(x.shape[0] // 8, 8, x.shape[1]), axis=0)


def put_rows(ref, at, v):
    for j in range(v.shape[1] // LANES):
        ref[pl.ds(at + j, 1), :] = v[:, j * LANES : (j + 1) * LANES]


def total(x):
    return jnp.sum(x, axis=0, keepdims=True)


def alive(r, large, shape):
    inside = jnp.where(r < SMALL_SIDE, SMALL_SIDE * FRAMES, 0)
    return jnp.where(lax.broadcasted_iota(jnp.int32, shape, 0) < inside, 1.0, large)


def is_large(res_ref):
    return jnp.where(res_ref[0] == 1, 1.0, 0.0).astype(F32)


def put_spots(tiles, r, x):
    for c in range(SIDE):
        for j, (ref, at) in enumerate(tiles):
            to = pl.ds(r * SIDE + c, FRAMES, stride=SPOTS)
            ref[(*at, to, slice(None))] = x[c * FRAMES : (c + 1) * FRAMES, j * LANES : (j + 1) * LANES]


def get_spots(tiles, r):
    rows = [
        jnp.concatenate([ref[(*at, pl.ds(r * SIDE + c, FRAMES, stride=SPOTS), slice(None))] for ref, at in tiles], axis=1)
        for c in range(SIDE)
    ]
    return jnp.concatenate(rows)


def six(ref):
    return [(ref, (j,)) for j in range(D // LANES)]


def line(ref):
    return ref[...].reshape(1, ref.shape[0])


def tile_at(j):
    return pl.ds(pl.multiple_of(j * LANES, LANES), LANES)


def rows_at(r, size):
    if isinstance(r, int):
        return pl.ds(r * size, size)
    return pl.ds(pl.multiple_of(r * size, size), size)


def bit_of(axis, bit):
    return lax.axis_index(axis) // bit % 2


def partner_of(axis, bit):
    me = lax.axis_index(axis)
    return {axis: me + (1 - 2 * (me // bit % 2)) * bit}


def halvings(rows):
    count = 0
    while rows % (32 << count) == 0:
        count += 1
    return count


def bits(axis, size):
    return [(axis, 1 << k) for k in range(size.bit_length() - 1)]


def send(src, dst, one, two, link):
    return pltpu.make_async_remote_copy(
        src_ref=src, dst_ref=dst, send_sem=one, recv_sem=two,
        device_id=partner_of(*link), device_id_type=pl.DeviceIdType.MESH,
    )


def greet(links):
    barrier = pltpu.get_barrier_semaphore()
    for link in links:
        pl.semaphore_signal(barrier, inc=1, device_id=partner_of(*link), device_id_type=pl.DeviceIdType.MESH)
    pl.semaphore_wait(barrier, len(links))


def some(start, rows):
    return pl.ds(pl.multiple_of(start, 16), rows)


def add_rows(dst, at, src, start, rows):
    block = next(b for b in (512, 256, 128, 64, 48, 32, 16) if rows % b == 0)

    def add(k, _):
        a, b = some(at + k * block, block), some(start + k * block, block)
        dst[a, :] = (dst[a, :].astype(F32) + src[b, :].astype(F32)).astype(BF16)
        return 0

    lax.fori_loop(0, rows // block, add, 0)


def chain(work, land, out, send_sem, recv_sem, own_sem, order, merge=None):
    rows, count = work.shape[0], halvings(work.shape[0])

    def span(s):
        off, size = 0, rows
        for k in range(min(s, count)):
            size //= 2
            off = off + bit_of(*order[k]) * size
        return off, size

    def halve(s, k):
        off, size = span(s)
        half, bit, at = size // 2, bit_of(*order[s]), rows - size
        keep, give = off + bit * half, off + (1 - bit) * half
        if s >= count:
            keep, give, half = off, off, size
        copy = send(work.at[some(give, half)], land.at[some(at, half)], send_sem.at[k], recv_sem.at[k], order[s])
        return copy, (work, keep, land, at, half)

    def join(k):
        ref, landing, link = merge
        return send(ref, landing, send_sem.at[k], recv_sem.at[k], link), (work, span(1)[0], landing, 0, ref.shape[0])

    def double(s, k):
        off, size = span(s + 1)
        here = out.at[some(off, size)]
        return send(here, here, send_sem.at[k], recv_sem.at[k], order[s]), None

    def own():
        off, size = span(len(order))
        copy = pltpu.make_async_copy(work.at[some(off, size)], out.at[some(off, size)], own_sem)
        copy.start()
        copy.wait()

    plans = [functools.partial(halve, s) for s in range(len(order))]
    if merge is not None:
        plans.insert(1, join)
    gather = len(plans)
    plans += [functools.partial(double, s) for s in reversed(range(min(len(order), count)))]

    def start(k):
        if k == gather:
            own()
        plans[k](k)[0].start()

    def finish(k):
        copy, todo = plans[k](k)
        copy.wait()
        if todo is not None:
            add_rows(*todo)

    def step(k):
        if k > 0:
            finish(k - 1)
        if k < len(plans):
            start(k)

    return [functools.partial(step, k) for k in range(len(plans) + 1)]


def at_ticks(tick, table, steps):
    for n in sorted(set(table)):
        due = [k for k in range(len(steps)) if table[min(k, len(table) - 1)] == n]

        @pl.when(tick == n)
        def _():
            for k in due:
                steps[k]()


def fwd_kernel(
    res_ref, x_ref, gain_ref, bias_ref, bp_ref, wq_ref, wk_ref, wv_ref, bq_ref, bk_ref, bv_ref, pw_ref, ln_ref,
    tall_ref, cmp_ref, sel_ref, marks_ref, code_ref, mem_ref, wp_ref, up_any, bu_any, down_any,
    mid_ref, xs_ref, field_ref, xh_ref, q_ref, k_ref, v_ref, p_ref, o_ref, att_ref, up_all, bu_all, down_all,
    send_sem, recv_sem, n_s, fld_s, pool_s, q_s, acc_s,
):
    g, h = pl.program_id(0), pl.program_id(1)
    large = is_large(res_ref)
    core, other = ("tensor", 1), ("tensor", 2)
    shards = ((up_any, up_all), (bu_any, bu_all), (down_any, down_all))

    def share(k, link, to):
        src = shards[k][0] if to < 2 else shards[k][1].at[1]
        return send(src, shards[k][1].at[to], send_sem.at[k, to], recv_sem.at[k, to], link)

    @pl.when((g == 0) & (h == 0))
    def _():
        greet((core, other))
        for k in range(3):
            share(k, other, 1).start()
            share(k, core, 0).start()

    @pl.when((h == PER - 1) & (g == GROUPS - 1))
    def _():
        for k in range(3):
            share(k, other, 1).wait()
            share(k, core, 2).start()


    @pl.when((g == 0) & (h == 0))
    def _():
        for j in range(D // LANES):
            acc_s[j] = x_ref[:, j * LANES : (j + 1) * LANES].astype(F32)

        def body(i, _):
            rows = rows_at(i, BAND)
            x = get_spots(six(acc_s), i)
            mid_ref[rows, :] = x + line(bp_ref)
            xs_ref[rows, :] = x.astype(BF16)
            xh, _ = row_norm(x)
            n_s[rows, :] = (xh * line(gain_ref) + line(bias_ref)).astype(BF16)
            return 0

        lax.fori_loop(0, SIDE, body, 0)
        for a in range(3):
            fld_s[a, 0:SIDE] = jnp.zeros((SIDE, 8, WIDE), F32)
            fld_s[a, SPOTS + SIDE : SPOTS + 2 * SIDE] = jnp.zeros((SIDE, 8, WIDE), F32)

    @pl.when(h == 0)
    def _():
        for p, (w, b) in enumerate(((wq_ref, bq_ref), (wk_ref, bk_ref), (wv_ref, bv_ref))):
            y = nn(n_s[...], w[...]) + b[...]
            field_ref[:, :, p * WIDE : (p + 1) * WIDE] = y.reshape(SPOTS, 8, WIDE)

        def branch(p, _):
            def spread(r, _):
                spots = rows_at(r, SIDE)
                ok = alive(r, large, (BAND, LANES)).reshape(SIDE, 8, LANES)
                there = rows_at(r + 1, SIDE)
                for j in range(3):
                    lanes, own = tile_at(3 * p + j), slice(j * LANES, (j + 1) * LANES)
                    y = field_ref[spots, :, lanes] * ok
                    field_ref[spots, :, lanes] = y
                    fld_s[0, there, :, own] = frame_shift(y, True)
                    fld_s[1, there, :, own] = y
                    fld_s[2, there, :, own] = frame_shift(y, False)
                return 0

            lax.fori_loop(0, SIDE, spread, 0)

            def pool(j, _):
                lanes, own = tile_at(3 * p + j), tile_at(j)
                w = [jnp.broadcast_to(pw_ref[p, t : t + 1, own], (8, LANES)) for t in range(TAPS)]

                def row(r, _):
                    acc = [None] * SIDE
                    for c_in in range(SIDE):
                        for b in range(3):
                            for a in range(3):
                                x = fld_s[a, (r + b) * SIDE + c_in, :, own]
                                for e in range(3):
                                    c = c_in - e + 1
                                    if 0 <= c < SIDE:
                                        term = w[9 * a + 3 * b + e] * x
                                        acc[c] = term if acc[c] is None else acc[c] + term
                    for c in range(SIDE):
                        pool_s[r * SIDE + c, :, lanes] = acc[c]
                    return 0

                lax.fori_loop(0, SIDE, row, 0)
                return 0

            lax.fori_loop(0, 3, pool, 0)
            return 0

        lax.fori_loop(0, 3, branch, 0)
        lane = lane_of((BAND, LANES))

        ones = ones_matrix()

        def norm(r, _):
            spots, rows = rows_at(r, SIDE), rows_at(r, BAND)
            bar = jnp.where(lane == MASK_LANE, NEG, 0.0) * (1.0 - alive(r, large, (BAND, LANES)))
            heads = []
            for p in range(3):
                heads += to_heads([
                    pool_s[spots, :, (3 * p + j) * LANES : (3 * p + j + 1) * LANES].reshape(BAND, LANES)
                    for j in range(3)
                ])
            x = jnp.concatenate(heads)
            c = jnp.where(lane_of(x.shape) < HEAD_DIM, x - fine_mean(x, ones), 0.0)
            rstd_all = lax.rsqrt(lane_mean(c * c, ones) + EPS)
            xh_all = c * rstd_all
            for k in range(3 * PER):
                p, i = k // PER, k % PER
                xh, rstd = xh_all[k * BAND : (k + 1) * BAND], rstd_all[k * BAND : (k + 1) * BAND]
                xh_ref[i, p, rows, :] = jnp.where(lane == HEAD_DIM, rstd, xh)
                y = xh * ln_ref[p : p + 1, :] + ln_ref[3 + p : 4 + p, :]
                if p == 0:
                    q_s[i, rows, :] = y
                elif p == 1:
                    k_ref[i, rows, :] = (y + marks_ref[rows, :] + bar).astype(BF16)
                else:
                    one = (lane == HEAD_DIM) | (lane == HEAD_DIM + 1)
                    v_ref[i, rows, :] = jnp.where(one, 1.0, y).astype(BF16)
            return 0

        lax.fori_loop(0, SIDE, norm, 0)
        code = code_ref[...]
        out = 1.0 - jnp.where(code == 2.0, 1.0, code * large)
        lane_m = lane_of(code.shape)
        for a, ref in enumerate((k_ref, v_ref)):
            tiles = [mem_ref[a, :, j * LANES : (j + 1) * LANES].astype(F32) for j in range(3)]
            for i, m in enumerate(to_heads(tiles)):
                if a == 0:
                    m = jnp.where(lane_m == MASK_LANE, out * NEG, m)
                else:
                    m = jnp.where((lane_m == HEAD_DIM) | (lane_m == HEAD_DIM + 1), 1.0, m)
                ref[i, LENGTH:KEYS, :] = m.astype(BF16)

    q = q_s[h]
    near = (nt(q.astype(BF16), tall_ref[...]) * sel_ref[...]).astype(BF16)
    ext = q * SCALE + nn(near, cmp_ref[...])
    q_ref[h] = jnp.where(lane_of((LENGTH, LANES)) == MASK_LANE, 1.0, ext).astype(BF16)

    lane = lane_of((LENGTH, LANES))
    scores = nt(q_ref[h], k_ref[h])
    e = jnp.exp(scores - jnp.max(scores, axis=-1, keepdims=True)).astype(BF16)
    p_ref[0] = e
    o = nn(e, v_ref[h])
    whole = o[:, HEAD_DIM : HEAD_DIM + 1]
    o = jnp.where(lane < HEAD_DIM, o * (1.0 / whole), 0.0)
    o_ref[0] = jnp.where(lane == HEAD_DIM, whole, o)
    q_s[h] += o

    @pl.when(h == PER - 1)
    def _():
        def join(r, _):
            rows = rows_at(r, BAND)
            for j, t in enumerate(to_dense([q_s[i, rows, :] for i in range(PER)])):
                att_ref[rows, j * LANES : (j + 1) * LANES] = t.astype(BF16)
            return 0

        lax.fori_loop(0, SIDE, join, 0)
        mid_ref[...] += nn(att_ref[...], wp_ref[...])

    @pl.when((h == PER - 1) & (g == GROUPS - 1))
    def _():
        for k in range(3):
            share(k, core, 0).wait()
            share(k, core, 2).wait()


def mlp_kernel(
    parts, res_ref, mid_ref, cot_ref, gain_ref, bias_ref, bd_ref, up_all, bu_all, down_all, up_any, bu_any, down_any,
    out_ref, gm_ref, gml_ref, small_ref, gup_ref, gdown_ref, gfar_ref,
    n_s, nt_s, go_s, y_s, gn_s, wide_s, stage_s, up_s, bu_s, down_s, grad_s, land_s, side_s, load_sem, send_sem, recv_sem,
):
    step = pl.program_id(0)
    large = is_large(res_ref)
    tiles, width = D // LANES, up_s.shape[2]
    cut, half = tiles * D, tiles * D // 2
    core, other, near = ("tensor", 1), ("tensor", 2), ("dp", 1)

    def slice_of(k):
        k = k // parts
        return (bit_of(*core) + 1 - k % 2) % 2 + 2 * ((bit_of(*other) + 1 - k // 2) % 2)

    def loads(k, own=False):
        up, bu, down = (up_any, bu_any, down_any) if own else [a.at[2 - k // parts] for a in (up_all, bu_all, down_all)]
        c = k % parts
        lanes = pl.ds(pl.multiple_of(c * width, LANES), width)
        return [
            pltpu.make_async_copy(up.at[:, lanes], up_s.at[k], load_sem.at[0, k]),
            pltpu.make_async_copy(bu.at[:, lanes], bu_s.at[k], load_sem.at[1, k]),
            pltpu.make_async_copy(down.at[some(c * width, width)], down_s.at[k], load_sem.at[2, k]),
        ]

    def to_core(k):
        return send(grad_s.at[2 * k], land_s.at[k], send_sem.at[k], recv_sem.at[k], core)

    def to_side():
        return send(grad_s.at[1, pl.ds(0, cut)], side_s.at[pl.ds(0, cut)], send_sem.at[2], recv_sem.at[2], other)

    def to_near():
        give = cut + (1 - bit_of(*near)) * half
        return send(grad_s.at[1, some(give, half)], side_s.at[pl.ds(cut, half)], send_sem.at[3], recv_sem.at[3], near)

    @pl.when(step == 0)
    def _():
        for k in range(parts * 4):
            for copy in loads(k, k >= 3 * parts):
                copy.start()
        greet((core, other, near))

    @pl.when(step == 2 * parts)
    def _():
        to_core(0).wait()
        add_rows(grad_s.at[1], 0, land_s.at[0], 0, 2 * cut)
        to_side().start()
        to_near().start()

    for k in range(2):

        @pl.when(step == (2 * k + 1) * parts)
        def _():
            to_core(k).start()

    @pl.when(step == 0)
    def _():
        for j in range(D // LANES):
            stage_s[j] = cot_ref[:, j * LANES : (j + 1) * LANES].astype(F32)

        def body(i, sums):
            rows = rows_at(i, BAND)
            xh, _ = row_norm(mid_ref[rows, :])
            n_s[rows, :] = (xh * line(gain_ref) + line(bias_ref)).astype(BF16)
            go = get_spots(six(stage_s), i) * alive(i, large, (BAND, D))
            wide_s[rows, :] = go
            go_s[rows, :] = go.astype(BF16)
            return sums + fold8(go)

        sums = lax.fori_loop(0, SIDE, body, jnp.zeros((8, D), F32))
        put_rows(small_ref, 12, total(sums))
        nt_s[...] = n_s[...].T

    @pl.when(step < 3 * parts)
    def _():
        for copy in loads(step):
            copy.wait()

    @pl.when(step >= 3 * parts)
    def _():
        for copy in loads(step, True):
            copy.wait()

    pre = nn(n_s[...], up_s[step]) + bu_s[step].astype(F32)[0:1, :]
    cdf = 0.5 * (1.0 + lax.erf(pre * 0.7071067811865476))
    act = (pre * cdf).astype(BF16)
    slope = cdf + pre * jnp.exp(pre * pre * -0.5) * 0.3989422804014327
    ga = nt(go_s[...], down_s[step])
    gh = ga * slope
    own, part = step // parts, step % parts
    put_rows(small_ref, 24 + slice_of(step) * tiles + part * (width // LANES), total(fold8(gh)))
    ghl = gh.astype(BF16)
    value = tn(act, go_s[...]).astype(BF16)
    for j in range(tiles):
        grad_s[own, some(cut + j * D + part * width, width), :] = value[:, j * LANES : (j + 1) * LANES]
    value = nn(nt_s[...], ghl).astype(BF16)
    for j in range(width // LANES):
        grad_s[own, some((part * (width // LANES) + j) * D, D), :] = value[:, j * LANES : (j + 1) * LANES]
    y = nn(act, down_s[step])
    gn = nt(ghl, up_s[step])

    @pl.when(step == 0)
    def _():
        y_s[...] = y
        gn_s[...] = gn

    @pl.when(step > 0)
    def _():
        y_s[...] += y
        gn_s[...] += gn

    @pl.when(step == pl.num_programs(0) - 1)
    def _():
        def body(i, sums):
            rows = rows_at(i, BAND)
            mid = mid_ref[rows, :]
            put_spots(six(stage_s), i, (mid + y_s[rows, :] + line(bd_ref)) * alive(i, large, (BAND, D)))
            xh, rstd = row_norm(mid)
            gy = gn_s[rows, :]
            gx = gy * line(gain_ref)
            m1 = jnp.mean(gx, axis=-1, keepdims=True)
            m2 = jnp.mean(gx * xh, axis=-1, keepdims=True)
            gm = wide_s[rows, :] + (gx - m1 - xh * m2) * rstd
            gm_ref[rows, :] = gm
            gml_ref[rows, :] = gm.astype(BF16)
            return sums[0] + fold8(gy * xh), sums[1] + fold8(gy), sums[2] + fold8(gm)

        zero = jnp.zeros((8, D), F32)
        sums = lax.fori_loop(0, SIDE, body, (zero, zero, zero))
        for j in range(D // LANES):
            out_ref[:, j * LANES : (j + 1) * LANES] = stage_s[j].astype(BF16)
        for at, v in zip((0, 6, 18), sums):
            put_rows(small_ref, at, total(v))
        to_core(1).wait()
        add_rows(grad_s.at[3], 0, land_s.at[1], 0, 2 * cut)
        to_side().wait()
        add_rows(grad_s.at[3], 0, side_s, 0, cut)
        to_near().wait()
        keep = cut + bit_of(*near) * half
        add_rows(grad_s.at[1], keep, side_s, cut, half)
        gup_ref[...] = grad_s[3, 0:cut, :]
        gdown_ref[...] = grad_s[3, cut : 2 * cut, :]
        gfar_ref[...] = grad_s[1, some(keep, half), :]


def bwd_kernel(
    order, res_ref, x_ref, gain_ref, bias_ref, gm_any, gml_ref, wq_ref, wk_ref, wv_ref, pw_ref, ln_ref,
    tall_ref, cmp_ref, sel_ref, pick_ref, wp_ref, field_ref, xh_ref, q_ref, k_ref, v_ref, p_ref, o_ref, att_ref,
    gup_any, gdown_any, gfar_any,
    gx_ref, small_ref, gwq_ref, gwk_ref, gwv_ref, gwp_ref, gup_out, gdown_out,
    gpw_s, gtall_s, n_s, do_s, ds_s, dpp_s, g_s, gq_s, gin_s,
    up_s, down_s, far_s, up_land, down_land, far_land, load_sem, own_sem, send_sem, recv_sem,
):
    g, h = pl.program_id(0), pl.program_id(1)
    large = is_large(res_ref)
    up_steps = chain(up_s, up_land, gup_out, send_sem.at[0], recv_sem.at[0], own_sem.at[0], order)
    side = (far_s, far_land, ("tensor", 2))
    down_steps = chain(down_s, down_land, gdown_out, send_sem.at[1], recv_sem.at[1], own_sem.at[1], order, side)

    def travel(tick):
        at_ticks(tick, UP_TICKS, up_steps)
        at_ticks(tick, DOWN_TICKS, down_steps)

    @pl.when((g == 0) & (h == 0))
    def _():
        loads = [
            pltpu.make_async_copy(src, dst, load_sem.at[k])
            for k, (src, dst) in enumerate(((gup_any, up_s), (gdown_any, down_s), (gfar_any, far_s)))
        ]
        for copy in loads:
            copy.start()
        greet((("tensor", 2), *order))
        for copy in loads:
            copy.wait()

    travel((PER + 3) * g + h)

    @pl.when((g == 0) & (h == 0))
    def _():
        def body(i, _):
            rows = rows_at(i, BAND)
            xh, _ = row_norm(x_ref[rows, :].astype(F32))
            n_s[rows, :] = (xh * line(gain_ref) + line(bias_ref)).astype(BF16)
            return 0

        lax.fori_loop(0, SIDE, body, 0)
        for a in range(3):
            g_s[a, 0:SIDE] = jnp.zeros((SIDE, 8, WIDE), F32)
            g_s[a, SPOTS + SIDE : SPOTS + 2 * SIDE] = jnp.zeros((SIDE, 8, WIDE), F32)
        gtall_s[...] = jnp.zeros(gtall_s.shape, F32)
        small_ref[...] = jnp.zeros(small_ref.shape, F32)
        gpw_s[...] = jnp.zeros(gpw_s.shape, F32)

    @pl.when(h == 0)
    def _():
        gin_s[:, 0:WIDE] = nt(gml_ref[...], wp_ref[...])

        def split(r, _):
            rows = rows_at(r, BAND)
            tiles = [gin_s[rows, j * LANES : (j + 1) * LANES] for j in range(3)]
            for i, t in enumerate(to_heads(tiles)):
                do_s[i, rows, :] = t
            return 0

        lax.fori_loop(0, SIDE, split, 0)
        gw = tn(att_ref[...], gml_ref[...])
        for j in range(D // LANES):
            gwp_ref[j] = gw[:, j * LANES : (j + 1) * LANES].astype(BF16)

    lane = lane_of((LENGTH, LANES))
    do = do_s[h]
    o = o_ref[0]
    inv = 1.0 / o[:, HEAD_DIM : HEAD_DIM + 1]
    ones = ones_matrix()
    delta = nn((do * o).astype(BF16), ones) * inv
    high = delta.astype(BF16).astype(F32)
    doe = jnp.where(lane == HEAD_DIM, -high, jnp.where(lane == HEAD_DIM + 1, high - delta, do * inv)).astype(BF16)
    ds_s[...] = (p_ref[0].astype(F32) * nt(doe, v_ref[0])).astype(BF16)
    dqe = nn(ds_s[...], k_ref[0])
    dk = tn(q_ref[0], ds_s[...]).T[:LENGTH]
    dv = tn(doe, p_ref[0]).T[:LENGTH]
    far = (nt(dqe.astype(BF16), cmp_ref[...]) * sel_ref[...]).astype(BF16)
    xq = xh_ref[0, 0]
    query = (jnp.where(lane < HEAD_DIM, xq, 0.0) * ln_ref[0:1, :] + ln_ref[3:4, :]).astype(BF16)
    gtall_s[...] += tn(far, query)
    dq = dqe * SCALE + do + nn(far, tall_ref[...])
    for p, gy in enumerate((dq, dk, dv)):
        raw = xh_ref[0, p]
        rstd = raw[:, HEAD_DIM : HEAD_DIM + 1]
        gx = gy * ln_ref[p : p + 1, :]
        m1 = lane_mean(gx, ones)
        m2 = lane_mean(gx * raw, ones)
        dpp_s[h, p] = (gx - m1 - raw * m2) * rstd
        small_ref[96 + p : 97 + p, :] += total(fold8(gy * raw))
        small_ref[99 + p : 100 + p, :] += total(fold8(gy))

    @pl.when(h == PER - 1)
    def _():
        def branch(p, _):
            def spread(r, _):
                there, rows = rows_at(r + 1, SIDE), rows_at(r, BAND)
                for j, t in enumerate(to_dense([dpp_s[i, p, rows, :] for i in range(PER)])):
                    lanes = slice(j * LANES, (j + 1) * LANES)
                    t = t.reshape(SIDE, 8, LANES)
                    g_s[0, there, :, lanes] = frame_shift(t, False)
                    g_s[1, there, :, lanes] = t
                    g_s[2, there, :, lanes] = frame_shift(t, True)
                return 0

            lax.fori_loop(0, SIDE, spread, 0)

            def pool(j, _):
                lanes, own = tile_at(3 * p + j), tile_at(j)
                w = [jnp.broadcast_to(pw_ref[p, t : t + 1, own], (8, LANES)) for t in range(TAPS)]

                def row(r, sums):
                    sums = list(sums)
                    x = [field_ref[r * SIDE + c, :, lanes] for c in range(SIDE)]
                    acc = [None] * SIDE
                    for c_in in range(SIDE):
                        for b in range(3):
                            for a in range(3):
                                t = g_s[a, (r + 2 - b) * SIDE + c_in, :, own]
                                for e in range(3):
                                    c, k = c_in + e - 1, 9 * a + 3 * b + e
                                    if 0 <= c < SIDE:
                                        term = w[k] * t
                                        acc[c] = term if acc[c] is None else acc[c] + term
                                        sums[k] = sums[k] + x[c] * t
                    for c in range(SIDE):
                        gin_s[pl.ds(pl.multiple_of(r * BAND + c * 8, 8), 8), lanes] = acc[c]
                    return tuple(sums)

                sums = lax.fori_loop(0, SIDE, row, tuple(jnp.zeros((8, LANES), F32) for _ in range(TAPS)))
                for t in range(TAPS):
                    gpw_s[t : t + 1, own] = total(sums[t])
                return 0

            lax.fori_loop(0, 3, pool, 0)
            travel((PER + 3) * g + PER + p)
            heads = to_heads([gpw_s[:, j * LANES : (j + 1) * LANES] for j in range(3)])
            small_ref[rows_at(p, 32), :] += heads[0] + heads[1] + heads[2] + heads[3]
            return 0

        lax.fori_loop(0, 3, branch, 0)

        def finish(r, sums):
            rows = rows_at(r, BAND)
            t = gin_s[rows, :] * alive(r, large, (BAND, 3 * WIDE))
            gq_s[rows, :] = t.astype(BF16)
            return sums + fold8(t)

        put_rows(small_ref, 168 + 9 * g, total(lax.fori_loop(0, SIDE, finish, jnp.zeros((8, 3 * WIDE), F32))))
        gm_load = pltpu.make_async_copy(gm_any, gin_s.at[:, pl.ds(0, D)], load_sem.at[3])

        @pl.when(g == GROUPS - 1)
        def _():
            gm_load.start()

        gn = None
        for p, (w, gw) in enumerate(((wq_ref, gwq_ref), (wk_ref, gwk_ref), (wv_ref, gwv_ref))):
            piece = gq_s[:, p * WIDE : (p + 1) * WIDE]
            value = tn(n_s[...], piece)
            for j in range(WIDE // LANES):
                gw[j] = value[:, j * LANES : (j + 1) * LANES].astype(BF16)
            term = nt(piece, w[...])
            gn = term if gn is None else gn + term

        @pl.when(g == 0)
        def _():
            gx_ref[...] = gn

        @pl.when(g > 0)
        def _():
            gx_ref[...] += gn

    @pl.when((h == PER - 1) & (g == GROUPS - 1))
    def _():
        pltpu.make_async_copy(gm_any, gin_s.at[:, pl.ds(0, D)], load_sem.at[3]).wait()
        stage = [(dpp_s, (j // 3, j % 3)) for j in range(D // LANES)]

        def body(i, sums):
            rows = rows_at(i, BAND)
            xh, rstd = row_norm(x_ref[rows, :].astype(F32))
            gy = gx_ref[rows, :]
            gx = gy * line(gain_ref)
            m1 = jnp.mean(gx, axis=-1, keepdims=True)
            m2 = jnp.mean(gx * xh, axis=-1, keepdims=True)
            put_spots(stage, i, gin_s[rows, 0:D] + (gx - m1 - xh * m2) * rstd)
            return sums[0] + fold8(gy * xh), sums[1] + fold8(gy)

        zero = jnp.zeros((8, D), F32)
        sums = lax.fori_loop(0, SIDE, body, (zero, zero))
        for j, (ref, at) in enumerate(stage):
            gx_ref[:, j * LANES : (j + 1) * LANES] = ref[at]
        put_rows(small_ref, 186, total(sums[0]))
        put_rows(small_ref, 192, total(sums[1]))
        rest, rel = gtall_s[...], None
        for _ in range(3):
            part = rest.astype(BF16)
            rest = rest - part.astype(F32)
            term = nn(pick_ref[...], part)
            rel = term if rel is None else rel + term
        small_ref[104:168, :] = rel
        travel(2 * (PER + 3))


def reduce_kernel(parts, pieces, links, *refs):
    n = len(pieces)
    ins, one, two, out, small = refs[:n], refs[n], refs[n + 1], refs[n + 2], refs[n + 3]
    big, land, small_land, load_sem, send_sem, recv_sem, own_sem, ssend_sem, srecv_sem = refs[n + 4 :]
    loads = [
        pltpu.make_async_copy(ref, big.at[pl.ds(first, rows)], load_sem.at[i])
        for i, (ref, (first, rows)) in enumerate(zip(ins, pieces))
    ]
    for copy in loads:
        copy.start()
    greet(links)
    small[0 : one.shape[0]] = one[...]
    small[one.shape[0] :] = two[...]
    for copy in loads:
        copy.wait()
    chains = []
    for i, (first, rows, order) in enumerate(parts):
        here = pl.ds(first, rows)
        chains.append(
            chain(big.at[here], land.at[here], out.at[here], send_sem.at[i], recv_sem.at[i], own_sem.at[i], order)
        )

    def extra(s):
        return send(small, small_land.at[s], ssend_sem.at[s], srecv_sem.at[s], links[s])

    for k in range(max(len(c) for c in chains)):
        for c in chains:
            if k < len(c):
                c[k]()
        if 0 < k <= len(links):
            extra(k - 1).wait()
            small[...] += small_land[k - 1]
        if k < len(links):
            extra(k).start()


def all_reduce(whole, one, two, sizes):
    dp, tensor = bits("dp", sizes["dp"]), bits("tensor", sizes["tensor"])
    links = tensor + dp
    small = sds((one.shape[0] + two.shape[0], LANES), F32)
    pieces, at = [], 0
    for a in whole:
        pieces.append((at, a.shape[0]))
        at += a.shape[0]
    core, rest = tensor[:1], tensor[1:]
    one_way, other_way = core + rest + dp, core + dp[:1] + rest + dp[1:]
    far_ways = [core + dp[1:2] + rest + dp[:1] + dp[2:], core + dp[1:2] + dp[:1] + rest + dp[2:]]
    ways = [one_way, other_way, far_ways[0], one_way, other_way, far_ways[1]]
    count = next(n for n in (12, 6, 3) if len(links) <= halvings(at // n) + 1)
    orders = (ways + ways)[:count]
    share = at // len(orders)
    parts = [(k * share, share, order) for k, order in enumerate(orders)]
    assert at % len(orders) == 0 and all(len(order) <= halvings(rows) + 1 for _, rows, order in parts)
    dma = pltpu.SemaphoreType.DMA
    stages = 2 * len(links)
    return pl.pallas_call(
        functools.partial(reduce_kernel, parts, pieces, links),
        in_specs=[pl.BlockSpec(memory_space=pl.ANY)] * len(pieces) + [pl.BlockSpec(memory_space=pltpu.VMEM)] * 2,
        out_specs=[pl.BlockSpec(memory_space=pltpu.VMEM)] * 2,
        out_shape=[sds((at, LANES), BF16), small],
        scratch_shapes=[
            pltpu.VMEM((at, LANES), BF16),
            pltpu.VMEM((at, LANES), BF16),
            pltpu.VMEM((len(links), *small.shape), F32),
            dma((len(pieces),)),
            dma((len(parts), stages)), dma((len(parts), stages)), dma((len(parts),)),
            dma((len(links),)), dma((len(links),)),
        ],
        compiler_params=pltpu.CompilerParams(
            vmem_limit_bytes=VMEM_LIMIT, collective_id=1, has_side_effects=True
        ),
        name="sum_all",
        cost_estimate=pl.CostEstimate(flops=10_000_000, bytes_accessed=20_000_000, transcendentals=0),
    )(*whole, one, two)


def unpack_kernel(big_ref, up_ref, down_ref, small_ref, *outs):
    squares, vectors, gb_ref, gpw_ref, gain_ref, bias_ref, rel_ref = outs[:4], outs[4:11], *outs[11:]
    for out, ref, first, n in zip(squares, (big_ref, big_ref, up_ref, down_ref), (0, 18, 0, 0), (18, 6, 6, 6)):
        for j in range(n):
            out[:, j * LANES : (j + 1) * LANES] = ref[first + j].astype(F32)

    @pl.when(pl.program_id(0) == 0)
    def _():
        own = 232 + 6 * lax.axis_index("tensor")
        for ref, at in zip(vectors, (186, 192, 226, 208, 214, 220, own)):
            for j in range(6):
                ref[j * LANES : (j + 1) * LANES] = small_ref[at + j, :]
        for g in range(GROUPS):
            for j in range(9):
                to = (j // 3) * D + g * WIDE + j % 3 * LANES
                gb_ref[to : to + LANES] = small_ref[168 + 9 * g + j, :]
        for p in range(3):
            gpw_ref[p] = small_ref[32 * p : 32 * p + TAPS, :HEAD_DIM]
        gain_ref[...] = small_ref[96:99, :HEAD_DIM]
        bias_ref[...] = small_ref[99:102, :HEAD_DIM]
        rel_ref[...] = small_ref[104 : 104 + REL_ROWS, :HEAD_DIM]


def unpack(big, up, down, small):
    def whole(*shape):
        return pl.BlockSpec(shape, lambda i: (0,) * len(shape))

    def band(width):
        return pl.BlockSpec((LANES, width), lambda i: (i, 0))

    shapes = [(D,)] * 7 + [(3 * D,), (3, TAPS, HEAD_DIM), (3, HEAD_DIM), (3, HEAD_DIM), (REL_ROWS, HEAD_DIM)]
    return pl.pallas_call(
        unpack_kernel,
        grid=(D // LANES,),
        in_specs=[
            *[pl.BlockSpec((n, LANES, LANES), lambda i: (0, i, 0)) for n in (24, 6, 6)], whole(*small.shape),
        ],
        out_specs=[band(3 * D), band(D), band(D), band(D), *[whole(*shape) for shape in shapes]],
        out_shape=[sds((D, 3 * D), F32), *[sds((D, D), F32)] * 3, *[sds(shape, F32) for shape in shapes]],
        name="unpack",
        cost_estimate=pl.CostEstimate(flops=0, bytes_accessed=22_000_000, transcendentals=0),
    )(big, up, down, small)


def position_tables():
    spot = np.arange(LENGTH) // FRAMES
    frame, row, column = np.arange(LENGTH) % FRAMES, spot // SIDE, spot % SIDE
    kinds = ((frame, FRAMES, 0), (row, SIDE, FRAMES), (column, SIDE, FRAMES + SIDE))
    bases = (FRAMES - 1, 2 * FRAMES - 1 + SIDE - 1, 2 * FRAMES - 1 + 2 * SIDE - 1 + SIDE - 1)
    pick = np.zeros((PAIRS, REL_ROWS), np.float32)
    squeeze = np.zeros((PAIRS, LANES), np.float32)
    select = np.zeros((LENGTH, PAIRS), np.float32)
    marks = np.zeros((LENGTH, LANES), np.float32)
    for tile, ((where, size, first), base) in enumerate(zip(kinds, bases)):
        for at in range(size):
            for m in range(size):
                col = tile * LANES + at * size + m
                pick[col, base + at - m] = 1.0
                squeeze[col, HEAD_DIM + first + m] = 1.0
                select[:, col] = where == at
        marks[np.arange(LENGTH), HEAD_DIM + first + where] = 1.0
    memory_at = np.arange(KEYS - LENGTH) % (MEM // 2)
    half, small = (SIDE + 1) // 2, (SMALL_SIDE + 1) // 2
    memory_inside = (memory_at // half % half < small) & (memory_at % half < small)
    exists = np.arange(KEYS - LENGTH) < MEM
    code = np.where(exists, 1.0 + memory_inside, 0.0).astype(np.float32)
    return pick, squeeze, select, marks, np.repeat(code[:, None], LANES, 1)


def blocked(shape, index, single=False):
    if single:
        return pl.BlockSpec(shape, index, pipeline_mode=pl.Buffered(1))
    return pl.BlockSpec(shape, index)


def const(shape):
    return blocked(shape, lambda *_: (0,) * len(shape), True)


def sds(shape, dtype):
    return jax.ShapeDtypeStruct(shape, dtype)


def per_device(
    inputs, res_ids, memory, gain_one, bias_one, w_qkv, b_qkv, pool_weight, pool_gain, pool_bias, rel_table,
    w_proj, b_proj, gain_two, bias_two, w_up, b_up, w_down, b_down, cotangent,
):
    split = lax.axis_size("tensor")
    pick, squeeze, select, marks, code = position_tables()
    assert split == 4
    b_rows = jnp.broadcast_to(b_up, (16, b_up.shape[0]))
    pw = jnp.pad(jnp.tile(pool_weight, (1, 1, PER)), ((0, 0), (0, 5), (0, 0)))
    ln = jnp.pad(jnp.concatenate([pool_gain, pool_bias]), ((0, 2), (0, LANES - HEAD_DIM)))
    tall = jnp.dot(pick, rel_table, precision=lax.Precision.HIGHEST)
    tall = jnp.pad(tall, ((0, 0), (0, LANES - HEAD_DIM))).astype(BF16)
    cmp = jnp.asarray(squeeze, BF16)
    mem = jnp.pad(memory, ((0, 0), (0, KEYS - LENGTH - MEM), (0, 0)))
    bq = b_qkv.reshape(1, -1)

    dma = pltpu.SemaphoreType.DMA
    anywhere = pl.BlockSpec(memory_space=pl.ANY)
    w_spec = [blocked((D, WIDE), lambda g, h, p=p: (0, GROUPS * p + g)) for p in range(3)]
    b_spec = [blocked((1, WIDE), lambda g, h, p=p: (0, GROUPS * p + g)) for p in range(3)]

    scalar = pl.BlockSpec(memory_space=pltpu.SMEM)
    row = const((D,))

    def per_group(*shape):
        return blocked(shape, lambda g, h: (g,) + (0,) * (len(shape) - 1))

    def per_head(*shape):
        return blocked(shape, lambda g, h: (PER * g + h,) + (0,) * (len(shape) - 1))

    field_spec = blocked((SPOTS, 8, 3 * WIDE), lambda g, h: (0, 0, g))
    att_spec = blocked((LENGTH, WIDE), lambda g, h: (0, g))
    mid, xs, field, xh, qx, kx, vx, probs, outs, att, up_all, bu_all, down_all = pl.pallas_call(
        fwd_kernel,
        grid=(GROUPS, PER),
        in_specs=[
            scalar, const((LENGTH, D)), row, row, row, *w_spec, *b_spec,
            const((3, 32, WIDE)), const((8, LANES)), const((PAIRS, LANES)), const((PAIRS, LANES)),
            const((LENGTH, PAIRS)), const((LENGTH, LANES)), const((KEYS - LENGTH, LANES)),
            blocked((2, KEYS - LENGTH, WIDE), lambda g, h: (0, 0, g)),
            blocked((WIDE, D), lambda g, h: (g, 0)), anywhere, anywhere, anywhere,
        ],
        out_specs=[
            const((LENGTH, D)), const((LENGTH, D)), field_spec, per_group(PER, 3, LENGTH, LANES), per_group(PER, LENGTH, LANES),
            per_group(PER, KEYS, LANES), per_group(PER, KEYS, LANES), per_head(1, LENGTH, KEYS),
            per_head(1, LENGTH, LANES), att_spec, anywhere, anywhere, anywhere,
        ],
        out_shape=[
            sds((LENGTH, D), F32), sds((LENGTH, D), BF16), sds((SPOTS, 8, 3 * D), F32), sds((HEADS, 3, LENGTH, LANES), F32),
            sds((HEADS, LENGTH, LANES), BF16), sds((HEADS, KEYS, LANES), BF16), sds((HEADS, KEYS, LANES), BF16),
            sds((HEADS, LENGTH, KEYS), BF16), sds((HEADS, LENGTH, LANES), F32), sds((LENGTH, D), BF16),
            *[sds((split - 1, *a.shape), BF16) for a in (w_up, b_rows, w_down)],
        ],
        scratch_shapes=[
            dma((3, 3)), dma((3, 3)),
            pltpu.VMEM((LENGTH, D), BF16),
            pltpu.VMEM((3, SPOTS + 2 * SIDE, 8, WIDE), F32),
            pltpu.VMEM((SPOTS, 8, 3 * WIDE), F32),
            pltpu.VMEM((PER, LENGTH, LANES), F32),
            pltpu.VMEM((D // LANES, LENGTH, LANES), F32),
        ],
        compiler_params=pltpu.CompilerParams(vmem_limit_bytes=VMEM_LIMIT, collective_id=4, has_side_effects=True),
        name="attend",
        cost_estimate=pl.CostEstimate(flops=2 * 3_500_000_000, bytes_accessed=60_000_000, transcendentals=6_500_000),
    )(
        res_ids, inputs, gain_one, bias_one, b_proj, w_qkv, w_qkv, w_qkv, bq, bq, bq, pw, ln,
        tall, cmp, jnp.asarray(select), jnp.asarray(marks), jnp.asarray(code), mem, w_proj, w_up, b_rows, w_down,
    )

    hidden = w_up.shape[1]
    piece = 384
    parts = hidden // piece
    tiles = hidden // LANES
    chunks, cut = split * parts, D // LANES * D
    out, gm, gml, small, gup, gdown, gfar = pl.pallas_call(
        functools.partial(mlp_kernel, parts),
        grid=(chunks,),
        in_specs=[scalar, const((LENGTH, D)), const((LENGTH, D)), row, row, row, *[anywhere] * 6],
        out_specs=[
            const((LENGTH, D)), const((LENGTH, D)), const((LENGTH, D)), const((24 + split * tiles, LANES)),
            const((cut, LANES)), const((cut, LANES)), const((cut // 2, LANES)),
        ],
        out_shape=[
            sds((LENGTH, D), BF16), sds((LENGTH, D), F32), sds((LENGTH, D), BF16), sds((24 + split * tiles, LANES), F32),
            sds((cut, LANES), BF16), sds((cut, LANES), BF16), sds((cut // 2, LANES), BF16),
        ],
        scratch_shapes=[
            pltpu.VMEM((LENGTH, D), BF16),
            pltpu.VMEM((D, LENGTH), BF16),
            pltpu.VMEM((LENGTH, D), BF16),
            *[pltpu.VMEM((LENGTH, D), F32)] * 3,
            pltpu.VMEM((D // LANES, LENGTH, LANES), F32),
            pltpu.VMEM((chunks, D, piece), BF16),
            pltpu.VMEM((chunks, 16, piece), BF16),
            pltpu.VMEM((chunks, piece, D), BF16),
            pltpu.VMEM((split, 2 * cut, LANES), BF16),
            pltpu.VMEM((2, 2 * cut, LANES), BF16),
            pltpu.VMEM((cut + cut // 2, LANES), BF16),
            dma((3, chunks)), dma((4,)), dma((4,)),
        ],
        compiler_params=pltpu.CompilerParams(vmem_limit_bytes=VMEM_LIMIT, collective_id=2, has_side_effects=True),
        name="mlp",
        cost_estimate=pl.CostEstimate(flops=2 * 11_300_000_000, bytes_accessed=40_000_000, transcendentals=5_000_000),
    )(res_ids, mid, cotangent, gain_two, bias_two, b_down, up_all, bu_all, down_all, w_up, b_rows, w_down)

    links = bits("dp", lax.axis_size("dp"))
    gx, small_one, gwq, gwk, gwv, gwp, gup, gdown = pl.pallas_call(
        functools.partial(bwd_kernel, links),
        grid=(GROUPS, PER),
        in_specs=[
            scalar, const((LENGTH, D)), row, row, anywhere, const((LENGTH, D)), *w_spec,
            const((3, 32, WIDE)), const((8, LANES)), const((PAIRS, LANES)), const((PAIRS, LANES)),
            const((LENGTH, PAIRS)), const((64, PAIRS)), blocked((WIDE, D), lambda g, h: (g, 0)),
            blocked((SPOTS, 8, 3 * WIDE), lambda g, h: (0, 0, g), True),
            per_head(1, 3, LENGTH, LANES), per_head(1, LENGTH, LANES), per_head(1, KEYS, LANES),
            per_head(1, KEYS, LANES), per_head(1, LENGTH, KEYS), per_head(1, LENGTH, LANES), att_spec,
            anywhere, anywhere, anywhere,
        ],
        out_specs=[
            const((LENGTH, D)), const((208, LANES)),
            *[blocked((3, D, LANES), lambda g, h: (g, 0, 0)) for _ in range(3)],
            blocked((6, WIDE, LANES), lambda g, h: (0, g, 0)), anywhere, anywhere,
        ],
        out_shape=[
            sds((LENGTH, D), F32), sds((208, LANES), F32), *[sds((6, D, LANES), BF16)] * 4,
            sds((cut, LANES), BF16), sds((cut, LANES), BF16),
        ],
        scratch_shapes=[
            pltpu.VMEM((32, WIDE), F32),
            pltpu.VMEM((PAIRS, LANES), F32),
            pltpu.VMEM((LENGTH, D), BF16),
            pltpu.VMEM((PER, LENGTH, LANES), F32),
            pltpu.VMEM((LENGTH, KEYS), BF16),
            pltpu.VMEM((PER, 3, LENGTH, LANES), F32),
            pltpu.VMEM((3, SPOTS + 2 * SIDE, 8, WIDE), F32),
            pltpu.VMEM((LENGTH, 3 * WIDE), BF16),
            pltpu.VMEM((LENGTH, 3 * WIDE), F32),
            pltpu.VMEM((cut, LANES), BF16), pltpu.VMEM((cut, LANES), BF16), pltpu.VMEM((cut // 2, LANES), BF16),
            pltpu.VMEM((cut, LANES), BF16), pltpu.VMEM((cut, LANES), BF16), pltpu.VMEM((cut // 2, LANES), BF16),
            dma((4,)), dma((2,)), dma((2, 2 * len(links) + 1)), dma((2, 2 * len(links) + 1)),
        ],
        compiler_params=pltpu.CompilerParams(vmem_limit_bytes=VMEM_LIMIT, collective_id=3, has_side_effects=True),
        name="attend_back",
        cost_estimate=pl.CostEstimate(flops=2 * 7_000_000_000, bytes_accessed=60_000_000, transcendentals=0),
    )(
        res_ids, xs, gain_one, bias_one, gm, gml, w_qkv, w_qkv, w_qkv, pw, ln, tall, cmp, jnp.asarray(select), jnp.asarray(np.pad(pick.T, ((0, 11), (0, 0))), BF16), w_proj,
        field, xh, qx, kx, vx, probs, outs, att, gup, gdown, gfar,
    )

    flat = [a.reshape(-1, LANES) for a in (gwq, gwk, gwv, gwp)]
    sizes = {axis: lax.axis_size(axis) for axis in ("dp", "tensor")}
    big, small = all_reduce(flat, small_one, small, sizes)
    outs = unpack(*[a.reshape(-1, D, LANES) for a in (big, gup, gdown)], small)
    squares, (gain1, bias1, bp, gain2, bias2, bd, bu), (gb, gpw, pg, pb, rel) = outs[:4], outs[4:11], outs[11:]

    return (
        out, gx, gain1, bias1, squares[0], gb, gpw, pg, pb, rel, squares[1], bp, gain2, bias2, squares[2], bu, squares[3], bd,
    )


def solution(mesh):
    rows = P(("dp", "tensor"), None)
    return jax.shard_map(
        per_device,
        mesh=mesh,
        in_specs=(
            rows, P(("dp", "tensor")), P(None, ("dp", "tensor"), None), *[P()] * 12,
            P(None, "tensor"), P("tensor"), P("tensor", None), P(), rows,
        ),
        out_specs=(rows, rows, *[P()] * 12, P(None, "tensor"), P("tensor"), P("tensor", None), P()),
        check_vma=False,
    )
```

```python
import functools

import jax
import jax.numpy as jnp
import numpy as np
from jax import lax
from jax.experimental import pallas as pl
from jax.experimental.pallas import tpu as pltpu
from jax.sharding import PartitionSpec as P

D = 768
HEADS = 8
HEAD_DIM = 96
FRAMES = 8
SIDE = 10
SMALL_SIDE = 7
SPOTS = SIDE * SIDE
LENGTH = FRAMES * SPOTS
MEM = 200
KEYS = 1024
OFFSETS = FRAMES + 2 * SIDE
REL_ROWS = 53
GROUPS = 2
PER = HEADS // GROUPS
WIDE = PER * HEAD_DIM
TAPS = 27
LANES = 128
BAND = SIDE * FRAMES
PAIRS = 384
MASK_LANE = HEAD_DIM + OFFSETS
EPS = 1e-6
SCALE = HEAD_DIM**-0.5
F32 = jnp.float32
BF16 = jnp.bfloat16
NEG = -1e30
UP_TICKS = (0, 3, 4, 5, 6, 8, 11)
DOWN_TICKS = (3, 5, 7, 9, 10, 11, 12, 14)
FIRST_TICKS = (7, 8, 10, 11, 12, 14)
VMEM_LIMIT = 60 * 1024 * 1024


def nn(a, b):
    return jnp.dot(a, b, preferred_element_type=F32)


def nt(a, b):
    return lax.dot_general(a, b, (((1,), (1,)), ((), ())), preferred_element_type=F32)


def tn(a, b):
    return lax.dot_general(a, b, (((0,), (0,)), ((), ())), preferred_element_type=F32)


def lane_of(shape):
    return lax.broadcasted_iota(jnp.int32, shape, len(shape) - 1)


def to_heads(tiles):
    t0, t1, t2 = tiles
    lane = lane_of(t0.shape)
    own = lane < HEAD_DIM
    h1 = pltpu.roll(jnp.where(lane >= 96, t0, t1), 32, t0.ndim - 1)
    h2 = pltpu.roll(jnp.where(lane >= 64, t1, t2), 64, t0.ndim - 1)
    h3 = pltpu.roll(t2, 96, t0.ndim - 1)
    return [jnp.where(own, h, 0.0) for h in (t0, h1, h2, h3)]


def to_dense(heads):
    p0, p1, p2, p3 = heads
    lane = lane_of(p0.shape)
    r1 = pltpu.roll(p1, 96, p0.ndim - 1)
    r2 = pltpu.roll(p2, 64, p0.ndim - 1)
    r3 = pltpu.roll(p3, 32, p0.ndim - 1)
    return [jnp.where(lane < 96, p0, r1), jnp.where(lane < 64, r1, r2), jnp.where(lane < 32, r2, r3)]


def row_norm(x):
    mean = jnp.mean(x, axis=-1, keepdims=True)
    c = x - mean
    rstd = lax.rsqrt(jnp.mean(c * c, axis=-1, keepdims=True) + EPS)
    return c * rstd, rstd


def ones_matrix():
    return jnp.where(lax.broadcasted_iota(jnp.int32, (LANES, LANES), 0) < HEAD_DIM, 1.0, 0.0).astype(BF16)


def lane_mean(x, ones):
    return nn(x.astype(BF16), ones) * (1 / HEAD_DIM)


def fine_mean(x, ones):
    high = x.astype(BF16)
    low = (x - high.astype(F32)).astype(BF16)
    return nn(jnp.concatenate([high, low], axis=1), jnp.concatenate([ones, ones])) * (1 / HEAD_DIM)


def frame_shift(x, up):
    frame = lax.broadcasted_iota(jnp.int32, x.shape, 1)
    if up:
        return jnp.where(frame == 0, 0.0, pltpu.roll(x, 1, 1))
    return jnp.where(frame == FRAMES - 1, 0.0, pltpu.roll(x, FRAMES - 1, 1))


def fold8(x):
    return jnp.sum(x.reshape(x.shape[0] // 8, 8, x.shape[1]), axis=0)


def put_rows(ref, at, v):
    for j in range(v.shape[1] // LANES):
        ref[pl.ds(at + j, 1), :] = v[:, j * LANES : (j + 1) * LANES]


def total(x):
    return jnp.sum(x, axis=0, keepdims=True)


def alive(r, large, shape):
    inside = jnp.where(r < SMALL_SIDE, SMALL_SIDE * FRAMES, 0)
    return jnp.where(lax.broadcasted_iota(jnp.int32, shape, 0) < inside, 1.0, large)


def is_large(res_ref):
    return jnp.where(res_ref[0] == 1, 1.0, 0.0).astype(F32)


def put_spots(tiles, r, x):
    for c in range(SIDE):
        for j, (ref, at) in enumerate(tiles):
            to = pl.ds(r * SIDE + c, FRAMES, stride=SPOTS)
            ref[(*at, to, slice(None))] = x[c * FRAMES : (c + 1) * FRAMES, j * LANES : (j + 1) * LANES]


def get_spots(tiles, r):
    rows = [
        jnp.concatenate([ref[(*at, pl.ds(r * SIDE + c, FRAMES, stride=SPOTS), slice(None))] for ref, at in tiles], axis=1)
        for c in range(SIDE)
    ]
    return jnp.concatenate(rows)


def six(ref):
    return [(ref, (j,)) for j in range(D // LANES)]


def line(ref):
    return ref[...].reshape(1, ref.shape[0])


def tile_at(j):
    return pl.ds(pl.multiple_of(j * LANES, LANES), LANES)


def rows_at(r, size):
    if isinstance(r, int):
        return pl.ds(r * size, size)
    return pl.ds(pl.multiple_of(r * size, size), size)


def bit_of(axis, bit):
    return lax.axis_index(axis) // bit % 2


def partner_of(axis, bit):
    me = lax.axis_index(axis)
    return {axis: me + (1 - 2 * (me // bit % 2)) * bit}


def halvings(rows):
    count = 0
    while rows % (32 << count) == 0:
        count += 1
    return count


def bits(axis, size):
    return [(axis, 1 << k) for k in range(size.bit_length() - 1)]


def send(src, dst, one, two, link):
    return pltpu.make_async_remote_copy(
        src_ref=src, dst_ref=dst, send_sem=one, recv_sem=two,
        device_id=partner_of(*link), device_id_type=pl.DeviceIdType.MESH,
    )


def greet(links):
    barrier = pltpu.get_barrier_semaphore()
    for link in links:
        pl.semaphore_signal(barrier, inc=1, device_id=partner_of(*link), device_id_type=pl.DeviceIdType.MESH)
    pl.semaphore_wait(barrier, len(links))


def some(start, rows):
    return pl.ds(pl.multiple_of(start, 16), rows)


def add_rows(dst, at, src, start, rows):
    block = next(b for b in (512, 256, 128, 64, 48, 32, 16) if rows % b == 0)

    def add(k, _):
        a, b = some(at + k * block, block), some(start + k * block, block)
        dst[a, :] = (dst[a, :].astype(F32) + src[b, :].astype(F32)).astype(BF16)
        return 0

    lax.fori_loop(0, rows // block, add, 0)


def span(rows, order, s):
    off, size = 0, rows
    for k in range(min(s, halvings(rows))):
        size //= 2
        off = off + bit_of(*order[k]) * size
    return off, size


def landing(rows, count):
    return rows + max(0, count - halvings(rows) - 1) * (rows >> halvings(rows))


def chain(work, land, out, send_sem, recv_sem, own_sem, order, merge=None, own=None):
    rows = (work if own is None else out).shape[0]
    count = halvings(rows)

    def halve(s, k):
        off, size = span(rows, order, s)
        half, bit, at = size // 2, bit_of(*order[s]), rows - size
        keep, give = off + bit * half, off + (1 - bit) * half
        if s >= count:
            keep, give, half, at = off, off, size, rows - size + (s - count) * size
        copy = send(work.at[some(give, half)], land.at[some(at, half)], send_sem.at[k], recv_sem.at[k], order[s])
        return copy, (work, keep, land, at, half)

    def join(k):
        ref, there, link = merge
        keep = span(rows, order, 1)[0]
        return send(ref, there, send_sem.at[k], recv_sem.at[k], link), (work, keep, there, 0, ref.shape[0])

    def double(s, k):
        off, size = span(rows, order, s + 1)
        here = out.at[some(off, size)]
        return send(here, here, send_sem.at[k], recv_sem.at[k], order[s]), None

    plans = []
    if own is None:
        plans = [functools.partial(halve, s) for s in range(len(order))]
    if merge is not None:
        plans.insert(1, join)
    gather = len(plans)
    if out is not None:
        plans += [functools.partial(double, s) for s in reversed(range(min(len(order), count)))]

    def start(k):
        if k == gather:
            off, size = span(rows, order, len(order))
            mine = work.at[some(off, size)] if own is None else own
            copy = pltpu.make_async_copy(mine, out.at[some(off, size)], own_sem)
            copy.start()
            copy.wait()
        plans[k](k)[0].start()

    def finish(k):
        copy, todo = plans[k](k)
        copy.wait()
        if todo is not None:
            add_rows(*todo)

    def step(k):
        if k > 0:
            finish(k - 1)
        if k < len(plans):
            start(k)

    return [functools.partial(step, k) for k in range(len(plans) + 1)]


def at_ticks(tick, table, steps):
    for n in sorted(set(table)):
        due = [k for k in range(len(steps)) if table[min(k, len(table) - 1)] == n]

        @pl.when(tick == n)
        def _():
            for k in due:
                steps[k]()


def fwd_kernel(
    res_ref, x_ref, gain_ref, bias_ref, bp_ref, wq_ref, wk_ref, wv_ref, bq_ref, bk_ref, bv_ref, pw_ref, ln_ref,
    tall_ref, cmp_ref, sel_ref, marks_ref, code_ref, mem_ref, wp_ref, up_any, bu_any, down_any,
    mid_ref, xs_ref, field_ref, xh_ref, q_ref, k_ref, v_ref, p_ref, o_ref, att_ref, up_all, bu_all, down_all,
    send_sem, recv_sem, n_s, fld_s, pool_s, q_s, acc_s,
):
    g, h = pl.program_id(0), pl.program_id(1)
    large = is_large(res_ref)
    core, other = ("tensor", 1), ("tensor", 2)
    shards = ((up_any, up_all), (bu_any, bu_all), (down_any, down_all))

    def share(k, link, to):
        src = shards[k][0] if to < 2 else shards[k][1].at[1]
        return send(src, shards[k][1].at[to], send_sem.at[k, to], recv_sem.at[k, to], link)

    @pl.when((g == 0) & (h == 0))
    def _():
        greet((core, other))
        for k in range(3):
            share(k, other, 1).start()
            share(k, core, 0).start()

    @pl.when((h == PER - 1) & (g == GROUPS - 1))
    def _():
        for k in range(3):
            share(k, other, 1).wait()
            share(k, core, 2).start()


    @pl.when((g == 0) & (h == 0))
    def _():
        for j in range(D // LANES):
            acc_s[j] = x_ref[:, j * LANES : (j + 1) * LANES].astype(F32)

        def body(i, _):
            rows = rows_at(i, BAND)
            x = get_spots(six(acc_s), i)
            mid_ref[rows, :] = x + line(bp_ref)
            xs_ref[rows, :] = x.astype(BF16)
            xh, _ = row_norm(x)
            n_s[rows, :] = (xh * line(gain_ref) + line(bias_ref)).astype(BF16)
            return 0

        lax.fori_loop(0, SIDE, body, 0)
        for a in range(3):
            fld_s[a, 0:SIDE] = jnp.zeros((SIDE, 8, WIDE), F32)
            fld_s[a, SPOTS + SIDE : SPOTS + 2 * SIDE] = jnp.zeros((SIDE, 8, WIDE), F32)

    @pl.when(h == 0)
    def _():
        for p, (w, b) in enumerate(((wq_ref, bq_ref), (wk_ref, bk_ref), (wv_ref, bv_ref))):
            y = nn(n_s[...], w[...]) + b[...]
            field_ref[:, :, p * WIDE : (p + 1) * WIDE] = y.reshape(SPOTS, 8, WIDE)

        def branch(p, _):
            def spread(r, _):
                spots = rows_at(r, SIDE)
                ok = alive(r, large, (BAND, LANES)).reshape(SIDE, 8, LANES)
                there = rows_at(r + 1, SIDE)
                for j in range(3):
                    lanes, own = tile_at(3 * p + j), slice(j * LANES, (j + 1) * LANES)
                    y = field_ref[spots, :, lanes] * ok
                    field_ref[spots, :, lanes] = y
                    fld_s[0, there, :, own] = frame_shift(y, True)
                    fld_s[1, there, :, own] = y
                    fld_s[2, there, :, own] = frame_shift(y, False)
                return 0

            lax.fori_loop(0, SIDE, spread, 0)

            def pool(j, _):
                lanes, own = tile_at(3 * p + j), tile_at(j)
                w = [jnp.broadcast_to(pw_ref[p, t : t + 1, own], (8, LANES)) for t in range(TAPS)]

                def row(r, _):
                    acc = [None] * SIDE
                    for c_in in range(SIDE):
                        for b in range(3):
                            for a in range(3):
                                x = fld_s[a, (r + b) * SIDE + c_in, :, own]
                                for e in range(3):
                                    c = c_in - e + 1
                                    if 0 <= c < SIDE:
                                        term = w[9 * a + 3 * b + e] * x
                                        acc[c] = term if acc[c] is None else acc[c] + term
                    for c in range(SIDE):
                        pool_s[r * SIDE + c, :, lanes] = acc[c]
                    return 0

                lax.fori_loop(0, SIDE, row, 0)
                return 0

            lax.fori_loop(0, 3, pool, 0)
            return 0

        lax.fori_loop(0, 3, branch, 0)
        lane = lane_of((BAND, LANES))

        ones = ones_matrix()

        def norm(r, _):
            spots, rows = rows_at(r, SIDE), rows_at(r, BAND)
            bar = jnp.where(lane == MASK_LANE, NEG, 0.0) * (1.0 - alive(r, large, (BAND, LANES)))
            heads = []
            for p in range(3):
                heads += to_heads([
                    pool_s[spots, :, (3 * p + j) * LANES : (3 * p + j + 1) * LANES].reshape(BAND, LANES)
                    for j in range(3)
                ])
            x = jnp.concatenate(heads)
            c = jnp.where(lane_of(x.shape) < HEAD_DIM, x - fine_mean(x, ones), 0.0)
            rstd_all = lax.rsqrt(lane_mean(c * c, ones) + EPS)
            xh_all = c * rstd_all
            for k in range(3 * PER):
                p, i = k // PER, k % PER
                xh, rstd = xh_all[k * BAND : (k + 1) * BAND], rstd_all[k * BAND : (k + 1) * BAND]
                xh_ref[i, p, rows, :] = jnp.where(lane == HEAD_DIM, rstd, xh)
                y = xh * ln_ref[p : p + 1, :] + ln_ref[3 + p : 4 + p, :]
                if p == 0:
                    q_s[i, rows, :] = y
                elif p == 1:
                    k_ref[i, rows, :] = (y + marks_ref[rows, :] + bar).astype(BF16)
                else:
                    one = (lane == HEAD_DIM) | (lane == HEAD_DIM + 1)
                    v_ref[i, rows, :] = jnp.where(one, 1.0, y).astype(BF16)
            return 0

        lax.fori_loop(0, SIDE, norm, 0)
        code = code_ref[...]
        out = 1.0 - jnp.where(code == 2.0, 1.0, code * large)
        lane_m = lane_of(code.shape)
        for a, ref in enumerate((k_ref, v_ref)):
            tiles = [mem_ref[a, :, j * LANES : (j + 1) * LANES].astype(F32) for j in range(3)]
            for i, m in enumerate(to_heads(tiles)):
                if a == 0:
                    m = jnp.where(lane_m == MASK_LANE, out * NEG, m)
                else:
                    m = jnp.where((lane_m == HEAD_DIM) | (lane_m == HEAD_DIM + 1), 1.0, m)
                ref[i, LENGTH:KEYS, :] = m.astype(BF16)

    q = q_s[h]
    near = (nt(q.astype(BF16), tall_ref[...]) * sel_ref[...]).astype(BF16)
    ext = q * SCALE + nn(near, cmp_ref[...])
    q_ref[h] = jnp.where(lane_of((LENGTH, LANES)) == MASK_LANE, 1.0, ext).astype(BF16)

    lane = lane_of((LENGTH, LANES))
    scores = nt(q_ref[h], k_ref[h])
    e = jnp.exp(scores - jnp.max(scores, axis=-1, keepdims=True)).astype(BF16)
    p_ref[0] = e
    o = nn(e, v_ref[h])
    whole = o[:, HEAD_DIM : HEAD_DIM + 1]
    o = jnp.where(lane < HEAD_DIM, o * (1.0 / whole), 0.0)
    o_ref[0] = jnp.where(lane == HEAD_DIM, whole, o)
    q_s[h] += o

    @pl.when(h == PER - 1)
    def _():
        def join(r, _):
            rows = rows_at(r, BAND)
            for j, t in enumerate(to_dense([q_s[i, rows, :] for i in range(PER)])):
                att_ref[rows, j * LANES : (j + 1) * LANES] = t.astype(BF16)
            return 0

        lax.fori_loop(0, SIDE, join, 0)
        mid_ref[...] += nn(att_ref[...], wp_ref[...])

    @pl.when((h == PER - 1) & (g == GROUPS - 1))
    def _():
        for k in range(3):
            share(k, core, 0).wait()
            share(k, core, 2).wait()


def mlp_kernel(
    res_ref, mid_ref, cot_ref, gain_ref, bias_ref, bd_ref, up_all, bu_all, down_all, up_any, bu_any, down_any,
    out_ref, gm_ref, gml_ref, small_ref, gup_ref, gdown_ref, gfar_ref,
    n_s, nt_s, go_s, y_s, gn_s, wide_s, stage_s, up_s, bu_s, down_s, grad_s, land_s, side_s, load_sem, send_sem, recv_sem,
):
    step = pl.program_id(0)
    large = is_large(res_ref)
    tiles = D // LANES
    cut, half = tiles * D, tiles * D // 2
    core, other, near = ("tensor", 1), ("tensor", 2), ("dp", 1)

    def slice_of(k):
        return (bit_of(*core) + 1 - k % 2) % 2 + 2 * ((bit_of(*other) + 1 - k // 2) % 2)

    def loads(k):
        up, bu, down = (up_any, bu_any, down_any) if k == 3 else [a.at[2 - k] for a in (up_all, bu_all, down_all)]
        pairs = ((up, up_s), (bu, bu_s), (down, down_s))
        return [pltpu.make_async_copy(src, dst.at[k % 2], load_sem.at[n, k]) for n, (src, dst) in enumerate(pairs)]

    def to_core(k):
        return send(grad_s.at[2 * k], land_s.at[k], send_sem.at[k], recv_sem.at[k], core)

    def to_side():
        return send(grad_s.at[1, pl.ds(0, cut)], side_s.at[pl.ds(0, cut)], send_sem.at[2], recv_sem.at[2], other)

    def to_near():
        give = cut + (1 - bit_of(*near)) * half
        return send(grad_s.at[1, some(give, half)], side_s.at[pl.ds(cut, half)], send_sem.at[3], recv_sem.at[3], near)

    @pl.when(step == 0)
    def _():
        for copy in loads(0):
            copy.start()
        greet((core, other, near))

    @pl.when(step == 2)
    def _():
        to_core(0).wait()
        add_rows(grad_s.at[1], 0, land_s.at[0], 0, 2 * cut)
        to_side().start()
        to_near().start()

    for k in range(2):

        @pl.when(step == 2 * k + 1)
        def _():
            to_core(k).start()

    @pl.when(step == 0)
    def _():
        for j in range(D // LANES):
            stage_s[j] = cot_ref[:, j * LANES : (j + 1) * LANES].astype(F32)

        def body(i, sums):
            rows = rows_at(i, BAND)
            xh, _ = row_norm(mid_ref[rows, :])
            n_s[rows, :] = (xh * line(gain_ref) + line(bias_ref)).astype(BF16)
            go = get_spots(six(stage_s), i) * alive(i, large, (BAND, D))
            wide_s[rows, :] = go
            go_s[rows, :] = go.astype(BF16)
            return sums + fold8(go)

        sums = lax.fori_loop(0, SIDE, body, jnp.zeros((8, D), F32))
        put_rows(small_ref, 12, total(sums))
        nt_s[...] = n_s[...].T

    for k in range(4):

        @pl.when(step == k)
        def _():
            if k < 3:
                for copy in loads(k + 1):
                    copy.start()
            for copy in loads(k):
                copy.wait()

    slot = step % 2
    pre = nn(n_s[...], up_s[slot]) + bu_s[slot].astype(F32)[0:1, :]
    cdf = 0.5 * (1.0 + lax.erf(pre * 0.7071067811865476))
    act = (pre * cdf).astype(BF16)
    slope = cdf + pre * jnp.exp(pre * pre * -0.5) * 0.3989422804014327
    ga = nt(go_s[...], down_s[slot])
    gh = ga * slope
    put_rows(small_ref, 24 + slice_of(step) * tiles, total(fold8(gh)))
    ghl = gh.astype(BF16)
    value = tn(act, go_s[...]).astype(BF16)
    for j in range(tiles):
        grad_s[step, cut + j * D : cut + (j + 1) * D, :] = value[:, j * LANES : (j + 1) * LANES]
    value = nn(nt_s[...], ghl).astype(BF16)
    for j in range(tiles):
        grad_s[step, j * D : (j + 1) * D, :] = value[:, j * LANES : (j + 1) * LANES]
    y = nn(act, down_s[slot])
    gn = nt(ghl, up_s[slot])

    @pl.when(step == 0)
    def _():
        y_s[...] = y
        gn_s[...] = gn

    @pl.when(step > 0)
    def _():
        y_s[...] += y
        gn_s[...] += gn

    @pl.when(step == pl.num_programs(0) - 1)
    def _():
        def body(i, sums):
            rows = rows_at(i, BAND)
            mid = mid_ref[rows, :]
            put_spots(six(stage_s), i, (mid + y_s[rows, :] + line(bd_ref)) * alive(i, large, (BAND, D)))
            xh, rstd = row_norm(mid)
            gy = gn_s[rows, :]
            gx = gy * line(gain_ref)
            m1 = jnp.mean(gx, axis=-1, keepdims=True)
            m2 = jnp.mean(gx * xh, axis=-1, keepdims=True)
            gm = wide_s[rows, :] + (gx - m1 - xh * m2) * rstd
            gm_ref[rows, :] = gm
            gml_ref[rows, :] = gm.astype(BF16)
            return sums[0] + fold8(gy * xh), sums[1] + fold8(gy), sums[2] + fold8(gm)

        zero = jnp.zeros((8, D), F32)
        sums = lax.fori_loop(0, SIDE, body, (zero, zero, zero))
        for j in range(D // LANES):
            out_ref[:, j * LANES : (j + 1) * LANES] = stage_s[j].astype(BF16)
        for at, v in zip((0, 6, 18), sums):
            put_rows(small_ref, at, total(v))
        to_core(1).wait()
        add_rows(grad_s.at[3], 0, land_s.at[1], 0, 2 * cut)
        to_side().wait()
        add_rows(grad_s.at[3], 0, side_s, 0, cut)
        to_near().wait()
        keep = cut + bit_of(*near) * half
        add_rows(grad_s.at[1], keep, side_s, cut, half)
        gup_ref[...] = grad_s[3, 0:cut, :]
        gdown_ref[...] = grad_s[3, cut : 2 * cut, :]
        gfar_ref[...] = grad_s[1, some(keep, half), :]


def bwd_kernel(
    order, first_orders, res_ref, x_ref, gain_ref, bias_ref, gm_any, gml_ref, wq_ref, wk_ref, wv_ref, pw_ref, ln_ref,
    tall_ref, cmp_ref, sel_ref, pick_ref, wp_ref, field_ref, xh_ref, q_ref, k_ref, v_ref, p_ref, o_ref, att_ref,
    gup_any, gdown_any, gfar_any,
    gx_ref, small_ref, first_ref, last_ref, gup_out, gdown_out,
    gpw_s, gtall_s, n_s, do_s, ds_s, dpp_s, g_s, gq_s, gin_s,
    up_s, down_s, far_s, up_land, down_land, far_land, first_s, first_land, load_sem, own_sem, send_sem, recv_sem,
):
    g, h = pl.program_id(0), pl.program_id(1)
    large = is_large(res_ref)
    up_steps = chain(up_s, up_land, gup_out, send_sem.at[0], recv_sem.at[0], own_sem.at[0], order)
    side = (far_s, far_land, ("tensor", 2))
    down_steps = chain(down_s, down_land, gdown_out, send_sem.at[1], recv_sem.at[1], own_sem.at[1], order, side)

    share, size = first_s.shape[0] // len(first_orders), first_ref.shape[0] // len(first_orders)
    first_steps = [
        chain(
            first_s.at[pl.ds(c * share, share)], first_land.at[c], None, send_sem.at[2 + c], recv_sem.at[2 + c], None, links
        )
        for c, links in enumerate(first_orders)
    ]

    def store(at, value):
        value = value.astype(BF16)
        for ref, group in ((first_s, 0), (last_ref, 1)):

            @pl.when(g == group)
            def _():
                ref[at : at + value.shape[0], :] = value

    def travel(tick):
        for steps in first_steps:
            at_ticks(tick, FIRST_TICKS, steps)
        at_ticks(tick, UP_TICKS, up_steps)
        at_ticks(tick, DOWN_TICKS, down_steps)

    @pl.when((g == 0) & (h == 0))
    def _():
        loads = [
            pltpu.make_async_copy(src, dst, load_sem.at[k])
            for k, (src, dst) in enumerate(((gup_any, up_s), (gdown_any, down_s), (gfar_any, far_s)))
        ]
        for copy in loads:
            copy.start()
        greet((("tensor", 1), ("tensor", 2), *order))
        for copy in loads:
            copy.wait()

    travel((PER + 3) * g + h)

    @pl.when((g == 0) & (h == 0))
    def _():
        def body(i, _):
            rows = rows_at(i, BAND)
            xh, _ = row_norm(x_ref[rows, :].astype(F32))
            n_s[rows, :] = (xh * line(gain_ref) + line(bias_ref)).astype(BF16)
            return 0

        lax.fori_loop(0, SIDE, body, 0)
        for a in range(3):
            g_s[a, 0:SIDE] = jnp.zeros((SIDE, 8, WIDE), F32)
            g_s[a, SPOTS + SIDE : SPOTS + 2 * SIDE] = jnp.zeros((SIDE, 8, WIDE), F32)
        gtall_s[...] = jnp.zeros(gtall_s.shape, F32)
        small_ref[...] = jnp.zeros(small_ref.shape, F32)
        gpw_s[...] = jnp.zeros(gpw_s.shape, F32)

    @pl.when(h == 0)
    def _():
        gin_s[:, 0:WIDE] = nt(gml_ref[...], wp_ref[...])

        def split(r, _):
            rows = rows_at(r, BAND)
            tiles = [gin_s[rows, j * LANES : (j + 1) * LANES] for j in range(3)]
            for i, t in enumerate(to_heads(tiles)):
                do_s[i, rows, :] = t
            return 0

        lax.fori_loop(0, SIDE, split, 0)
        gw = tn(att_ref[...], gml_ref[...])
        for j in range(D // LANES):
            store(9 * D + j * WIDE, gw[:, j * LANES : (j + 1) * LANES])

    lane = lane_of((LENGTH, LANES))
    do = do_s[h]
    o = o_ref[0]
    inv = 1.0 / o[:, HEAD_DIM : HEAD_DIM + 1]
    ones = ones_matrix()
    delta = nn((do * o).astype(BF16), ones) * inv
    high = delta.astype(BF16).astype(F32)
    doe = jnp.where(lane == HEAD_DIM, -high, jnp.where(lane == HEAD_DIM + 1, high - delta, do * inv)).astype(BF16)
    ds_s[...] = (p_ref[0].astype(F32) * nt(doe, v_ref[0])).astype(BF16)
    dqe = nn(ds_s[...], k_ref[0])
    dk = tn(q_ref[0], ds_s[...]).T[:LENGTH]
    dv = tn(doe, p_ref[0]).T[:LENGTH]
    far = (nt(dqe.astype(BF16), cmp_ref[...]) * sel_ref[...]).astype(BF16)
    xq = xh_ref[0, 0]
    query = (jnp.where(lane < HEAD_DIM, xq, 0.0) * ln_ref[0:1, :] + ln_ref[3:4, :]).astype(BF16)
    gtall_s[...] += tn(far, query)
    dq = dqe * SCALE + do + nn(far, tall_ref[...])
    for p, gy in enumerate((dq, dk, dv)):
        raw = xh_ref[0, p]
        rstd = raw[:, HEAD_DIM : HEAD_DIM + 1]
        gx = gy * ln_ref[p : p + 1, :]
        m1 = lane_mean(gx, ones)
        m2 = lane_mean(gx * raw, ones)
        dpp_s[h, p] = (gx - m1 - raw * m2) * rstd
        small_ref[96 + p : 97 + p, :] += total(fold8(gy * raw))
        small_ref[99 + p : 100 + p, :] += total(fold8(gy))

    @pl.when(h == PER - 1)
    def _():
        def branch(p, _):
            def spread(r, _):
                there, rows = rows_at(r + 1, SIDE), rows_at(r, BAND)
                for j, t in enumerate(to_dense([dpp_s[i, p, rows, :] for i in range(PER)])):
                    lanes = slice(j * LANES, (j + 1) * LANES)
                    t = t.reshape(SIDE, 8, LANES)
                    g_s[0, there, :, lanes] = frame_shift(t, False)
                    g_s[1, there, :, lanes] = t
                    g_s[2, there, :, lanes] = frame_shift(t, True)
                return 0

            lax.fori_loop(0, SIDE, spread, 0)

            def pool(j, _):
                lanes, own = tile_at(3 * p + j), tile_at(j)
                w = [jnp.broadcast_to(pw_ref[p, t : t + 1, own], (8, LANES)) for t in range(TAPS)]

                def row(r, sums):
                    sums = list(sums)
                    x = [field_ref[r * SIDE + c, :, lanes] for c in range(SIDE)]
                    acc = [None] * SIDE
                    for c_in in range(SIDE):
                        for b in range(3):
                            for a in range(3):
                                t = g_s[a, (r + 2 - b) * SIDE + c_in, :, own]
                                for e in range(3):
                                    c, k = c_in + e - 1, 9 * a + 3 * b + e
                                    if 0 <= c < SIDE:
                                        term = w[k] * t
                                        acc[c] = term if acc[c] is None else acc[c] + term
                                        sums[k] = sums[k] + x[c] * t
                    for c in range(SIDE):
                        gin_s[pl.ds(pl.multiple_of(r * BAND + c * 8, 8), 8), lanes] = acc[c]
                    return tuple(sums)

                sums = lax.fori_loop(0, SIDE, row, tuple(jnp.zeros((8, LANES), F32) for _ in range(TAPS)))
                for t in range(TAPS):
                    gpw_s[t : t + 1, own] = total(sums[t])
                return 0

            lax.fori_loop(0, 3, pool, 0)
            travel((PER + 3) * g + PER + p)
            heads = to_heads([gpw_s[:, j * LANES : (j + 1) * LANES] for j in range(3)])
            small_ref[rows_at(p, 32), :] += heads[0] + heads[1] + heads[2] + heads[3]
            return 0

        lax.fori_loop(0, 3, branch, 0)

        def finish(r, sums):
            rows = rows_at(r, BAND)
            t = gin_s[rows, :] * alive(r, large, (BAND, 3 * WIDE))
            gq_s[rows, :] = t.astype(BF16)
            return sums + fold8(t)

        put_rows(small_ref, 168 + 9 * g, total(lax.fori_loop(0, SIDE, finish, jnp.zeros((8, 3 * WIDE), F32))))
        gm_load = pltpu.make_async_copy(gm_any, gin_s.at[:, pl.ds(0, D)], load_sem.at[3])

        @pl.when(g == GROUPS - 1)
        def _():
            gm_load.start()

        gn = None
        for p, w in enumerate((wq_ref, wk_ref, wv_ref)):
            piece = gq_s[:, p * WIDE : (p + 1) * WIDE]
            value = tn(n_s[...], piece)
            for j in range(WIDE // LANES):
                store((3 * p + j) * D, value[:, j * LANES : (j + 1) * LANES])
            term = nt(piece, w[...])
            gn = term if gn is None else gn + term

        @pl.when(g == 0)
        def _():
            gx_ref[...] = gn

        @pl.when(g > 0)
        def _():
            gx_ref[...] += gn

    @pl.when((h == PER - 1) & (g == GROUPS - 1))
    def _():
        pltpu.make_async_copy(gm_any, gin_s.at[:, pl.ds(0, D)], load_sem.at[3]).wait()
        stage = [(dpp_s, (j // 3, j % 3)) for j in range(D // LANES)]

        def body(i, sums):
            rows = rows_at(i, BAND)
            xh, rstd = row_norm(x_ref[rows, :].astype(F32))
            gy = gx_ref[rows, :]
            gx = gy * line(gain_ref)
            m1 = jnp.mean(gx, axis=-1, keepdims=True)
            m2 = jnp.mean(gx * xh, axis=-1, keepdims=True)
            put_spots(stage, i, gin_s[rows, 0:D] + (gx - m1 - xh * m2) * rstd)
            return sums[0] + fold8(gy * xh), sums[1] + fold8(gy)

        zero = jnp.zeros((8, D), F32)
        sums = lax.fori_loop(0, SIDE, body, (zero, zero))
        for j, (ref, at) in enumerate(stage):
            gx_ref[:, j * LANES : (j + 1) * LANES] = ref[at]
        put_rows(small_ref, 186, total(sums[0]))
        put_rows(small_ref, 192, total(sums[1]))
        rest, rel = gtall_s[...], None
        for _ in range(3):
            part = rest.astype(BF16)
            rest = rest - part.astype(F32)
            term = nn(pick_ref[...], part)
            rel = term if rel is None else rel + term
        small_ref[104:168, :] = rel
        travel(2 * (PER + 3))
        for c, links in enumerate(first_orders):
            off, _ = span(share, links, len(links))
            first_ref[c * size : (c + 1) * size, :] = first_s[some(c * share + off, size), :]


def reduce_kernel(parts, first_orders, links, first_any, last_any, one, two, first_out, out, small, *scratch):
    big, land, own_s, small_land, load_sem, send_sem, recv_sem, own_sem, ssend_sem, srecv_sem = scratch
    loads = [
        pltpu.make_async_copy(src, dst, load_sem.at[k]) for k, (src, dst) in enumerate(((last_any, big), (first_any, own_s)))
    ]
    for copy in loads:
        copy.start()
    greet(links)
    small[0 : one.shape[0]] = one[...]
    small[one.shape[0] :] = two[...]
    for copy in loads:
        copy.wait()
    share, size = first_out.shape[0] // len(first_orders), own_s.shape[0] // len(first_orders)
    chains = []
    for i, (first, rows, order) in enumerate(parts):
        here = pl.ds(first, rows)
        chains.append(chain(big.at[here], land.at[i], out.at[here], send_sem.at[i], recv_sem.at[i], own_sem.at[i], order))
    for c, order in enumerate(first_orders):
        i, mine = len(parts) + c, own_s.at[pl.ds(c * size, size)]
        there = first_out.at[pl.ds(c * share, share)]
        chains.append(chain(None, None, there, send_sem.at[i], recv_sem.at[i], own_sem.at[i], order, own=mine))

    def extra(s):
        return send(small, small_land.at[s], ssend_sem.at[s], srecv_sem.at[s], links[s])

    for k in range(max(len(c) for c in chains)):
        for c in chains:
            if k < len(c):
                c[k]()
        if 0 < k <= len(links):
            extra(k - 1).wait()
            small[...] += small_land[k - 1]
        if k < len(links):
            extra(k).start()


def all_reduce(first, last, one, two, links, first_orders):
    small = sds((one.shape[0] + two.shape[0], LANES), F32)
    core, rest, dp = links[:1], links[1:2], links[2:]
    one_way, other_way = core + rest + dp, core + dp[:1] + rest + dp[1:]
    far_ways = [core + dp[1:2] + rest + dp[:1] + dp[2:], core + dp[1:2] + dp[:1] + rest + dp[2:]]
    ways = [one_way, other_way, far_ways[0], one_way, other_way, far_ways[1]]
    at = last.shape[0]
    count = 6 if len(links) <= halvings(at // 6) else 3
    share = at // count
    parts = [(k * share, share, order) for k, order in enumerate(ways[:count])]
    total_chains, stages = count + len(first_orders), 2 * len(links)
    dma = pltpu.SemaphoreType.DMA
    return pl.pallas_call(
        functools.partial(reduce_kernel, parts, first_orders, links),
        in_specs=[pl.BlockSpec(memory_space=pl.ANY)] * 2 + [pl.BlockSpec(memory_space=pltpu.VMEM)] * 2,
        out_specs=[pl.BlockSpec(memory_space=pltpu.VMEM)] * 3,
        out_shape=[sds((at, LANES), BF16), sds((at, LANES), BF16), small],
        scratch_shapes=[
            pltpu.VMEM((at, LANES), BF16),
            pltpu.VMEM((count, landing(share, len(links)), LANES), BF16),
            pltpu.VMEM(first.shape, BF16),
            pltpu.VMEM((len(links), *small.shape), F32),
            dma((2,)),
            dma((total_chains, stages)), dma((total_chains, stages)), dma((total_chains,)),
            dma((len(links),)), dma((len(links),)),
        ],
        compiler_params=pltpu.CompilerParams(
            vmem_limit_bytes=VMEM_LIMIT, collective_id=1, has_side_effects=True
        ),
        name="sum_all",
        cost_estimate=pl.CostEstimate(flops=10_000_000, bytes_accessed=20_000_000, transcendentals=0),
    )(first, last, one, two)


def unpack_kernel(first_ref, last_ref, up_ref, down_ref, small_ref, *outs):
    squares, vectors, gb_ref, gpw_ref, gain_ref, bias_ref, rel_ref = outs[:4], outs[4:11], *outs[11:]
    i = pl.program_id(0)
    for g, ref in enumerate((first_ref, last_ref)):
        for j in range(9):
            to = (j // 3) * D + g * WIDE + j % 3 * LANES
            squares[0][:, to : to + LANES] = ref[j].astype(F32)
        for m in range(3):
            rows = pl.ds(pl.multiple_of(g * WIDE + i % 3 * LANES, LANES), LANES)
            squares[1][rows, tile_at(2 * m + i // 3)] = ref[9 + m].astype(F32)
    for out, ref in ((squares[2], up_ref), (squares[3], down_ref)):
        for j in range(6):
            out[:, j * LANES : (j + 1) * LANES] = ref[j].astype(F32)

    @pl.when(pl.program_id(0) == 0)
    def _():
        own = 232 + 6 * lax.axis_index("tensor")
        for ref, at in zip(vectors, (186, 192, 226, 208, 214, 220, own)):
            for j in range(6):
                ref[j * LANES : (j + 1) * LANES] = small_ref[at + j, :]
        for g in range(GROUPS):
            for j in range(9):
                to = (j // 3) * D + g * WIDE + j % 3 * LANES
                gb_ref[to : to + LANES] = small_ref[168 + 9 * g + j, :]
        for p in range(3):
            gpw_ref[p] = small_ref[32 * p : 32 * p + TAPS, :HEAD_DIM]
        gain_ref[...] = small_ref[96:99, :HEAD_DIM]
        bias_ref[...] = small_ref[99:102, :HEAD_DIM]
        rel_ref[...] = small_ref[104 : 104 + REL_ROWS, :HEAD_DIM]


def unpack(first, last, up, down, small):
    def whole(*shape):
        return pl.BlockSpec(shape, lambda i: (0,) * len(shape))

    def band(width):
        return pl.BlockSpec((LANES, width), lambda i: (i, 0))

    shapes = [(D,)] * 7 + [(3 * D,), (3, TAPS, HEAD_DIM), (3, HEAD_DIM), (3, HEAD_DIM), (REL_ROWS, HEAD_DIM)]
    return pl.pallas_call(
        unpack_kernel,
        grid=(D // LANES,),
        in_specs=[
            *[pl.BlockSpec((n, LANES, LANES), lambda i: (0, i, 0)) for n in (12, 12, 6, 6)], whole(*small.shape),
        ],
        out_specs=[band(3 * D), whole(D, D), band(D), band(D), *[whole(*shape) for shape in shapes]],
        out_shape=[sds((D, 3 * D), F32), *[sds((D, D), F32)] * 3, *[sds(shape, F32) for shape in shapes]],
        name="unpack",
        cost_estimate=pl.CostEstimate(flops=0, bytes_accessed=22_000_000, transcendentals=0),
    )(first, last, up, down, small)


def prepare_kernel(w_ref, gain_ref, bias_ref, rel_ref, pick_ref, bu_ref, bq_in, mem_in, pw_ref, ln_ref, tall_ref, rows_ref, bq_ref, mem_ref, pad_s, rel_s):
    pad_s[...] = jnp.zeros(pad_s.shape, F32)
    for p in range(3):
        pad_s[0:TAPS, 0:HEAD_DIM] = w_ref[p]
        for j, t in enumerate(to_dense([pad_s[...]] * PER)):
            pw_ref[p, :, j * LANES : (j + 1) * LANES] = t
    ln_ref[...] = jnp.zeros(ln_ref.shape, F32)
    ln_ref[0:3, 0:HEAD_DIM] = gain_ref[...]
    ln_ref[3:6, 0:HEAD_DIM] = bias_ref[...]
    rel_s[...] = jnp.zeros(rel_s.shape, F32)
    rel_s[0:REL_ROWS, 0:HEAD_DIM] = rel_ref[...]
    tall_ref[...] = tn(pick_ref[...], rel_s[...].astype(BF16)).astype(BF16)
    rows_ref[...] = jnp.broadcast_to(line(bu_ref).astype(F32), rows_ref.shape).astype(BF16)
    bq_ref[...] = line(bq_in)
    for a in range(2):
        mem = mem_in[a].astype(F32)
        mem_ref[a] = jnp.concatenate([mem, jnp.zeros((KEYS - LENGTH - MEM, D), F32)]).astype(BF16)


def position_tables():
    spot = np.arange(LENGTH) // FRAMES
    frame, row, column = np.arange(LENGTH) % FRAMES, spot // SIDE, spot % SIDE
    kinds = ((frame, FRAMES, 0), (row, SIDE, FRAMES), (column, SIDE, FRAMES + SIDE))
    bases = (FRAMES - 1, 2 * FRAMES - 1 + SIDE - 1, 2 * FRAMES - 1 + 2 * SIDE - 1 + SIDE - 1)
    pick = np.zeros((PAIRS, REL_ROWS), np.float32)
    squeeze = np.zeros((PAIRS, LANES), np.float32)
    select = np.zeros((LENGTH, PAIRS), np.float32)
    marks = np.zeros((LENGTH, LANES), np.float32)
    for tile, ((where, size, first), base) in enumerate(zip(kinds, bases)):
        for at in range(size):
            for m in range(size):
                col = tile * LANES + at * size + m
                pick[col, base + at - m] = 1.0
                squeeze[col, HEAD_DIM + first + m] = 1.0
                select[:, col] = where == at
        marks[np.arange(LENGTH), HEAD_DIM + first + where] = 1.0
    memory_at = np.arange(KEYS - LENGTH) % (MEM // 2)
    half, small = (SIDE + 1) // 2, (SMALL_SIDE + 1) // 2
    memory_inside = (memory_at // half % half < small) & (memory_at % half < small)
    exists = np.arange(KEYS - LENGTH) < MEM
    code = np.where(exists, 1.0 + memory_inside, 0.0).astype(np.float32)
    return pick, squeeze, select, marks, np.repeat(code[:, None], LANES, 1)


def blocked(shape, index, single=False):
    if single:
        return pl.BlockSpec(shape, index, pipeline_mode=pl.Buffered(1))
    return pl.BlockSpec(shape, index)


def const(shape):
    return blocked(shape, lambda *_: (0,) * len(shape), True)


def sds(shape, dtype):
    return jax.ShapeDtypeStruct(shape, dtype)


def per_device(
    inputs, res_ids, memory, gain_one, bias_one, w_qkv, b_qkv, pool_weight, pool_gain, pool_bias, rel_table,
    w_proj, b_proj, gain_two, bias_two, w_up, b_up, w_down, b_down, cotangent,
):
    split = lax.axis_size("tensor")
    pick, squeeze, select, marks, code = position_tables()
    assert split == 4
    pick_rows = jnp.asarray(np.pad(pick.T, ((0, 11), (0, 0))), BF16)
    cmp = jnp.asarray(squeeze, BF16)
    pw, ln, tall, b_rows, bq, mem = pl.pallas_call(
        prepare_kernel,
        out_shape=[
            sds((3, 32, WIDE), F32), sds((8, LANES), F32), sds((PAIRS, LANES), BF16), sds((16, b_up.shape[0]), BF16),
            sds((1, 3 * D), F32), sds((2, KEYS - LENGTH, D), BF16),
        ],
        scratch_shapes=[pltpu.VMEM((32, LANES), F32), pltpu.VMEM((64, LANES), F32)],
        name="prepare",
    )(pool_weight, pool_gain, pool_bias, rel_table, pick_rows, b_up, b_qkv, memory)

    dma = pltpu.SemaphoreType.DMA
    anywhere = pl.BlockSpec(memory_space=pl.ANY)
    w_spec = [blocked((D, WIDE), lambda g, h, p=p: (0, GROUPS * p + g)) for p in range(3)]
    b_spec = [blocked((1, WIDE), lambda g, h, p=p: (0, GROUPS * p + g)) for p in range(3)]

    scalar = pl.BlockSpec(memory_space=pltpu.SMEM)
    row = const((D,))

    def per_group(*shape):
        return blocked(shape, lambda g, h: (g,) + (0,) * (len(shape) - 1))

    def per_head(*shape):
        return blocked(shape, lambda g, h: (PER * g + h,) + (0,) * (len(shape) - 1))

    field_spec = blocked((SPOTS, 8, 3 * WIDE), lambda g, h: (0, 0, g))
    att_spec = blocked((LENGTH, WIDE), lambda g, h: (0, g))
    mid, xs, field, xh, qx, kx, vx, probs, outs, att, up_all, bu_all, down_all = pl.pallas_call(
        fwd_kernel,
        grid=(GROUPS, PER),
        in_specs=[
            scalar, const((LENGTH, D)), row, row, row, *w_spec, *b_spec,
            const((3, 32, WIDE)), const((8, LANES)), const((PAIRS, LANES)), const((PAIRS, LANES)),
            const((LENGTH, PAIRS)), const((LENGTH, LANES)), const((KEYS - LENGTH, LANES)),
            blocked((2, KEYS - LENGTH, WIDE), lambda g, h: (0, 0, g)),
            blocked((WIDE, D), lambda g, h: (g, 0)), anywhere, anywhere, anywhere,
        ],
        out_specs=[
            const((LENGTH, D)), const((LENGTH, D)), field_spec, per_group(PER, 3, LENGTH, LANES), per_group(PER, LENGTH, LANES),
            per_group(PER, KEYS, LANES), per_group(PER, KEYS, LANES), per_head(1, LENGTH, KEYS),
            per_head(1, LENGTH, LANES), att_spec, anywhere, anywhere, anywhere,
        ],
        out_shape=[
            sds((LENGTH, D), F32), sds((LENGTH, D), BF16), sds((SPOTS, 8, 3 * D), F32), sds((HEADS, 3, LENGTH, LANES), F32),
            sds((HEADS, LENGTH, LANES), BF16), sds((HEADS, KEYS, LANES), BF16), sds((HEADS, KEYS, LANES), BF16),
            sds((HEADS, LENGTH, KEYS), BF16), sds((HEADS, LENGTH, LANES), F32), sds((LENGTH, D), BF16),
            *[sds((split - 1, *a.shape), BF16) for a in (w_up, b_rows, w_down)],
        ],
        scratch_shapes=[
            dma((3, 3)), dma((3, 3)),
            pltpu.VMEM((LENGTH, D), BF16),
            pltpu.VMEM((3, SPOTS + 2 * SIDE, 8, WIDE), F32),
            pltpu.VMEM((SPOTS, 8, 3 * WIDE), F32),
            pltpu.VMEM((PER, LENGTH, LANES), F32),
            pltpu.VMEM((D // LANES, LENGTH, LANES), F32),
        ],
        compiler_params=pltpu.CompilerParams(vmem_limit_bytes=VMEM_LIMIT, collective_id=4, has_side_effects=True),
        name="attend",
        cost_estimate=pl.CostEstimate(flops=2 * 3_500_000_000, bytes_accessed=60_000_000, transcendentals=6_500_000),
    )(
        res_ids, inputs, gain_one, bias_one, b_proj, w_qkv, w_qkv, w_qkv, bq, bq, bq, pw, ln,
        tall, cmp, jnp.asarray(select), jnp.asarray(marks), jnp.asarray(code), mem, w_proj, w_up, b_rows, w_down,
    )

    assert w_up.shape[1] == D
    tiles = D // LANES
    cut = tiles * D
    out, gm, gml, small, gup, gdown, gfar = pl.pallas_call(
        mlp_kernel,
        grid=(split,),
        in_specs=[scalar, const((LENGTH, D)), const((LENGTH, D)), row, row, row, *[anywhere] * 6],
        out_specs=[
            const((LENGTH, D)), const((LENGTH, D)), const((LENGTH, D)), const((24 + split * tiles, LANES)),
            const((cut, LANES)), const((cut, LANES)), const((cut // 2, LANES)),
        ],
        out_shape=[
            sds((LENGTH, D), BF16), sds((LENGTH, D), F32), sds((LENGTH, D), BF16), sds((24 + split * tiles, LANES), F32),
            sds((cut, LANES), BF16), sds((cut, LANES), BF16), sds((cut // 2, LANES), BF16),
        ],
        scratch_shapes=[
            pltpu.VMEM((LENGTH, D), BF16),
            pltpu.VMEM((D, LENGTH), BF16),
            pltpu.VMEM((LENGTH, D), BF16),
            *[pltpu.VMEM((LENGTH, D), F32)] * 3,
            pltpu.VMEM((D // LANES, LENGTH, LANES), F32),
            pltpu.VMEM((2, D, D), BF16),
            pltpu.VMEM((2, 16, D), BF16),
            pltpu.VMEM((2, D, D), BF16),
            pltpu.VMEM((split, 2 * cut, LANES), BF16),
            pltpu.VMEM((2, 2 * cut, LANES), BF16),
            pltpu.VMEM((cut + cut // 2, LANES), BF16),
            dma((3, split)), dma((4,)), dma((4,)),
        ],
        compiler_params=pltpu.CompilerParams(vmem_limit_bytes=VMEM_LIMIT, collective_id=2, has_side_effects=True),
        name="mlp",
        cost_estimate=pl.CostEstimate(flops=2 * 11_300_000_000, bytes_accessed=40_000_000, transcendentals=5_000_000),
    )(res_ids, mid, cotangent, gain_two, bias_two, b_down, up_all, bu_all, down_all, w_up, b_rows, w_down)

    links = bits("dp", lax.axis_size("dp"))
    pieces, every = 12 * D, bits("tensor", split) + links
    first_orders = [every, [every[0], links[0], every[1], *links[1:]]]
    share = pieces // len(first_orders)
    kept = len(first_orders) * (share >> min(len(every), halvings(share)))
    gx, small_one, first, last, gup, gdown = pl.pallas_call(
        functools.partial(bwd_kernel, links, first_orders),
        grid=(GROUPS, PER),
        in_specs=[
            scalar, const((LENGTH, D)), row, row, anywhere, const((LENGTH, D)), *w_spec,
            const((3, 32, WIDE)), const((8, LANES)), const((PAIRS, LANES)), const((PAIRS, LANES)),
            const((LENGTH, PAIRS)), const((64, PAIRS)), blocked((WIDE, D), lambda g, h: (g, 0)),
            blocked((SPOTS, 8, 3 * WIDE), lambda g, h: (0, 0, g), True),
            per_head(1, 3, LENGTH, LANES), per_head(1, LENGTH, LANES), per_head(1, KEYS, LANES),
            per_head(1, KEYS, LANES), per_head(1, LENGTH, KEYS), per_head(1, LENGTH, LANES), att_spec,
            anywhere, anywhere, anywhere,
        ],
        out_specs=[
            const((LENGTH, D)), const((208, LANES)),
            const((kept, LANES)), const((pieces, LANES)), anywhere, anywhere,
        ],
        out_shape=[
            sds((LENGTH, D), F32), sds((208, LANES), F32), sds((kept, LANES), BF16), sds((pieces, LANES), BF16),
            sds((cut, LANES), BF16), sds((cut, LANES), BF16),
        ],
        scratch_shapes=[
            pltpu.VMEM((32, WIDE), F32),
            pltpu.VMEM((PAIRS, LANES), F32),
            pltpu.VMEM((LENGTH, D), BF16),
            pltpu.VMEM((PER, LENGTH, LANES), F32),
            pltpu.VMEM((LENGTH, KEYS), BF16),
            pltpu.VMEM((PER, 3, LENGTH, LANES), F32),
            pltpu.VMEM((3, SPOTS + 2 * SIDE, 8, WIDE), F32),
            pltpu.VMEM((LENGTH, 3 * WIDE), BF16),
            pltpu.VMEM((LENGTH, 3 * WIDE), F32),
            pltpu.VMEM((cut, LANES), BF16), pltpu.VMEM((cut, LANES), BF16), pltpu.VMEM((cut // 2, LANES), BF16),
            pltpu.VMEM((cut, LANES), BF16), pltpu.VMEM((cut, LANES), BF16), pltpu.VMEM((cut // 2, LANES), BF16),
            pltpu.VMEM((pieces, LANES), BF16), pltpu.VMEM((len(first_orders), landing(share, len(every)), LANES), BF16),
            dma((4,)), dma((2,)), dma((4, 2 * len(every))), dma((4, 2 * len(every))),
        ],
        compiler_params=pltpu.CompilerParams(vmem_limit_bytes=VMEM_LIMIT, collective_id=3, has_side_effects=True),
        name="attend_back",
        cost_estimate=pl.CostEstimate(flops=2 * 7_000_000_000, bytes_accessed=60_000_000, transcendentals=0),
    )(
        res_ids, xs, gain_one, bias_one, gm, gml, w_qkv, w_qkv, w_qkv, pw, ln, tall, cmp, jnp.asarray(select), pick_rows, w_proj,
        field, xh, qx, kx, vx, probs, outs, att, gup, gdown, gfar,
    )

    first, last, small = all_reduce(first, last, small_one, small, every, first_orders)
    outs = unpack(*[a.reshape(-1, D, LANES) for a in (first, last, gup, gdown)], small)
    squares, (gain1, bias1, bp, gain2, bias2, bd, bu), (gb, gpw, pg, pb, rel) = outs[:4], outs[4:11], outs[11:]

    return (
        out, gx, gain1, bias1, squares[0], gb, gpw, pg, pb, rel, squares[1], bp, gain2, bias2, squares[2], bu, squares[3], bd,
    )


def solution(mesh):
    rows = P(("dp", "tensor"), None)
    return jax.shard_map(
        per_device,
        mesh=mesh,
        in_specs=(
            rows, P(("dp", "tensor")), P(None, ("dp", "tensor"), None), *[P()] * 12,
            P(None, "tensor"), P("tensor"), P("tensor", None), P(), rows,
        ),
        out_specs=(rows, rows, *[P()] * 12, P(None, "tensor"), P("tensor"), P("tensor", None), P()),
        check_vma=False,
    )
```

```python
import functools

import jax
import jax.numpy as jnp
import numpy as np
from jax import lax
from jax.experimental import pallas as pl
from jax.experimental.pallas import tpu as pltpu
from jax.sharding import PartitionSpec as P

D = 768
HEADS = 8
HEAD_DIM = 96
FRAMES = 8
SIDE = 10
SMALL_SIDE = 7
SPOTS = SIDE * SIDE
LENGTH = FRAMES * SPOTS
MEM = 200
KEYS = 1024
OFFSETS = FRAMES + 2 * SIDE
REL_ROWS = 53
GROUPS = 2
PER = HEADS // GROUPS
WIDE = PER * HEAD_DIM
TAPS = 27
LANES = 128
BAND = SIDE * FRAMES
PAIRS = 384
MASK_LANE = HEAD_DIM + OFFSETS
EPS = 1e-6
SCALE = HEAD_DIM**-0.5
F32 = jnp.float32
BF16 = jnp.bfloat16
NEG = -1e30
UP_TICKS = (0, 3, 4, 5, 6, 8, 11)
DOWN_TICKS = (3, 5, 7, 9, 10, 11, 12, 14)
FIRST_TICKS = (7, 9, 11, 12, 13, 14)
VMEM_LIMIT = 60 * 1024 * 1024


def nn(a, b):
    return jnp.dot(a, b, preferred_element_type=F32)


def nt(a, b):
    return lax.dot_general(a, b, (((1,), (1,)), ((), ())), preferred_element_type=F32)


def tn(a, b):
    return lax.dot_general(a, b, (((0,), (0,)), ((), ())), preferred_element_type=F32)


def lane_of(shape):
    return lax.broadcasted_iota(jnp.int32, shape, len(shape) - 1)


def to_heads(tiles):
    t0, t1, t2 = tiles
    lane = lane_of(t0.shape)
    own = lane < HEAD_DIM
    h1 = pltpu.roll(jnp.where(lane >= 96, t0, t1), 32, t0.ndim - 1)
    h2 = pltpu.roll(jnp.where(lane >= 64, t1, t2), 64, t0.ndim - 1)
    h3 = pltpu.roll(t2, 96, t0.ndim - 1)
    return [jnp.where(own, h, 0.0) for h in (t0, h1, h2, h3)]


def to_dense(heads):
    p0, p1, p2, p3 = heads
    lane = lane_of(p0.shape)
    r1 = pltpu.roll(p1, 96, p0.ndim - 1)
    r2 = pltpu.roll(p2, 64, p0.ndim - 1)
    r3 = pltpu.roll(p3, 32, p0.ndim - 1)
    return [jnp.where(lane < 96, p0, r1), jnp.where(lane < 64, r1, r2), jnp.where(lane < 32, r2, r3)]


def row_norm(x):
    mean = jnp.mean(x, axis=-1, keepdims=True)
    c = x - mean
    rstd = lax.rsqrt(jnp.mean(c * c, axis=-1, keepdims=True) + EPS)
    return c * rstd, rstd


def ones_matrix():
    return jnp.where(lax.broadcasted_iota(jnp.int32, (LANES, LANES), 0) < HEAD_DIM, 1.0, 0.0).astype(BF16)


def lane_mean(x, ones):
    return nn(x.astype(BF16), ones) * (1 / HEAD_DIM)


def fine_mean(x, ones):
    high = x.astype(BF16)
    low = (x - high.astype(F32)).astype(BF16)
    return nn(jnp.concatenate([high, low], axis=1), jnp.concatenate([ones, ones])) * (1 / HEAD_DIM)


def frame_shift(x, up):
    frame = lax.broadcasted_iota(jnp.int32, x.shape, 1)
    if up:
        return jnp.where(frame == 0, 0.0, pltpu.roll(x, 1, 1))
    return jnp.where(frame == FRAMES - 1, 0.0, pltpu.roll(x, FRAMES - 1, 1))


def fold8(x):
    return jnp.sum(x.reshape(x.shape[0] // 8, 8, x.shape[1]), axis=0)


def put_rows(ref, at, v):
    for j in range(v.shape[1] // LANES):
        ref[pl.ds(at + j, 1), :] = v[:, j * LANES : (j + 1) * LANES]


def total(x):
    return jnp.sum(x, axis=0, keepdims=True)


def alive(r, large, shape):
    inside = jnp.where(r < SMALL_SIDE, SMALL_SIDE * FRAMES, 0)
    return jnp.where(lax.broadcasted_iota(jnp.int32, shape, 0) < inside, 1.0, large)


def is_large(res_ref):
    return jnp.where(res_ref[0] == 1, 1.0, 0.0).astype(F32)


def put_spots(tiles, r, x):
    for c in range(SIDE):
        for j, (ref, at) in enumerate(tiles):
            to = pl.ds(r * SIDE + c, FRAMES, stride=SPOTS)
            ref[(*at, to, slice(None))] = x[c * FRAMES : (c + 1) * FRAMES, j * LANES : (j + 1) * LANES]


def get_spots(tiles, r):
    rows = [
        jnp.concatenate([ref[(*at, pl.ds(r * SIDE + c, FRAMES, stride=SPOTS), slice(None))] for ref, at in tiles], axis=1)
        for c in range(SIDE)
    ]
    return jnp.concatenate(rows)


def six(ref):
    return [(ref, (j,)) for j in range(D // LANES)]


def line(ref):
    return ref[...].reshape(1, ref.shape[0])


def tile_at(j):
    return pl.ds(pl.multiple_of(j * LANES, LANES), LANES)


def rows_at(r, size):
    if isinstance(r, int):
        return pl.ds(r * size, size)
    return pl.ds(pl.multiple_of(r * size, size), size)


def bit_of(axis, bit):
    return lax.axis_index(axis) // bit % 2


def partner_of(axis, bit):
    me = lax.axis_index(axis)
    return {axis: me + (1 - 2 * (me // bit % 2)) * bit}


def halvings(rows):
    count = 0
    while rows % (32 << count) == 0:
        count += 1
    return count


def bits(axis, size):
    return [(axis, 1 << k) for k in range(size.bit_length() - 1)]


def send(src, dst, one, two, link):
    return pltpu.make_async_remote_copy(
        src_ref=src, dst_ref=dst, send_sem=one, recv_sem=two,
        device_id=partner_of(*link), device_id_type=pl.DeviceIdType.MESH,
    )


def hail(links):
    barrier = pltpu.get_barrier_semaphore()
    for link in links:
        pl.semaphore_signal(barrier, inc=1, device_id=partner_of(*link), device_id_type=pl.DeviceIdType.MESH)


def meet(links):
    pl.semaphore_wait(pltpu.get_barrier_semaphore(), len(links))


def greet(links):
    hail(links)
    meet(links)


def some(start, rows):
    return pl.ds(pl.multiple_of(start, 16), rows)


def add_rows(dst, at, src, start, rows):
    block = next(b for b in (512, 256, 128, 64, 48, 32, 16) if rows % b == 0)

    def add(k, _):
        a, b = some(at + k * block, block), some(start + k * block, block)
        dst[a, :] = (dst[a, :].astype(F32) + src[b, :].astype(F32)).astype(BF16)
        return 0

    lax.fori_loop(0, rows // block, add, 0)


def add_up(dst, *sources):
    block = 256

    def add(k, _):
        parts = [ref[some(at + k * block, block), :].astype(F32) for ref, at in sources]
        dst[some(k * block, block), :] = sum(parts[1:], parts[0]).astype(BF16)
        return 0

    lax.fori_loop(0, dst.shape[0] // block, add, 0)


def span(rows, order, s):
    off, size = 0, rows
    for k in range(min(s, halvings(rows))):
        size //= 2
        off = off + bit_of(*order[k]) * size
    return off, size


def landing(rows, count):
    return rows + max(0, count - halvings(rows) - 1) * (rows >> halvings(rows))


def chain(work, land, out, send_sem, recv_sem, own_sem, order, merge=None, own=None):
    rows = (work if own is None else out).shape[0]
    count = halvings(rows)

    def halve(s, k):
        off, size = span(rows, order, s)
        half, bit, at = size // 2, bit_of(*order[s]), rows - size
        keep, give = off + bit * half, off + (1 - bit) * half
        if s >= count:
            keep, give, half, at = off, off, size, rows - size + (s - count) * size
        copy = send(work.at[some(give, half)], land.at[some(at, half)], send_sem.at[k], recv_sem.at[k], order[s])
        return copy, (work, keep, land, at, half)

    def join(k):
        ref, there, link = merge
        keep = span(rows, order, 1)[0]
        return send(ref, there, send_sem.at[k], recv_sem.at[k], link), (work, keep, there, 0, ref.shape[0])

    def double(s, k):
        off, size = span(rows, order, s + 1)
        here = out.at[some(off, size)]
        return send(here, here, send_sem.at[k], recv_sem.at[k], order[s]), None

    plans = []
    if own is None:
        plans = [functools.partial(halve, s) for s in range(len(order))]
    if merge is not None:
        plans.insert(1, join)
    gather = len(plans)
    if out is not None:
        plans += [functools.partial(double, s) for s in reversed(range(min(len(order), count)))]

    def start(k):
        if k == gather:
            off, size = span(rows, order, len(order))
            mine = work.at[some(off, size)] if own is None else own
            copy = pltpu.make_async_copy(mine, out.at[some(off, size)], own_sem)
            copy.start()
            copy.wait()
        plans[k](k)[0].start()

    def finish(k):
        copy, todo = plans[k](k)
        copy.wait()
        if todo is not None:
            add_rows(*todo)

    def step(k):
        if k > 0:
            finish(k - 1)
        if k < len(plans):
            start(k)

    return [functools.partial(step, k) for k in range(len(plans) + 1)]


def at_ticks(tick, table, steps):
    for n in sorted(set(table)):
        due = [k for k in range(len(steps)) if table[min(k, len(table) - 1)] == n]

        @pl.when(tick == n)
        def _():
            for k in due:
                steps[k]()


def fwd_kernel(
    res_ref, x_ref, gain_ref, bias_ref, bp_ref, wq_ref, wk_ref, wv_ref, bq_ref, bk_ref, bv_ref, pw_ref, ln_ref,
    tall_ref, cmp_ref, sel_ref, marks_ref, code_ref, mem_ref, wp_ref, up_any, bu_any, down_any,
    mid_ref, xs_ref, field_ref, xh_ref, q_ref, k_ref, v_ref, p_ref, o_ref, att_ref, up_all, bu_all, down_all,
    send_sem, recv_sem, n_s, fld_s, pool_s, q_s, acc_s,
):
    g, h = pl.program_id(0), pl.program_id(1)
    large = is_large(res_ref)
    core, other = ("tensor", 1), ("tensor", 2)
    shards = ((up_any, up_all), (bu_any, bu_all), (down_any, down_all))

    def share(k, link, to):
        src = shards[k][0] if to < 2 else shards[k][1].at[1]
        return send(src, shards[k][1].at[to], send_sem.at[k, to], recv_sem.at[k, to], link)

    @pl.when((g == 0) & (h == 0))
    def _():
        greet((core, other))
        for k in range(3):
            share(k, other, 1).start()
            share(k, core, 0).start()

    @pl.when((h == PER - 1) & (g == GROUPS - 1))
    def _():
        for k in range(3):
            share(k, other, 1).wait()
            share(k, core, 2).start()


    @pl.when((g == 0) & (h == 0))
    def _():
        for j in range(D // LANES):
            acc_s[j] = x_ref[:, j * LANES : (j + 1) * LANES].astype(F32)

        def body(i, _):
            rows = rows_at(i, BAND)
            x = get_spots(six(acc_s), i)
            mid_ref[rows, :] = x + line(bp_ref)
            xs_ref[rows, :] = x.astype(BF16)
            xh, _ = row_norm(x)
            n_s[rows, :] = (xh * line(gain_ref) + line(bias_ref)).astype(BF16)
            return 0

        lax.fori_loop(0, SIDE, body, 0)
        for a in range(3):
            fld_s[a, 0:SIDE] = jnp.zeros((SIDE, 8, WIDE), F32)
            fld_s[a, SPOTS + SIDE : SPOTS + 2 * SIDE] = jnp.zeros((SIDE, 8, WIDE), F32)

    @pl.when(h == 0)
    def _():
        for p, (w, b) in enumerate(((wq_ref, bq_ref), (wk_ref, bk_ref), (wv_ref, bv_ref))):
            y = nn(n_s[...], w[...]) + b[...]
            field_ref[:, :, p * WIDE : (p + 1) * WIDE] = y.reshape(SPOTS, 8, WIDE)

        def branch(p, _):
            def spread(r, _):
                spots = rows_at(r, SIDE)
                ok = alive(r, large, (BAND, LANES)).reshape(SIDE, 8, LANES)
                there = rows_at(r + 1, SIDE)
                for j in range(3):
                    lanes, own = tile_at(3 * p + j), slice(j * LANES, (j + 1) * LANES)
                    y = field_ref[spots, :, lanes] * ok
                    field_ref[spots, :, lanes] = y
                    fld_s[0, there, :, own] = frame_shift(y, True)
                    fld_s[1, there, :, own] = y
                    fld_s[2, there, :, own] = frame_shift(y, False)
                return 0

            lax.fori_loop(0, SIDE, spread, 0)

            def pool(j, _):
                lanes, own = tile_at(3 * p + j), tile_at(j)
                w = [jnp.broadcast_to(pw_ref[p, t : t + 1, own], (8, LANES)) for t in range(TAPS)]

                def row(r, _):
                    acc = [None] * SIDE
                    for c_in in range(SIDE):
                        for b in range(3):
                            for a in range(3):
                                x = fld_s[a, (r + b) * SIDE + c_in, :, own]
                                for e in range(3):
                                    c = c_in - e + 1
                                    if 0 <= c < SIDE:
                                        term = w[9 * a + 3 * b + e] * x
                                        acc[c] = term if acc[c] is None else acc[c] + term
                    for c in range(SIDE):
                        pool_s[r * SIDE + c, :, lanes] = acc[c]
                    return 0

                lax.fori_loop(0, SIDE, row, 0)
                return 0

            lax.fori_loop(0, 3, pool, 0)
            return 0

        lax.fori_loop(0, 3, branch, 0)
        lane = lane_of((BAND, LANES))

        ones = ones_matrix()

        def norm(r, _):
            spots, rows = rows_at(r, SIDE), rows_at(r, BAND)
            bar = jnp.where(lane == MASK_LANE, NEG, 0.0) * (1.0 - alive(r, large, (BAND, LANES)))
            heads = []
            for p in range(3):
                heads += to_heads([
                    pool_s[spots, :, (3 * p + j) * LANES : (3 * p + j + 1) * LANES].reshape(BAND, LANES)
                    for j in range(3)
                ])
            x = jnp.concatenate(heads)
            c = jnp.where(lane_of(x.shape) < HEAD_DIM, x - fine_mean(x, ones), 0.0)
            rstd_all = lax.rsqrt(lane_mean(c * c, ones) + EPS)
            xh_all = c * rstd_all
            for k in range(3 * PER):
                p, i = k // PER, k % PER
                xh, rstd = xh_all[k * BAND : (k + 1) * BAND], rstd_all[k * BAND : (k + 1) * BAND]
                xh_ref[i, p, rows, :] = jnp.where(lane == HEAD_DIM, rstd, xh)
                y = xh * ln_ref[p : p + 1, :] + ln_ref[3 + p : 4 + p, :]
                if p == 0:
                    q_s[i, rows, :] = y
                elif p == 1:
                    k_ref[i, rows, :] = (y + marks_ref[rows, :] + bar).astype(BF16)
                else:
                    one = (lane == HEAD_DIM) | (lane == HEAD_DIM + 1)
                    v_ref[i, rows, :] = jnp.where(one, 1.0, y).astype(BF16)
            return 0

        lax.fori_loop(0, SIDE, norm, 0)
        code = code_ref[...]
        out = 1.0 - jnp.where(code == 2.0, 1.0, code * large)
        lane_m = lane_of(code.shape)
        for a, ref in enumerate((k_ref, v_ref)):
            tiles = [mem_ref[a, :, j * LANES : (j + 1) * LANES].astype(F32) for j in range(3)]
            for i, m in enumerate(to_heads(tiles)):
                if a == 0:
                    m = jnp.where(lane_m == MASK_LANE, out * NEG, m)
                else:
                    m = jnp.where((lane_m == HEAD_DIM) | (lane_m == HEAD_DIM + 1), 1.0, m)
                ref[i, LENGTH:KEYS, :] = m.astype(BF16)

    q = q_s[h]
    near = (nt(q.astype(BF16), tall_ref[...]) * sel_ref[...]).astype(BF16)
    ext = q * SCALE + nn(near, cmp_ref[...])
    q_ref[h] = jnp.where(lane_of((LENGTH, LANES)) == MASK_LANE, 1.0, ext).astype(BF16)

    lane = lane_of((LENGTH, LANES))
    scores = nt(q_ref[h], k_ref[h])
    e = jnp.exp(scores - jnp.max(scores, axis=-1, keepdims=True)).astype(BF16)
    p_ref[0] = e
    o = nn(e, v_ref[h])
    whole = o[:, HEAD_DIM : HEAD_DIM + 1]
    o = jnp.where(lane < HEAD_DIM, o * (1.0 / whole), 0.0)
    o_ref[0] = jnp.where(lane == HEAD_DIM, whole, o)
    q_s[h] += o

    @pl.when(h == PER - 1)
    def _():
        def join(r, _):
            rows = rows_at(r, BAND)
            for j, t in enumerate(to_dense([q_s[i, rows, :] for i in range(PER)])):
                att_ref[rows, j * LANES : (j + 1) * LANES] = t.astype(BF16)
            return 0

        lax.fori_loop(0, SIDE, join, 0)
        mid_ref[...] += nn(att_ref[...], wp_ref[...])

    @pl.when((h == PER - 1) & (g == GROUPS - 1))
    def _():
        for k in range(3):
            share(k, core, 0).wait()
            share(k, core, 2).wait()


def mlp_kernel(
    res_ref, mid_ref, cot_ref, gain_ref, bias_ref, bd_ref, up_all, bu_all, down_all, up_any, bu_any, down_any,
    out_ref, gm_ref, gml_ref, small_ref, gup_ref, gdown_ref, gfar_ref,
    n_s, nt_s, go_s, y_s, gn_s, wide_s, stage_s, up_s, bu_s, down_s, grad_s, land_s, side_s, load_sem, send_sem, recv_sem,
):
    step = pl.program_id(0)
    large = is_large(res_ref)
    tiles = D // LANES
    cut, half = tiles * D, tiles * D // 2
    core, other, near = ("tensor", 1), ("tensor", 2), ("dp", 1)

    def slice_of(k):
        return (bit_of(*core) + 1 - k % 2) % 2 + 2 * ((bit_of(*other) + 1 - k // 2) % 2)

    def loads(k):
        up, bu, down = (up_any, bu_any, down_any) if k == 3 else [a.at[2 - k] for a in (up_all, bu_all, down_all)]
        pairs = ((up, up_s), (bu, bu_s), (down, down_s))
        return [pltpu.make_async_copy(src, dst.at[k % 2], load_sem.at[n, k]) for n, (src, dst) in enumerate(pairs)]

    def to_core(k):
        return send(grad_s.at[2 * k], land_s.at[k], send_sem.at[k], recv_sem.at[k], core)

    def to_side():
        return send(grad_s.at[1, pl.ds(0, cut)], side_s.at[pl.ds(0, cut)], send_sem.at[2], recv_sem.at[2], other)

    def to_near():
        give = cut + (1 - bit_of(*near)) * half
        return send(grad_s.at[1, some(give, half)], side_s.at[pl.ds(cut, half)], send_sem.at[3], recv_sem.at[3], near)

    @pl.when(step == 0)
    def _():
        for copy in loads(0):
            copy.start()
        hail((core, other, near))

    for k in range(2):

        @pl.when(step == 2 * k + 1)
        def _():
            if k == 0:
                meet((core, other, near))
            to_core(k).start()

    @pl.when(step == 2)
    def _():
        to_core(0).wait()
        add_rows(grad_s.at[1], 0, land_s.at[0], 0, 2 * cut)
        to_side().start()
        to_near().start()

    @pl.when(step == 0)
    def _():
        for j in range(D // LANES):
            stage_s[j] = cot_ref[:, j * LANES : (j + 1) * LANES].astype(F32)

        def body(i, sums):
            rows = rows_at(i, BAND)
            xh, _ = row_norm(mid_ref[rows, :])
            n_s[rows, :] = (xh * line(gain_ref) + line(bias_ref)).astype(BF16)
            go = get_spots(six(stage_s), i) * alive(i, large, (BAND, D))
            wide_s[rows, :] = go
            go_s[rows, :] = go.astype(BF16)
            return sums + fold8(go)

        sums = lax.fori_loop(0, SIDE, body, jnp.zeros((8, D), F32))
        put_rows(small_ref, 12, total(sums))
        nt_s[...] = n_s[...].T

    for k in range(4):

        @pl.when(step == k)
        def _():
            if k < 3:
                for copy in loads(k + 1):
                    copy.start()
            for copy in loads(k):
                copy.wait()

    slot = step % 2
    pre = nn(n_s[...], up_s[slot]) + bu_s[slot].astype(F32)[0:1, :]
    cdf = 0.5 * (1.0 + lax.erf(pre * 0.7071067811865476))
    act = (pre * cdf).astype(BF16)
    slope = cdf + pre * jnp.exp(pre * pre * -0.5) * 0.3989422804014327
    ga = nt(go_s[...], down_s[slot])
    gh = ga * slope
    put_rows(small_ref, 24 + slice_of(step) * tiles, total(fold8(gh)))
    ghl = gh.astype(BF16)
    value = tn(act, go_s[...]).astype(BF16)
    for j in range(tiles):
        grad_s[step, cut + j * D : cut + (j + 1) * D, :] = value[:, j * LANES : (j + 1) * LANES]
    value = nn(nt_s[...], ghl).astype(BF16)
    for j in range(tiles):
        grad_s[step, j * D : (j + 1) * D, :] = value[:, j * LANES : (j + 1) * LANES]
    y = nn(act, down_s[slot])
    gn = nt(ghl, up_s[slot])

    @pl.when(step == 0)
    def _():
        y_s[...] = y
        gn_s[...] = gn

    @pl.when(step > 0)
    def _():
        y_s[...] += y
        gn_s[...] += gn

    @pl.when(step == pl.num_programs(0) - 1)
    def _():
        def body(i, sums):
            rows = rows_at(i, BAND)
            mid = mid_ref[rows, :]
            put_spots(six(stage_s), i, (mid + y_s[rows, :] + line(bd_ref)) * alive(i, large, (BAND, D)))
            xh, rstd = row_norm(mid)
            gy = gn_s[rows, :]
            gx = gy * line(gain_ref)
            m1 = jnp.mean(gx, axis=-1, keepdims=True)
            m2 = jnp.mean(gx * xh, axis=-1, keepdims=True)
            gm = wide_s[rows, :] + (gx - m1 - xh * m2) * rstd
            gm_ref[rows, :] = gm
            gml_ref[rows, :] = gm.astype(BF16)
            return sums[0] + fold8(gy * xh), sums[1] + fold8(gy), sums[2] + fold8(gm)

        zero = jnp.zeros((8, D), F32)
        sums = lax.fori_loop(0, SIDE, body, (zero, zero, zero))
        for j in range(D // LANES):
            out_ref[:, j * LANES : (j + 1) * LANES] = stage_s[j].astype(BF16)
        for at, v in zip((0, 6, 18), sums):
            put_rows(small_ref, at, total(v))
        to_core(1).wait()
        to_side().wait()
        to_near().wait()
        keep = cut + bit_of(*near) * half
        far, own = grad_s.at[1], grad_s.at[3]
        add_up(gup_ref, (own, 0), (land_s.at[1], 0), (side_s, 0))
        add_up(gdown_ref, (own, cut), (land_s.at[1], cut))
        add_up(gfar_ref, (far, keep), (side_s, cut))


def bwd_kernel(
    order, first_orders, res_ref, x_ref, gain_ref, bias_ref, gm_any, gml_ref, wq_ref, wk_ref, wv_ref, pw_ref, ln_ref,
    tall_ref, cmp_ref, sel_ref, pick_ref, wp_ref, field_ref, xh_ref, q_ref, k_ref, v_ref, p_ref, o_ref, att_ref,
    gup_any, gdown_any, gfar_any,
    gx_ref, small_ref, first_ref, last_ref, gup_out, gdown_out,
    gpw_s, gtall_s, n_s, do_s, ds_s, dpp_s, g_s, gq_s, gin_s,
    up_s, down_s, far_s, up_land, down_land, far_land, first_s, first_land, load_sem, own_sem, send_sem, recv_sem,
):
    g, h = pl.program_id(0), pl.program_id(1)
    large = is_large(res_ref)
    up_steps = chain(up_s, up_land, gup_out, send_sem.at[0], recv_sem.at[0], own_sem.at[0], order)
    side = (far_s, far_land, ("tensor", 2))
    down_steps = chain(down_s, down_land, gdown_out, send_sem.at[1], recv_sem.at[1], own_sem.at[1], order, side)

    share, size = first_s.shape[0] // len(first_orders), first_ref.shape[0] // len(first_orders)
    first_steps = [
        chain(
            first_s.at[pl.ds(c * share, share)], first_land.at[c], None, send_sem.at[2 + c], recv_sem.at[2 + c], None, links
        )
        for c, links in enumerate(first_orders)
    ]

    def store(at, value):
        value = value.astype(BF16)
        for ref, group in ((first_s, 0), (last_ref, 1)):

            @pl.when(g == group)
            def _():
                ref[at : at + value.shape[0], :] = value

    def travel(tick):
        for steps in first_steps:
            at_ticks(tick, FIRST_TICKS, steps)
        at_ticks(tick, UP_TICKS, up_steps)
        at_ticks(tick, DOWN_TICKS, down_steps)

    loads = [
        pltpu.make_async_copy(src, dst, load_sem.at[k])
        for k, (src, dst) in enumerate(((gup_any, up_s), (gdown_any, down_s), (gfar_any, far_s)))
    ]

    @pl.when((g == 0) & (h == 0))
    def _():
        for copy in loads:
            copy.start()
        hail((("tensor", 1), ("tensor", 2), *order))


    @pl.when((g == 0) & (h == 0))
    def _():
        def body(i, _):
            rows = rows_at(i, BAND)
            xh, _ = row_norm(x_ref[rows, :].astype(F32))
            n_s[rows, :] = (xh * line(gain_ref) + line(bias_ref)).astype(BF16)
            return 0

        lax.fori_loop(0, SIDE, body, 0)
        for a in range(3):
            g_s[a, 0:SIDE] = jnp.zeros((SIDE, 8, WIDE), F32)
            g_s[a, SPOTS + SIDE : SPOTS + 2 * SIDE] = jnp.zeros((SIDE, 8, WIDE), F32)
        gtall_s[...] = jnp.zeros(gtall_s.shape, F32)
        small_ref[...] = jnp.zeros(small_ref.shape, F32)
        gpw_s[...] = jnp.zeros(gpw_s.shape, F32)

    @pl.when((g == 0) & (h == 0))
    def _():
        meet((("tensor", 1), ("tensor", 2), *order))
        for copy in loads:
            copy.wait()

    travel((PER + 3) * g + h)

    @pl.when(h == 0)
    def _():
        gin_s[:, 0:WIDE] = nt(gml_ref[...], wp_ref[...])

        def split(r, _):
            rows = rows_at(r, BAND)
            tiles = [gin_s[rows, j * LANES : (j + 1) * LANES] for j in range(3)]
            for i, t in enumerate(to_heads(tiles)):
                do_s[i, rows, :] = t
            return 0

        lax.fori_loop(0, SIDE, split, 0)
        gw = tn(att_ref[...], gml_ref[...])
        for j in range(D // LANES):
            store(9 * D + j * WIDE, gw[:, j * LANES : (j + 1) * LANES])

    lane = lane_of((LENGTH, LANES))
    do = do_s[h]
    o = o_ref[0]
    inv = 1.0 / o[:, HEAD_DIM : HEAD_DIM + 1]
    ones = ones_matrix()
    delta = nn((do * o).astype(BF16), ones) * inv
    high = delta.astype(BF16).astype(F32)
    doe = jnp.where(lane == HEAD_DIM, -high, jnp.where(lane == HEAD_DIM + 1, high - delta, do * inv)).astype(BF16)
    ds_s[...] = (p_ref[0].astype(F32) * nt(doe, v_ref[0])).astype(BF16)
    dqe = nn(ds_s[...], k_ref[0])
    dk = tn(q_ref[0], ds_s[...]).T[:LENGTH]
    dv = tn(doe, p_ref[0]).T[:LENGTH]
    far = (nt(dqe.astype(BF16), cmp_ref[...]) * sel_ref[...]).astype(BF16)
    xq = xh_ref[0, 0]
    query = (jnp.where(lane < HEAD_DIM, xq, 0.0) * ln_ref[0:1, :] + ln_ref[3:4, :]).astype(BF16)
    gtall_s[...] += tn(far, query)
    dq = dqe * SCALE + do + nn(far, tall_ref[...])
    for p, gy in enumerate((dq, dk, dv)):
        raw = xh_ref[0, p]
        rstd = raw[:, HEAD_DIM : HEAD_DIM + 1]
        gx = gy * ln_ref[p : p + 1, :]
        m1 = lane_mean(gx, ones)
        m2 = lane_mean(gx * raw, ones)
        dpp_s[h, p] = (gx - m1 - raw * m2) * rstd
        small_ref[96 + p : 97 + p, :] += total(fold8(gy * raw))
        small_ref[99 + p : 100 + p, :] += total(fold8(gy))

    @pl.when(h == PER - 1)
    def _():
        def branch(p, _):
            def spread(r, _):
                there, rows = rows_at(r + 1, SIDE), rows_at(r, BAND)
                for j, t in enumerate(to_dense([dpp_s[i, p, rows, :] for i in range(PER)])):
                    lanes = slice(j * LANES, (j + 1) * LANES)
                    t = t.reshape(SIDE, 8, LANES)
                    g_s[0, there, :, lanes] = frame_shift(t, False)
                    g_s[1, there, :, lanes] = t
                    g_s[2, there, :, lanes] = frame_shift(t, True)
                return 0

            lax.fori_loop(0, SIDE, spread, 0)

            def pool(j, _):
                lanes, own = tile_at(3 * p + j), tile_at(j)
                w = [jnp.broadcast_to(pw_ref[p, t : t + 1, own], (8, LANES)) for t in range(TAPS)]

                def row(r, sums):
                    sums = list(sums)
                    x = [field_ref[r * SIDE + c, :, lanes] for c in range(SIDE)]
                    acc = [None] * SIDE
                    for c_in in range(SIDE):
                        for b in range(3):
                            for a in range(3):
                                t = g_s[a, (r + 2 - b) * SIDE + c_in, :, own]
                                for e in range(3):
                                    c, k = c_in + e - 1, 9 * a + 3 * b + e
                                    if 0 <= c < SIDE:
                                        term = w[k] * t
                                        acc[c] = term if acc[c] is None else acc[c] + term
                                        sums[k] = sums[k] + x[c] * t
                    for c in range(SIDE):
                        gin_s[pl.ds(pl.multiple_of(r * BAND + c * 8, 8), 8), lanes] = acc[c]
                    return tuple(sums)

                sums = lax.fori_loop(0, SIDE, row, tuple(jnp.zeros((8, LANES), F32) for _ in range(TAPS)))
                for t in range(TAPS):
                    gpw_s[t : t + 1, own] = total(sums[t])
                return 0

            lax.fori_loop(0, 3, pool, 0)
            travel((PER + 3) * g + PER + p)
            heads = to_heads([gpw_s[:, j * LANES : (j + 1) * LANES] for j in range(3)])
            small_ref[rows_at(p, 32), :] += heads[0] + heads[1] + heads[2] + heads[3]
            return 0

        lax.fori_loop(0, 3, branch, 0)

        def finish(r, sums):
            rows = rows_at(r, BAND)
            t = gin_s[rows, :] * alive(r, large, (BAND, 3 * WIDE))
            gq_s[rows, :] = t.astype(BF16)
            return sums + fold8(t)

        put_rows(small_ref, 168 + 9 * g, total(lax.fori_loop(0, SIDE, finish, jnp.zeros((8, 3 * WIDE), F32))))
        gm_load = pltpu.make_async_copy(gm_any, gin_s.at[:, pl.ds(0, D)], load_sem.at[3])

        @pl.when(g == GROUPS - 1)
        def _():
            gm_load.start()

        gn = None
        for p, w in enumerate((wq_ref, wk_ref, wv_ref)):
            piece = gq_s[:, p * WIDE : (p + 1) * WIDE]
            value = tn(n_s[...], piece)
            for j in range(WIDE // LANES):
                store((3 * p + j) * D, value[:, j * LANES : (j + 1) * LANES])
            term = nt(piece, w[...])
            gn = term if gn is None else gn + term

        @pl.when(g == 0)
        def _():
            gx_ref[...] = gn

        @pl.when(g > 0)
        def _():
            gx_ref[...] += gn

    @pl.when((h == PER - 1) & (g == GROUPS - 1))
    def _():
        pltpu.make_async_copy(gm_any, gin_s.at[:, pl.ds(0, D)], load_sem.at[3]).wait()
        stage = [(dpp_s, (j // 3, j % 3)) for j in range(D // LANES)]

        def body(i, sums):
            rows = rows_at(i, BAND)
            xh, rstd = row_norm(x_ref[rows, :].astype(F32))
            gy = gx_ref[rows, :]
            gx = gy * line(gain_ref)
            m1 = jnp.mean(gx, axis=-1, keepdims=True)
            m2 = jnp.mean(gx * xh, axis=-1, keepdims=True)
            put_spots(stage, i, gin_s[rows, 0:D] + (gx - m1 - xh * m2) * rstd)
            return sums[0] + fold8(gy * xh), sums[1] + fold8(gy)

        zero = jnp.zeros((8, D), F32)
        sums = lax.fori_loop(0, SIDE, body, (zero, zero))
        for j, (ref, at) in enumerate(stage):
            gx_ref[:, j * LANES : (j + 1) * LANES] = ref[at]
        put_rows(small_ref, 186, total(sums[0]))
        put_rows(small_ref, 192, total(sums[1]))
        rest, rel = gtall_s[...], None
        for _ in range(3):
            part = rest.astype(BF16)
            rest = rest - part.astype(F32)
            term = nn(pick_ref[...], part)
            rel = term if rel is None else rel + term
        small_ref[104:168, :] = rel
        travel(2 * (PER + 3))
        for c, links in enumerate(first_orders):
            off, _ = span(share, links, len(links))
            first_ref[c * size : (c + 1) * size, :] = first_s[some(c * share + off, size), :]


def reduce_kernel(parts, first_orders, links, first_any, last_any, one, two, first_out, out, small, *scratch):
    big, land, own_s, small_land, load_sem, send_sem, recv_sem, own_sem, ssend_sem, srecv_sem = scratch
    loads = [
        pltpu.make_async_copy(src, dst, load_sem.at[k]) for k, (src, dst) in enumerate(((last_any, big), (first_any, own_s)))
    ]
    for copy in loads:
        copy.start()
    greet(links)
    small[0 : one.shape[0]] = one[...]
    small[one.shape[0] :] = two[...]
    for copy in loads:
        copy.wait()
    share, size = first_out.shape[0] // len(first_orders), own_s.shape[0] // len(first_orders)
    chains = []
    for i, (first, rows, order) in enumerate(parts):
        here = pl.ds(first, rows)
        chains.append(chain(big.at[here], land.at[i], out.at[here], send_sem.at[i], recv_sem.at[i], own_sem.at[i], order))
    for c, order in enumerate(first_orders):
        i, mine = len(parts) + c, own_s.at[pl.ds(c * size, size)]
        there = first_out.at[pl.ds(c * share, share)]
        chains.append(chain(None, None, there, send_sem.at[i], recv_sem.at[i], own_sem.at[i], order, own=mine))

    def extra(s):
        return send(small, small_land.at[s], ssend_sem.at[s], srecv_sem.at[s], links[s])

    for k in range(max(len(c) for c in chains)):
        for c in chains:
            if k < len(c):
                c[k]()
        if 0 < k <= len(links):
            extra(k - 1).wait()
            small[...] += small_land[k - 1]
        if k < len(links):
            extra(k).start()


def all_reduce(first, last, one, two, links, first_orders):
    small = sds((one.shape[0] + two.shape[0], LANES), F32)
    core, rest, dp = links[:1], links[1:2], links[2:]
    one_way, other_way = core + rest + dp, core + dp[:1] + rest + dp[1:]
    far_ways = [core + dp[1:2] + rest + dp[:1] + dp[2:], core + dp[1:2] + dp[:1] + rest + dp[2:]]
    ways = [one_way, other_way, far_ways[0], one_way, other_way, far_ways[1]]
    at = last.shape[0]
    count = 6 if len(links) <= halvings(at // 6) else 3
    share = at // count
    parts = [(k * share, share, order) for k, order in enumerate(ways[:count])]
    total_chains, stages = count + len(first_orders), 2 * len(links)
    dma = pltpu.SemaphoreType.DMA
    return pl.pallas_call(
        functools.partial(reduce_kernel, parts, first_orders, links),
        in_specs=[pl.BlockSpec(memory_space=pl.ANY)] * 2 + [pl.BlockSpec(memory_space=pltpu.VMEM)] * 2,
        out_specs=[pl.BlockSpec(memory_space=pltpu.VMEM)] * 3,
        out_shape=[sds((at, LANES), BF16), sds((at, LANES), BF16), small],
        scratch_shapes=[
            pltpu.VMEM((at, LANES), BF16),
            pltpu.VMEM((count, landing(share, len(links)), LANES), BF16),
            pltpu.VMEM(first.shape, BF16),
            pltpu.VMEM((len(links), *small.shape), F32),
            dma((2,)),
            dma((total_chains, stages)), dma((total_chains, stages)), dma((total_chains,)),
            dma((len(links),)), dma((len(links),)),
        ],
        compiler_params=pltpu.CompilerParams(
            vmem_limit_bytes=VMEM_LIMIT, collective_id=1, has_side_effects=True
        ),
        name="sum_all",
        cost_estimate=pl.CostEstimate(flops=10_000_000, bytes_accessed=20_000_000, transcendentals=0),
    )(first, last, one, two)


def unpack_kernel(first_ref, last_ref, up_ref, down_ref, small_ref, *outs):
    squares, vectors, gb_ref, gpw_ref, gain_ref, bias_ref, rel_ref = outs[:4], outs[4:11], *outs[11:]
    i = pl.program_id(0)
    for g, ref in enumerate((first_ref, last_ref)):
        for j in range(9):
            to = (j // 3) * D + g * WIDE + j % 3 * LANES
            squares[0][:, to : to + LANES] = ref[j].astype(F32)
        for m in range(3):
            rows = pl.ds(pl.multiple_of(g * WIDE + i % 3 * LANES, LANES), LANES)
            squares[1][rows, tile_at(2 * m + i // 3)] = ref[9 + m].astype(F32)
    for out, ref in ((squares[2], up_ref), (squares[3], down_ref)):
        for j in range(6):
            out[:, j * LANES : (j + 1) * LANES] = ref[j].astype(F32)

    @pl.when(pl.program_id(0) == 0)
    def _():
        own = 232 + 6 * lax.axis_index("tensor")
        for ref, at in zip(vectors, (186, 192, 226, 208, 214, 220, own)):
            for j in range(6):
                ref[j * LANES : (j + 1) * LANES] = small_ref[at + j, :]
        for g in range(GROUPS):
            for j in range(9):
                to = (j // 3) * D + g * WIDE + j % 3 * LANES
                gb_ref[to : to + LANES] = small_ref[168 + 9 * g + j, :]
        for p in range(3):
            gpw_ref[p] = small_ref[32 * p : 32 * p + TAPS, :HEAD_DIM]
        gain_ref[...] = small_ref[96:99, :HEAD_DIM]
        bias_ref[...] = small_ref[99:102, :HEAD_DIM]
        rel_ref[...] = small_ref[104 : 104 + REL_ROWS, :HEAD_DIM]


def unpack(first, last, up, down, small):
    def whole(*shape):
        return pl.BlockSpec(shape, lambda i: (0,) * len(shape))

    def band(width):
        return pl.BlockSpec((LANES, width), lambda i: (i, 0))

    shapes = [(D,)] * 7 + [(3 * D,), (3, TAPS, HEAD_DIM), (3, HEAD_DIM), (3, HEAD_DIM), (REL_ROWS, HEAD_DIM)]
    return pl.pallas_call(
        unpack_kernel,
        grid=(D // LANES,),
        in_specs=[
            *[pl.BlockSpec((n, LANES, LANES), lambda i: (0, i, 0)) for n in (12, 12, 6, 6)], whole(*small.shape),
        ],
        out_specs=[band(3 * D), whole(D, D), band(D), band(D), *[whole(*shape) for shape in shapes]],
        out_shape=[sds((D, 3 * D), F32), *[sds((D, D), F32)] * 3, *[sds(shape, F32) for shape in shapes]],
        name="unpack",
        cost_estimate=pl.CostEstimate(flops=0, bytes_accessed=22_000_000, transcendentals=0),
    )(first, last, up, down, small)


def prepare_kernel(w_ref, gain_ref, bias_ref, rel_ref, pick_ref, bu_ref, bq_in, mem_in, pw_ref, ln_ref, tall_ref, rows_ref, bq_ref, mem_ref, pad_s, rel_s):
    pad_s[...] = jnp.zeros(pad_s.shape, F32)
    for p in range(3):
        pad_s[0:TAPS, 0:HEAD_DIM] = w_ref[p]
        for j, t in enumerate(to_dense([pad_s[...]] * PER)):
            pw_ref[p, :, j * LANES : (j + 1) * LANES] = t
    ln_ref[...] = jnp.zeros(ln_ref.shape, F32)
    ln_ref[0:3, 0:HEAD_DIM] = gain_ref[...]
    ln_ref[3:6, 0:HEAD_DIM] = bias_ref[...]
    rel_s[...] = jnp.zeros(rel_s.shape, F32)
    rel_s[0:REL_ROWS, 0:HEAD_DIM] = rel_ref[...]
    tall_ref[...] = tn(pick_ref[...], rel_s[...].astype(BF16)).astype(BF16)
    rows_ref[...] = jnp.broadcast_to(line(bu_ref).astype(F32), rows_ref.shape).astype(BF16)
    bq_ref[...] = line(bq_in)
    for a in range(2):
        mem = mem_in[a].astype(F32)
        mem_ref[a] = jnp.concatenate([mem, jnp.zeros((KEYS - LENGTH - MEM, D), F32)]).astype(BF16)


def position_tables():
    spot = np.arange(LENGTH) // FRAMES
    frame, row, column = np.arange(LENGTH) % FRAMES, spot // SIDE, spot % SIDE
    kinds = ((frame, FRAMES, 0), (row, SIDE, FRAMES), (column, SIDE, FRAMES + SIDE))
    bases = (FRAMES - 1, 2 * FRAMES - 1 + SIDE - 1, 2 * FRAMES - 1 + 2 * SIDE - 1 + SIDE - 1)
    pick = np.zeros((PAIRS, REL_ROWS), np.float32)
    squeeze = np.zeros((PAIRS, LANES), np.float32)
    select = np.zeros((LENGTH, PAIRS), np.float32)
    marks = np.zeros((LENGTH, LANES), np.float32)
    for tile, ((where, size, first), base) in enumerate(zip(kinds, bases)):
        for at in range(size):
            for m in range(size):
                col = tile * LANES + at * size + m
                pick[col, base + at - m] = 1.0
                squeeze[col, HEAD_DIM + first + m] = 1.0
                select[:, col] = where == at
        marks[np.arange(LENGTH), HEAD_DIM + first + where] = 1.0
    memory_at = np.arange(KEYS - LENGTH) % (MEM // 2)
    half, small = (SIDE + 1) // 2, (SMALL_SIDE + 1) // 2
    memory_inside = (memory_at // half % half < small) & (memory_at % half < small)
    exists = np.arange(KEYS - LENGTH) < MEM
    code = np.where(exists, 1.0 + memory_inside, 0.0).astype(np.float32)
    return pick, squeeze, select, marks, np.repeat(code[:, None], LANES, 1)


def blocked(shape, index, single=False):
    if single:
        return pl.BlockSpec(shape, index, pipeline_mode=pl.Buffered(1))
    return pl.BlockSpec(shape, index)


def const(shape):
    return blocked(shape, lambda *_: (0,) * len(shape), True)


def sds(shape, dtype):
    return jax.ShapeDtypeStruct(shape, dtype)


def per_device(
    inputs, res_ids, memory, gain_one, bias_one, w_qkv, b_qkv, pool_weight, pool_gain, pool_bias, rel_table,
    w_proj, b_proj, gain_two, bias_two, w_up, b_up, w_down, b_down, cotangent,
):
    split = lax.axis_size("tensor")
    pick, squeeze, select, marks, code = position_tables()
    assert split == 4
    pick_rows = jnp.asarray(np.pad(pick.T, ((0, 11), (0, 0))), BF16)
    cmp = jnp.asarray(squeeze, BF16)
    pw, ln, tall, b_rows, bq, mem = pl.pallas_call(
        prepare_kernel,
        out_shape=[
            sds((3, 32, WIDE), F32), sds((8, LANES), F32), sds((PAIRS, LANES), BF16), sds((16, b_up.shape[0]), BF16),
            sds((1, 3 * D), F32), sds((2, KEYS - LENGTH, D), BF16),
        ],
        scratch_shapes=[pltpu.VMEM((32, LANES), F32), pltpu.VMEM((64, LANES), F32)],
        name="prepare",
    )(pool_weight, pool_gain, pool_bias, rel_table, pick_rows, b_up, b_qkv, memory)

    dma = pltpu.SemaphoreType.DMA
    anywhere = pl.BlockSpec(memory_space=pl.ANY)
    w_spec = [blocked((D, WIDE), lambda g, h, p=p: (0, GROUPS * p + g)) for p in range(3)]
    b_spec = [blocked((1, WIDE), lambda g, h, p=p: (0, GROUPS * p + g)) for p in range(3)]

    scalar = pl.BlockSpec(memory_space=pltpu.SMEM)
    row = const((D,))

    def per_group(*shape):
        return blocked(shape, lambda g, h: (g,) + (0,) * (len(shape) - 1))

    def per_head(*shape):
        return blocked(shape, lambda g, h: (PER * g + h,) + (0,) * (len(shape) - 1))

    field_spec = blocked((SPOTS, 8, 3 * WIDE), lambda g, h: (0, 0, g))
    att_spec = blocked((LENGTH, WIDE), lambda g, h: (0, g))
    mid, xs, field, xh, qx, kx, vx, probs, outs, att, up_all, bu_all, down_all = pl.pallas_call(
        fwd_kernel,
        grid=(GROUPS, PER),
        in_specs=[
            scalar, const((LENGTH, D)), row, row, row, *w_spec, *b_spec,
            const((3, 32, WIDE)), const((8, LANES)), const((PAIRS, LANES)), const((PAIRS, LANES)),
            const((LENGTH, PAIRS)), const((LENGTH, LANES)), const((KEYS - LENGTH, LANES)),
            blocked((2, KEYS - LENGTH, WIDE), lambda g, h: (0, 0, g)),
            blocked((WIDE, D), lambda g, h: (g, 0)), anywhere, anywhere, anywhere,
        ],
        out_specs=[
            const((LENGTH, D)), const((LENGTH, D)), field_spec, per_group(PER, 3, LENGTH, LANES), per_group(PER, LENGTH, LANES),
            per_group(PER, KEYS, LANES), per_group(PER, KEYS, LANES), per_head(1, LENGTH, KEYS),
            per_head(1, LENGTH, LANES), att_spec, anywhere, anywhere, anywhere,
        ],
        out_shape=[
            sds((LENGTH, D), F32), sds((LENGTH, D), BF16), sds((SPOTS, 8, 3 * D), F32), sds((HEADS, 3, LENGTH, LANES), F32),
            sds((HEADS, LENGTH, LANES), BF16), sds((HEADS, KEYS, LANES), BF16), sds((HEADS, KEYS, LANES), BF16),
            sds((HEADS, LENGTH, KEYS), BF16), sds((HEADS, LENGTH, LANES), F32), sds((LENGTH, D), BF16),
            *[sds((split - 1, *a.shape), BF16) for a in (w_up, b_rows, w_down)],
        ],
        scratch_shapes=[
            dma((3, 3)), dma((3, 3)),
            pltpu.VMEM((LENGTH, D), BF16),
            pltpu.VMEM((3, SPOTS + 2 * SIDE, 8, WIDE), F32),
            pltpu.VMEM((SPOTS, 8, 3 * WIDE), F32),
            pltpu.VMEM((PER, LENGTH, LANES), F32),
            pltpu.VMEM((D // LANES, LENGTH, LANES), F32),
        ],
        compiler_params=pltpu.CompilerParams(vmem_limit_bytes=VMEM_LIMIT, collective_id=4, has_side_effects=True),
        name="attend",
        cost_estimate=pl.CostEstimate(flops=2 * 3_500_000_000, bytes_accessed=60_000_000, transcendentals=6_500_000),
    )(
        res_ids, inputs, gain_one, bias_one, b_proj, w_qkv, w_qkv, w_qkv, bq, bq, bq, pw, ln,
        tall, cmp, jnp.asarray(select), jnp.asarray(marks), jnp.asarray(code), mem, w_proj, w_up, b_rows, w_down,
    )

    assert w_up.shape[1] == D
    tiles = D // LANES
    cut = tiles * D
    out, gm, gml, small, gup, gdown, gfar = pl.pallas_call(
        mlp_kernel,
        grid=(split,),
        in_specs=[scalar, const((LENGTH, D)), const((LENGTH, D)), row, row, row, *[anywhere] * 6],
        out_specs=[
            const((LENGTH, D)), const((LENGTH, D)), const((LENGTH, D)), const((24 + split * tiles, LANES)),
            const((cut, LANES)), const((cut, LANES)), const((cut // 2, LANES)),
        ],
        out_shape=[
            sds((LENGTH, D), BF16), sds((LENGTH, D), F32), sds((LENGTH, D), BF16), sds((24 + split * tiles, LANES), F32),
            sds((cut, LANES), BF16), sds((cut, LANES), BF16), sds((cut // 2, LANES), BF16),
        ],
        scratch_shapes=[
            pltpu.VMEM((LENGTH, D), BF16),
            pltpu.VMEM((D, LENGTH), BF16),
            pltpu.VMEM((LENGTH, D), BF16),
            *[pltpu.VMEM((LENGTH, D), F32)] * 3,
            pltpu.VMEM((D // LANES, LENGTH, LANES), F32),
            pltpu.VMEM((2, D, D), BF16),
            pltpu.VMEM((2, 16, D), BF16),
            pltpu.VMEM((2, D, D), BF16),
            pltpu.VMEM((split, 2 * cut, LANES), BF16),
            pltpu.VMEM((2, 2 * cut, LANES), BF16),
            pltpu.VMEM((cut + cut // 2, LANES), BF16),
            dma((3, split)), dma((4,)), dma((4,)),
        ],
        compiler_params=pltpu.CompilerParams(vmem_limit_bytes=VMEM_LIMIT, collective_id=2, has_side_effects=True),
        name="mlp",
        cost_estimate=pl.CostEstimate(flops=2 * 11_300_000_000, bytes_accessed=40_000_000, transcendentals=5_000_000),
    )(res_ids, mid, cotangent, gain_two, bias_two, b_down, up_all, bu_all, down_all, w_up, b_rows, w_down)

    links = bits("dp", lax.axis_size("dp"))
    pieces, every = 12 * D, bits("tensor", split) + links
    first_orders = [every, [every[0], links[0], every[1], *links[1:]]]
    share = pieces // len(first_orders)
    kept = len(first_orders) * (share >> min(len(every), halvings(share)))
    gx, small_one, first, last, gup, gdown = pl.pallas_call(
        functools.partial(bwd_kernel, links, first_orders),
        grid=(GROUPS, PER),
        in_specs=[
            scalar, const((LENGTH, D)), row, row, anywhere, const((LENGTH, D)), *w_spec,
            const((3, 32, WIDE)), const((8, LANES)), const((PAIRS, LANES)), const((PAIRS, LANES)),
            const((LENGTH, PAIRS)), const((64, PAIRS)), blocked((WIDE, D), lambda g, h: (g, 0)),
            blocked((SPOTS, 8, 3 * WIDE), lambda g, h: (0, 0, g), True),
            per_head(1, 3, LENGTH, LANES), per_head(1, LENGTH, LANES), per_head(1, KEYS, LANES),
            per_head(1, KEYS, LANES), per_head(1, LENGTH, KEYS), per_head(1, LENGTH, LANES), att_spec,
            anywhere, anywhere, anywhere,
        ],
        out_specs=[
            const((LENGTH, D)), const((208, LANES)),
            const((kept, LANES)), const((pieces, LANES)), anywhere, anywhere,
        ],
        out_shape=[
            sds((LENGTH, D), F32), sds((208, LANES), F32), sds((kept, LANES), BF16), sds((pieces, LANES), BF16),
            sds((cut, LANES), BF16), sds((cut, LANES), BF16),
        ],
        scratch_shapes=[
            pltpu.VMEM((32, WIDE), F32),
            pltpu.VMEM((PAIRS, LANES), F32),
            pltpu.VMEM((LENGTH, D), BF16),
            pltpu.VMEM((PER, LENGTH, LANES), F32),
            pltpu.VMEM((LENGTH, KEYS), BF16),
            pltpu.VMEM((PER, 3, LENGTH, LANES), F32),
            pltpu.VMEM((3, SPOTS + 2 * SIDE, 8, WIDE), F32),
            pltpu.VMEM((LENGTH, 3 * WIDE), BF16),
            pltpu.VMEM((LENGTH, 3 * WIDE), F32),
            pltpu.VMEM((cut, LANES), BF16), pltpu.VMEM((cut, LANES), BF16), pltpu.VMEM((cut // 2, LANES), BF16),
            pltpu.VMEM((cut, LANES), BF16), pltpu.VMEM((cut, LANES), BF16), pltpu.VMEM((cut // 2, LANES), BF16),
            pltpu.VMEM((pieces, LANES), BF16), pltpu.VMEM((len(first_orders), landing(share, len(every)), LANES), BF16),
            dma((4,)), dma((2,)), dma((4, 2 * len(every))), dma((4, 2 * len(every))),
        ],
        compiler_params=pltpu.CompilerParams(vmem_limit_bytes=VMEM_LIMIT, collective_id=3, has_side_effects=True),
        name="attend_back",
        cost_estimate=pl.CostEstimate(flops=2 * 7_000_000_000, bytes_accessed=60_000_000, transcendentals=0),
    )(
        res_ids, xs, gain_one, bias_one, gm, gml, w_qkv, w_qkv, w_qkv, pw, ln, tall, cmp, jnp.asarray(select), pick_rows, w_proj,
        field, xh, qx, kx, vx, probs, outs, att, gup, gdown, gfar,
    )

    first, last, small = all_reduce(first, last, small_one, small, every, first_orders)
    outs = unpack(*[a.reshape(-1, D, LANES) for a in (first, last, gup, gdown)], small)
    squares, (gain1, bias1, bp, gain2, bias2, bd, bu), (gb, gpw, pg, pb, rel) = outs[:4], outs[4:11], outs[11:]

    return (
        out, gx, gain1, bias1, squares[0], gb, gpw, pg, pb, rel, squares[1], bp, gain2, bias2, squares[2], bu, squares[3], bd,
    )


def solution(mesh):
    rows = P(("dp", "tensor"), None)
    return jax.shard_map(
        per_device,
        mesh=mesh,
        in_specs=(
            rows, P(("dp", "tensor")), P(None, ("dp", "tensor"), None), *[P()] * 12,
            P(None, "tensor"), P("tensor"), P("tensor", None), P(), rows,
        ),
        out_specs=(rows, rows, *[P()] * 12, P(None, "tensor"), P("tensor"), P("tensor", None), P()),
        check_vma=False,
    )
```
